32 devices in a mesh: blk: 8 (over z, y), order: 4 (over x, core).
Axes of the slice: x: 2, y: 2, z: 4, core: 2. Of those that a mesh axis runs over, the one named last changes fastest.
Arguments:
- harmonics: float32 [64, 4, 8192], P('order', None, 'blk'), may hold values from -6 to 6
- legendre: float32 [64, 2, 64, 8192], P('order', None, 'blk'), may hold values from -0.0078125 to 0.0078125
- sky_map: float32 [64, 2, 16384], P(('blk', 'order')), may hold values from -6 to 6
- cycle_length: int32 [64], P(('blk', 'order')), may hold values from 4 to 16384, as said below
- cycle_offset: int32 [64], P(('blk', 'order')), may hold values from 0 to 1, as said below
- cycle_weight: float32 [64], P(('blk', 'order')), may hold values from 0.1 to 0.4
- order_ids: int32 [64], P('order'), may hold values from 0 to 8191, as said below
Outputs:
- refined: float32 [64, 4, 8192], P('order', None, 'blk')
- residual: float32 [64, 2, 16384], P(('blk', 'order'))
The draws below stay inside these ranges and needn't reach their ends.
Inputs may be any that keep to these rules, and one draw needn't show every extreme that they name: `cycle_length`: cycle lengths are multiples of 4. Of each device's 2 consecutive cycles, those at even places have 4 * 4096 pixels, those at odd places 4 j pixels for some j from 1 to 4095. `cycle_offset`: 1 on every cycle of fewer than 16384 pixels. `order_ids`: the orders are distinct; 0 and 8191 are among them. Slot s (from 0) of each index of order holds an order from s * 512 to (s + 1) * 512 - 1.
All inputs are finite; a program needn't handle non-finite values.
Results may differ from the reference program's by a relative error of at most 0.0003.
Values sent between devices are 32-bit elements; how exact they have to be, the bound alone decides.
No kernel may reach another device: no remote copies, remote signals or barrier semaphores. Data moves between devices by JAX's collectives and lax.ppermute only.
A program may use at most 192 MiB of HBM per device.

```python
import math
import jax
import jax.numpy as jnp
from jax import lax

NSIDE = 4096
L = 8192
NPAD = 16384
M_DEV = 16
R_OWN = 2
M_TOT = 64
CYCLES = 64


def cycle_plan(key):
    position = jnp.arange(CYCLES, dtype=jnp.int32)
    within_device = position % R_OWN
    belt_cycle = NSIDE + jax.random.randint(jax.random.fold_in(key, 11), (CYCLES,), 0, 2 * NSIDE + 1)
    polar_cycle = 1 + jax.random.randint(jax.random.fold_in(key, 12), (CYCLES,), 0, NSIDE - 1)
    polar_cycle = jnp.where(position == 1, 1, polar_cycle)
    equator = within_device % 2 == 0
    length = jnp.where(equator, 4 * NSIDE, 4 * polar_cycle)
    offset = jnp.where(equator, (belt_cycle - NSIDE + 1) % 2, 1)
    return (length.astype(jnp.int32), offset.astype(jnp.int32))


def draw_cycle_length(key, part):
    return cycle_plan(key)[0]


def draw_cycle_offset(key, part):
    return cycle_plan(key)[1]


def draw_order_ids(key, part):
    stratum = L // M_DEV
    groups = M_TOT // M_DEV

    def one_slot(slot):
        picks = jax.random.permutation(jax.random.fold_in(key, 30 + slot), stratum - 2)[:groups]
        return (picks + 1 + slot * stratum).astype(jnp.int32)
    table = jax.vmap(one_slot)(jnp.arange(M_DEV, dtype=jnp.int32))
    chosen = jnp.transpose(table).reshape(M_TOT).astype(jnp.int32)
    chosen = chosen.at[0].set(0)
    chosen = chosen.at[M_TOT - 1].set(L - 1)
    return chosen


def block_levels(key, dims, cuts, low, largest):
    def one(dim, blocks):
        heights = jax.random.uniform(jax.random.fold_in(jax.random.fold_in(key, 6), dim), (blocks,), jnp.float32, low / len(cuts), largest / len(cuts))
        return jnp.repeat(jnp.exp(heights), dims[dim] // blocks).reshape((-1,) + (1,) * (len(dims) - dim - 1))

    gain = one(*cuts[0])
    for cut in cuts[1:]:
        gain = gain * one(*cut)
    return gain


def scatter_about(stream_key, shape, spread, most, split=(), kind=jnp.bfloat16):
    result = spread * jax.random.normal(stream_key, shape, jnp.float32)
    if split:
        result = result * block_levels(stream_key, shape, split, -0.22, 0.18)
    return jnp.clip(result, -most, most).astype(kind)


def setup_inputs(seed: int = 0) -> dict:
    key_of = jax.random.split(jax.random.key(seed), 8)
    harmonics = scatter_about(key_of[0], (M_TOT, 4, L), 1.0, 6.0, ((0, 4), (2, 8)), jnp.float32)
    legendre = scatter_about(key_of[1], (M_TOT, 2, CYCLES, L), (L * M_TOT) ** -0.5, 0.0078125, ((0, 4), (2, 8)), jnp.float32)
    sky_map = scatter_about(key_of[2], (CYCLES, 2, NPAD), 1.0, 6.0, ((0, 32),), jnp.float32)
    cycle_length = draw_cycle_length(jax.random.fold_in(key_of[7], 71), 0)
    cycle_offset = draw_cycle_offset(jax.random.fold_in(key_of[7], 71), 0)
    cycle_weight = jnp.clip(jnp.exp(math.log(0.4) - 1.3862944 * jax.random.uniform(key_of[5], (CYCLES,), jnp.float32) ** block_levels(key_of[5], (CYCLES,), ((0, 32),), -0.2, 0.2)), 0.1, 0.4)
    order_ids = draw_order_ids(jax.random.fold_in(key_of[7], 71), 0)
    return {"harmonics": harmonics, "legendre": legendre, "sky_map": sky_map, "cycle_length": cycle_length, "cycle_offset": cycle_offset, "cycle_weight": cycle_weight, "order_ids": order_ids}


HIGHEST = lax.Precision.HIGHEST

def cycle_tables(orders, length, offset, first_pixel, block_width):
    pixels = first_pixel + lax.iota(jnp.int32, block_width)
    phase_turns = orders[:, None] * (2 * pixels + offset)[None, :] % (2 * length)
    angles = phase_turns.astype(jnp.float32) * (math.pi / length.astype(jnp.float32))
    inside = (pixels < length).astype(jnp.float32)
    return (jnp.concatenate([jnp.cos(angles), jnp.sin(angles)], axis=0), inside)

def synth_weights(phases, factor):
    scaled = phases * factor[:, None]
    first_row = jnp.concatenate([scaled[:, 0], -scaled[:, 1]])
    second_row = jnp.concatenate([scaled[:, 2], -scaled[:, 3]])
    return jnp.stack([first_row, second_row])

def fold_totals(totals, weighting):
    half = totals.shape[1] // 2
    return weighting * jnp.stack([totals[0, :half], -totals[0, half:], totals[1, :half], -totals[1, half:]], axis=1)

def assemble(products):
    positive = products[:, 0]
    negative = products[:, 1]
    return jnp.stack([-positive[:, 0] + negative[:, 3], -positive[:, 1] - negative[:, 2], -positive[:, 2] - negative[:, 1], -positive[:, 3] + negative[:, 0]], axis=1)

def adjoint_coeffs(returned):
    positive = -returned
    negative = jnp.stack([returned[:, 3], -returned[:, 2], -returned[:, 1], returned[:, 0]], axis=1)
    return jnp.stack([positive, negative], axis=1)

def reference(harmonics, legendre, sky_map, cycle_length, cycle_offset, cycle_weight, order_ids):
    degrees = jnp.arange(L, dtype=jnp.int32)
    valid_mask = (degrees[None, :] >= jnp.maximum(order_ids, 2)[:, None]).astype(jnp.float32)
    coefficients = harmonics * valid_mask[:, None, :]

    def forward(operands):
        tables, values = operands
        return jnp.einsum('trl,cl->tcr', tables, values, precision=HIGHEST)
    products = lax.map(forward, (legendre, coefficients))
    phases = assemble(products)
    factor = jnp.where(order_ids == 0, 1.0, 2.0).astype(jnp.float32)
    normalise = math.sqrt(L * M_TOT / (CYCLES * NPAD))

    def per_cycle(inputs):
        cycle_phases, sky_row, length, offset, weight = inputs
        weights = synth_weights(cycle_phases, factor)
        trig_table, inside = cycle_tables(order_ids, length, offset, 0, NPAD)
        modelled = jnp.dot(weights, trig_table, precision=HIGHEST)
        residual = (sky_row - modelled) * inside[None, :]
        totals = lax.dot_general(residual, trig_table, (((1,), (1,)), ((), ())), precision=HIGHEST)
        return (residual, fold_totals(totals, weight * normalise))
    residual, analysed = lax.map(per_cycle, (jnp.transpose(phases, (2, 0, 1)), sky_map, cycle_length, cycle_offset, cycle_weight))
    coeffs = adjoint_coeffs(jnp.transpose(analysed, (1, 2, 0)))

    def backward(operands):
        tables, weights = operands
        return jnp.einsum('trl,tar->al', tables, weights, precision=HIGHEST)
    update = lax.map(backward, (legendre, coeffs))
    refined = valid_mask[:, None, :] * (harmonics + update)
    return (refined, residual)
```

```python
import math

import jax
import jax.numpy as jnp
from jax import lax
from jax.experimental import pallas as pl
from jax.experimental.pallas import tpu as pltpu
from jax.sharding import PartitionSpec as P

HIGHEST = lax.Precision.HIGHEST
LANES = 128
VMEM = pltpu.VMEM
MIB = 1024 * 1024


def slot_ranges(slots):
    return [(0, slots // 2), (slots // 2, slots)]


def needed(block, first_slot, width, stratum):
    return (block + 1) * width > stratum * first_slot


def trig_tables(ids, length, offset, rows, columns):
    period = (2 * length)[:, None, None]
    scale = (math.pi / length.astype(jnp.float32))[:, None, None]
    coarse = 2 * columns * lax.iota(jnp.int32, rows)[None, :, None] + offset[:, None, None]
    angle = (ids[None, None, :] * coarse % period).astype(jnp.float32) * scale
    cos_a, sin_a = jnp.cos(angle), jnp.sin(angle)
    fine = 2 * lax.iota(jnp.int32, columns)[None, None, :]
    angle = (ids[None, :, None] * fine % period).astype(jnp.float32) * scale
    table_b = jnp.concatenate([jnp.cos(angle), jnp.sin(angle)], axis=1)
    return (
        jnp.concatenate([cos_a, -sin_a], axis=2),
        jnp.concatenate([sin_a, cos_a], axis=2),
        table_b,
    )


def pixel_mask(shape, length):
    pixel = lax.broadcasted_iota(jnp.int32, shape, 0) * shape[1]
    pixel = pixel + lax.broadcasted_iota(jnp.int32, shape, 1)
    return pixel < length


def sky_kernel(
    normalise, groups, slots, cycles,
    ids_ref, meta_ref, length_ref, lanes_ref, sky_ref, acs_ref, asc_ref, bt_ref,
    pieces_ref, gram_ref,
):
    me = lax.axis_index("order")
    rows, both = acs_ref.shape[1:]
    every = both // 2
    row8 = lax.broadcasted_iota(jnp.int32, (8, both), 0)
    sums = [jnp.zeros((8, both), jnp.float32) for _ in range(4)]
    for c in range(cycles):
        inside = pixel_mask((rows, LANES), length_ref[c])
        scale = meta_ref[0, slots + 2 * cycles + c] * normalise
        for q in range(2):
            section = jnp.where(inside, sky_ref[c, q], 0.0)
            spun = lax.dot_general(
                section, bt_ref[c], (((1,), (1,)), ((), ())), precision=HIGHEST,
                preferred_element_type=jnp.float32,
            )
            even = jnp.sum(spun * acs_ref[c], axis=0, keepdims=True) * scale
            odd = jnp.sum(spun * asc_ref[c], axis=0, keepdims=True) * -scale
            sums[2 * q] = jnp.where(row8 == c, even, sums[2 * q])
            sums[2 * q + 1] = jnp.where(row8 == c, odd, sums[2 * q + 1])
    source = lax.broadcasted_iota(jnp.int32, (both, LANES), 0) % every
    lane = lax.broadcasted_iota(jnp.int32, (both, LANES), 1)
    for d in range(groups):
        piece = jnp.zeros((8, LANES), jnp.float32)
        for a in range(4):
            place = ((lane - a * slots) == (source - d * slots)) & (lane // slots == a)
            piece = piece + jnp.dot(
                sums[a], place.astype(jnp.float32), precision=HIGHEST,
                preferred_element_type=jnp.float32,
            )
        pieces_ref[d] = piece
    count, wide = gram_ref.shape[1:]
    row = lax.broadcasted_iota(jnp.int32, (count, wide), 0)
    length = jnp.ones((count, wide), jnp.float32)
    offset = jnp.zeros((count, wide), jnp.float32)
    weight = jnp.zeros((count, wide), jnp.float32)
    for r in range(count):
        d = (r // cycles) ^ me
        c = r % cycles
        length = jnp.where(row == r, meta_ref[d, slots + c], length)
        offset = jnp.where(row == r, meta_ref[d, slots + cycles + c], offset)
        weight = jnp.where(row == r, meta_ref[d, slots + 2 * cycles + c], weight)
    others = jnp.broadcast_to(lanes_ref[...], (count, wide))
    lane = lax.broadcasted_iota(jnp.int32, (count, wide), 1)
    cosine = (lane // slots) % 2 == 0
    factor = jnp.where(others == 0.0, 0.5, 1.0) * normalise * weight * length

    def response(n):
        turns = jnp.round(n / length)
        sign = jnp.where((offset > 0.5) & (turns.astype(jnp.int32) % 2 != 0), -1.0, 1.0)
        return jnp.where(turns * length == n, sign, 0.0)

    def one(m, carry):
        mine = ids_ref[m].astype(jnp.float32)
        near = response(mine - others)
        far = response(mine + others)
        gram_ref[m] = factor * (near + jnp.where(cosine, far, -far))
        return carry

    lax.fori_loop(0, gram_ref.shape[0], one, 0)


def load_tables(legendre, tables, sems, stratum):
    copies = []
    for m in range(tables.shape[0]):
        part = (m, slice(None), slice(None), pl.ds(stratum * m, tables.shape[3] - stratum * m))
        copies.append(pltpu.make_async_copy(legendre.at[part], tables.at[part], sems.at[m]))
    return copies


def forward_kernel(ranges, blocks, groups, stratum, ids_ref, legendre, pieces_ref, *rest):
    parts = rest[: len(ranges) * blocks]
    phases_ref, *messages, tables, sems = rest[len(ranges) * blocks :]
    me = lax.axis_index("blk")
    slots = tables.shape[0]
    count = tables.shape[2]
    width = parts[0].shape[2]
    copies = load_tables(legendre, tables, sems, stratum)
    for copy in copies:
        copy.start()
    lane = lax.broadcasted_iota(jnp.int32, (count, LANES), 1)
    phases = jnp.zeros((count, LANES), jnp.float32)
    for index, (low, high) in enumerate(ranges):
        for m in range(low, high):
            copies[m].wait()
            floor = jnp.maximum(ids_ref[m], 2)
            total = [jnp.zeros((count, LANES), jnp.float32)] * 4
            for d in range(blocks):
                block = me ^ d
                part = parts[index * blocks + d]

                def use(carry, part=part, block=block, m=m, low=low, floor=floor):
                    t0, t1, t2, t3 = carry
                    first = pl.multiple_of(block * width, LANES)
                    for t in range(width // LANES):
                        keep = lane >= floor - first - t * LANES
                        span = pl.ds(first + t * LANES, LANES)
                        plus = jnp.where(keep, tables[m, 0, :, span], 0.0)
                        minus = jnp.where(keep, tables[m, 1, :, span], 0.0)
                        here = pl.ds(t * LANES, LANES)
                        c0, c1, c2, c3 = [part[m - low, a : a + 1, here] for a in range(4)]
                        t0 = t0 - plus * c0 + minus * c3
                        t1 = t1 - plus * c1 - minus * c2
                        t2 = t2 - plus * c2 - minus * c1
                        t3 = t3 - plus * c3 + minus * c0
                    return [t0, t1, t2, t3]

                total = lax.cond(
                    (block + 1) * width > stratum * m, use, lambda carry: carry, total
                )
            for a in range(4):
                value = jnp.sum(total[a], axis=1, keepdims=True)
                phases = jnp.where(lane == a * slots + m, value, phases)
    phases_ref[...] = phases
    for d in range(1, groups):
        messages[d - 1][:count] = phases
        messages[d - 1][count:] = pieces_ref[d]


def fold_rows(values, row):
    for step in (1, 2, 4):
        low = (row & step) == 0
        values = [
            jnp.where(low, values[i], values[i + 1])
            + pltpu.roll(jnp.where(low, values[i + 1], values[i]), step, 0)
            for i in range(0, len(values), 2)
        ]
    return values[0]


def backward_kernel(
    ranges, blocks, groups, cycles, stratum, legendre, gram_ref, pieces_ref, phases_ref, *rest
):
    messages = rest[: groups - 1]
    outs = rest[groups - 1 : groups - 1 + len(ranges) * blocks]
    tables, sky, sems = rest[groups - 1 + len(ranges) * blocks :]
    me = lax.axis_index("blk")
    owner = lax.axis_index("order")
    slots = tables.shape[0]
    count = tables.shape[2]
    width = outs[0].shape[2]
    copies = load_tables(legendre, tables, sems, stratum)
    for copy in copies:
        copy.start()
    wide = 4 * slots
    pairs = []
    for d in range(groups):
        phases = phases_ref[...] if d == 0 else messages[d - 1][:count]
        piece = pieces_ref[0] if d == 0 else messages[d - 1][count:]
        sky[pl.ds((owner ^ d) * cycles, cycles)] = piece[:cycles]
        pairs.append(phases)
    lane = lax.broadcasted_iota(jnp.int32, (count, LANES), 1)
    row8 = lax.broadcasted_iota(jnp.int32, (8, LANES), 0)
    per = LANES // wide
    packed = []
    for start in range(0, groups, per):
        value = pairs[start]
        for k in range(1, per):
            value = jnp.where(
                lane // wide == k, pltpu.roll(pairs[start + k], k * wide, 1), value
            )
        packed.append(value)
    observed = sky[...]
    for index, (low, high) in enumerate(ranges):
        for m in range(low, high):
            total = jnp.where((lane < wide) & (lane % slots == m), observed, 0.0)
            for k, value in enumerate(packed):
                total = total - gram_ref[m, :, k * LANES : (k + 1) * LANES] * value
            an = []
            for a in range(4):
                value = jnp.where((lane % wide) // slots == a, total, 0.0)
                value = jnp.sum(value, axis=1, keepdims=True)
                an.append(jnp.broadcast_to(value, (count, LANES)))
            copies[m].wait()
            for d in range(blocks):
                block = me ^ d
                out = outs[index * blocks + d]

                @pl.when((block + 1) * width > stratum * m)
                def _(an=an, out=out, block=block, m=m, low=low):
                    first = pl.multiple_of(block * width, LANES)
                    for t in range(0, width // LANES, 2):
                        values = []
                        for u in range(2):
                            span = pl.ds(first + (t + u) * LANES, LANES)
                            plus = tables[m, 0, :, span]
                            minus = tables[m, 1, :, span]
                            four = [
                                minus * an[3] - plus * an[0],
                                -(plus * an[1] + minus * an[2]),
                                -(plus * an[2] + minus * an[1]),
                                minus * an[0] - plus * an[3],
                            ]
                            values += [
                                sum(v[8 * k : 8 * k + 8] for k in range(count // 8)) for v in four
                            ]
                        folded = fold_rows(values, row8)
                        for u in range(2):
                            out[m - low, :, pl.ds((t + u) * LANES, LANES)] = folded[
                                4 * u : 4 * u + 4
                            ]


def residual_kernel(
    groups, slots, cycles,
    length_ref, ids_ref, sky_ref, acs_ref, asc_ref, bt_ref, phases_ref, *rest
):
    messages = rest[: groups - 1]
    out_ref, spread = rest[groups - 1 :]
    owner = lax.axis_index("order")
    rows, both = acs_ref.shape[1:]
    every = both // 2
    count = phases_ref.shape[0]
    source = lax.broadcasted_iota(jnp.int32, (LANES, both), 0)
    lane = lax.broadcasted_iota(jnp.int32, (LANES, both), 1) % every
    factor = jnp.where(ids_ref[...] == 0.0, 1.0, 2.0)
    for a in range(4):
        total = jnp.zeros((count, both), jnp.float32)
        for d in range(groups):
            phases = phases_ref[...] if d == 0 else messages[d - 1][:count]
            place = (lane - d * slots == source - a * slots) & (lane // slots == d)
            total = total + jnp.dot(
                phases, place.astype(jnp.float32), precision=HIGHEST,
                preferred_element_type=jnp.float32,
            )
        spread[a] = total * factor
    for c in range(cycles):
        inside = pixel_mask((rows, LANES), length_ref[c])
        for q in range(2):
            real = spread[2 * q, pl.ds(owner * cycles + c, 1)]
            imag = spread[2 * q + 1, pl.ds(owner * cycles + c, 1)]
            weights = real * acs_ref[c] - imag * asc_ref[c]
            model = jnp.dot(
                weights, bt_ref[c], precision=HIGHEST, preferred_element_type=jnp.float32
            )
            out_ref[c, q] = jnp.where(inside, sky_ref[c, q] - model, 0.0)


def smem():
    return pl.BlockSpec(memory_space=pltpu.SMEM)


def vmem():
    return pl.BlockSpec(memory_space=VMEM)


def shape(*dims):
    return jax.ShapeDtypeStruct(dims, jnp.float32)


def body(harmonics, legendre, sky_map, cycle_length, cycle_offset, cycle_weight, order_ids):
    groups = lax.axis_size("order")
    blocks = lax.axis_size("blk")
    slots, _, width = harmonics.shape
    count, degrees = legendre.shape[2:]
    cycles, _, pixels = sky_map.shape
    rows = pixels // LANES
    stratum = degrees // slots
    every = slots * groups
    normalise = math.sqrt(degrees * every / (cycles * groups * blocks * pixels))
    ranges = slot_ranges(slots)

    meta = jnp.concatenate(
        [
            order_ids.astype(jnp.float32),
            cycle_length.astype(jnp.float32),
            cycle_offset.astype(jnp.float32),
            cycle_weight,
        ]
    )
    meta = jnp.pad(meta, (0, LANES - meta.shape[0]))[None]

    def swap(value, axis, step, keep=lambda source: True):
        size = lax.axis_size(axis)
        return lax.ppermute(
            value, axis, [(i, i ^ step) for i in range(size) if keep(i)]
        )

    metas = jnp.concatenate([meta] + [swap(meta, "order", d) for d in range(1, groups)])

    parts = []
    for low, high in ranges:
        own = harmonics[low:high]

        def far(block, low=low):
            return needed(block, low, width, stratum)

        got = [own] + [swap(own, "blk", d, far) for d in range(2, blocks, 2)]
        line = []
        for k, value in enumerate(got):
            line += [value, swap(value, "blk", 1, lambda b, k=k: far(b ^ (2 * k)))]
        parts += line

    ids = metas[:, :slots].reshape(every)
    acs, asc, table_b = trig_tables(
        ids.astype(jnp.int32), cycle_length, cycle_offset, rows, LANES
    )
    sky = sky_map.reshape(cycles, 2, rows, LANES)
    lane_ids = jnp.broadcast_to(ids.reshape(groups, 1, slots), (groups, 4, slots))
    lane_ids = lane_ids.reshape(1, 4 * every)
    pieces, gram = pl.pallas_call(
        lambda *refs: sky_kernel(normalise, groups, slots, cycles, *refs),
        out_shape=(shape(groups, 8, LANES), shape(slots, count, 4 * every)),
        in_specs=[smem(), smem(), smem()] + [vmem()] * 5,
        out_specs=(vmem(), vmem()),
        compiler_params=pltpu.CompilerParams(vmem_limit_bytes=16 * MIB),
        cost_estimate=pl.CostEstimate(flops=10**8, bytes_accessed=2 * MIB, transcendentals=0),
        name="sky_analysis",
    )(order_ids, metas, cycle_length, lane_ids, sky, acs, asc, table_b)

    table_scratch = [
        pltpu.VMEM(legendre.shape, jnp.float32),
        pltpu.SemaphoreType.DMA((slots,)),
    ]
    hbm = pl.BlockSpec(memory_space=pl.ANY)
    outs = pl.pallas_call(
        lambda *refs: forward_kernel(ranges, blocks, groups, stratum, *refs),
        out_shape=[shape(count, LANES)] + [shape(count + 8, LANES)] * (groups - 1),
        in_specs=[smem(), hbm, vmem()] + [vmem()] * len(parts),
        out_specs=[vmem()] * groups,
        scratch_shapes=table_scratch,
        compiler_params=pltpu.CompilerParams(vmem_limit_bytes=40 * MIB),
        cost_estimate=pl.CostEstimate(flops=10**8, bytes_accessed=8 * MIB, transcendentals=0),
        name="forward",
    )(order_ids, legendre, pieces, *parts)
    phases = outs[0]
    messages = [swap(outs[d], "order", d) for d in range(1, groups)]

    partial = pl.pallas_call(
        lambda *refs: backward_kernel(ranges, blocks, groups, cycles, stratum, *refs),
        out_shape=[shape(high - low, 4, width) for low, high in ranges for _ in range(blocks)],
        in_specs=[hbm] + [vmem()] * (2 + groups),
        out_specs=[vmem()] * (len(ranges) * blocks),
        scratch_shapes=[table_scratch[0], pltpu.VMEM((count, LANES), jnp.float32), table_scratch[1]],
        compiler_params=pltpu.CompilerParams(vmem_limit_bytes=40 * MIB),
        cost_estimate=pl.CostEstimate(flops=10**8, bytes_accessed=8 * MIB, transcendentals=0),
        name="backward",
    )(legendre, gram, pieces, phases, *messages)

    residual = pl.pallas_call(
        lambda *refs: residual_kernel(groups, slots, cycles, *refs),
        out_shape=shape(cycles, 2, rows, LANES),
        in_specs=[smem()] + [vmem()] * (5 + groups),
        out_specs=vmem(),
        scratch_shapes=[pltpu.VMEM((4, count, 2 * every), jnp.float32)],
        compiler_params=pltpu.CompilerParams(vmem_limit_bytes=16 * MIB),
        cost_estimate=pl.CostEstimate(flops=10**8, bytes_accessed=2 * MIB, transcendentals=0),
        name="residual",
    )(cycle_length, jnp.concatenate([ids, ids])[None], sky, acs, asc, table_b, phases, *messages)
    residual = residual.reshape(sky_map.shape)

    updates = []
    for index, (low, high) in enumerate(ranges):
        piece = partial[index * blocks : (index + 1) * blocks]

        def far(block, low=low):
            return needed(block, low, width, stratum)

        sums = {}
        for k in reversed(range(blocks // 2)):
            moved = swap(piece[2 * k + 1], "blk", 1, lambda b, k=k: far(b ^ 1 ^ (2 * k)))
            sums[k] = piece[2 * k] + moved
        total = sums[0]
        for k in reversed(range(1, blocks // 2)):
            total = total + swap(sums[k], "blk", 2 * k, lambda b, k=k: far(b ^ (2 * k)))
        updates.append(total)
    update = jnp.concatenate(updates)
    floors = jnp.maximum(order_ids, 2)
    degree = lax.axis_index("blk") * width + lax.iota(jnp.int32, width)
    valid = degree[None, :] >= floors[:, None]
    refined = jnp.where(valid[:, None, :], harmonics + update, 0.0)
    return (refined, residual)


def solution(mesh):
    return jax.shard_map(
        body,
        mesh=mesh,
        in_specs=(
            P("order", None, "blk"),
            P("order", None, "blk", None),
            P(("blk", "order"), None, None),
            P(("blk", "order")),
            P(("blk", "order")),
            P(("blk", "order")),
            P("order"),
        ),
        out_specs=(P("order", None, "blk"), P(("blk", "order"), None, None)),
        check_vma=False,
    )
```

```python
import math

import jax
import jax.numpy as jnp
from jax import lax
from jax.experimental import pallas as pl
from jax.experimental.pallas import tpu as pltpu
from jax.sharding import PartitionSpec as P

HIGHEST = lax.Precision.HIGHEST
LANES = 128
VMEM = pltpu.VMEM
MIB = 1024 * 1024


def needed(block, first_slot, width, stratum):
    return (block + 1) * width > stratum * first_slot


def ring_of(blocks):
    return list(range(0, blocks, 2)) + list(range(blocks - 1, 0, -2))


def ring_place(block, blocks):
    return jnp.where(block % 2 == 0, block // 2, blocks - 1 - block // 2)


def block_at(place, blocks):
    place = lax.rem(place + 2 * blocks, blocks)
    return jnp.where(place < blocks // 2, 2 * place, 2 * (blocks - 1 - place) + 1)


def sin_pi(x):
    turns = jnp.round(x)
    y = (x - turns) * math.pi
    z = y * y
    value = -1.0 / 39916800
    for term in (1.0 / 362880, -1.0 / 5040, 1.0 / 120, -1.0 / 6, 1.0):
        value = value * z + term
    value = value * y
    return jnp.where(turns.astype(jnp.int32) % 2 != 0, -value, value)


def half_turns(order, step, length):
    total = order * step
    period = 2 * length
    scale = 0.5 / length.astype(jnp.float32)
    for _ in range(2):
        total = total - jnp.floor(total.astype(jnp.float32) * scale).astype(jnp.int32) * period
    return total.astype(jnp.float32) / length.astype(jnp.float32)


def pixel_mask(shape, length):
    pixel = lax.broadcasted_iota(jnp.int32, shape, 0) // 2 * shape[1]
    pixel = pixel + lax.broadcasted_iota(jnp.int32, shape, 1)
    return pixel < length


def meta_kernel(slots, cycles, ids, length, offset, weight, out_ref, *scratch):
    *held, sems = scratch
    copies = [
        pltpu.make_async_copy(source, target, sems.at[k])
        for k, (source, target) in enumerate(zip((ids, length, offset, weight), held))
    ]
    for copy in copies:
        copy.start()
    for copy in copies:
        copy.wait()
    lane = lax.broadcasted_iota(jnp.int32, (1, LANES), 1)
    out = jnp.zeros((1, LANES), jnp.float32)
    for m in range(slots):
        out = jnp.where(lane == m, held[0][m].astype(jnp.float32), out)
    for c in range(cycles):
        for k in range(3):
            value = held[1 + k][c].astype(jnp.float32)
            out = jnp.where(lane == slots + k * cycles + c, value, out)
    out_ref[...] = out


def entry(meta, at):
    return meta[:, at : at + 1]


def spread_ids(metas, slots, sources):
    per = LANES // slots
    lane = lax.broadcasted_iota(jnp.int32, (1, LANES), 1)
    pieces = []
    for start in range(0, len(sources), per):
        piece = jnp.zeros((1, LANES), jnp.float32)
        for k in range(per):
            value = metas[sources[start + k]]
            value = pltpu.roll(value, k * slots, 1) if k else value
            piece = jnp.where(lane // slots == k, value, piece)
        pieces.append(piece)
    return jnp.concatenate(pieces, axis=1)


def sky_kernel(normalise, groups, slots, cycles, *rest):
    metas = [ref[...] for ref in rest[:groups]]
    sky_ref, legendre = rest[groups : groups + 2]
    pieces_ref, gram_ref, acs_ref, asc_ref, fine_ref, tables, sems = rest[groups + 2 :]
    copies = table_copies(legendre, tables, sems)
    for copy in copies:
        copy.start()
    me = lax.axis_index("order")
    rows, both = acs_ref.shape[1:]
    every = both // 2
    ids = spread_ids(metas, slots, [d for _ in range(2) for d in range(groups)])
    ids = ids.astype(jnp.int32)
    row8 = lax.broadcasted_iota(jnp.int32, (8, both), 0)
    sums = [jnp.zeros((8, both), jnp.float32) for _ in range(4)]
    for c in range(cycles):
        length = entry(metas[0], slots + c).astype(jnp.int32)
        offset = entry(metas[0], slots + cycles + c).astype(jnp.int32)
        coarse = lax.broadcasted_iota(jnp.int32, (rows, both), 0) // 2 * (2 * LANES) + offset
        x = half_turns(ids, coarse, length)
        first = lax.broadcasted_iota(jnp.int32, (rows, both), 1) < every
        acs = sin_pi(x + jnp.where(first, 0.5, 1.0))
        asc = sin_pi(x + jnp.where(first, 0.0, 0.5))
        acs_ref[c] = acs
        asc_ref[c] = asc
        fine = 2 * lax.broadcasted_iota(jnp.int32, (LANES, both), 0)
        x = half_turns(ids, fine, length)
        first = lax.broadcasted_iota(jnp.int32, (LANES, both), 1) < every
        table = sin_pi(x + jnp.where(first, 0.5, 0.0))
        fine_ref[c] = table
        section = jnp.where(pixel_mask((rows, LANES), length), sky_ref[c], 0.0)
        spun = jnp.dot(section, table, precision=HIGHEST, preferred_element_type=jnp.float32)
        weight = entry(metas[0], slots + 2 * cycles + c) * normalise
        for k, value in enumerate((spun * acs, spun * asc)):
            value = sum(value[8 * i : 8 * i + 8] for i in range(rows // 8))
            for q in range(2):
                total = jnp.sum(jnp.where(row8 % 2 == q, value, 0.0), axis=0, keepdims=True)
                total = total * (-weight if k else weight)
                sums[2 * q + k] = jnp.where(row8 == c, total, sums[2 * q + k])
    source = lax.broadcasted_iota(jnp.int32, (both, LANES), 0) % every
    lane = lax.broadcasted_iota(jnp.int32, (both, LANES), 1)
    for d in range(groups):
        piece = jnp.zeros((8, LANES), jnp.float32)
        for a in range(4):
            place = ((lane - a * slots) == (source - d * slots)) & (lane // slots == a)
            piece = piece + jnp.dot(
                sums[a], place.astype(jnp.float32), precision=HIGHEST,
                preferred_element_type=jnp.float32,
            )
        pieces_ref[d] = piece
    count, wide = gram_ref.shape[1:]
    row = lax.broadcasted_iota(jnp.int32, (count, wide), 0)
    length = jnp.ones((count, wide), jnp.float32)
    offset = jnp.zeros((count, wide), jnp.float32)
    weight = jnp.zeros((count, wide), jnp.float32)
    for d in range(groups):
        for c in range(cycles):
            here = row == (me ^ d) * cycles + c
            length = jnp.where(here, entry(metas[d], slots + c), length)
            offset = jnp.where(here, entry(metas[d], slots + cycles + c), offset)
            weight = jnp.where(here, entry(metas[d], slots + 2 * cycles + c), weight)
    others = spread_ids(metas, slots, [d for d in range(groups) for _ in range(4)])
    lane = lax.broadcasted_iota(jnp.int32, (count, wide), 1)
    cosine = (lane // slots) % 2 == 0
    factor = jnp.where(others == 0.0, 0.5, 1.0) * normalise * weight * length
    inverse = 1.0 / length
    odd = offset > 0.5

    def response(n):
        turns = jnp.round(n * inverse)
        sign = jnp.where(odd & (turns.astype(jnp.int32) % 2 != 0), -1.0, 1.0)
        return jnp.where(turns * length == n, sign, 0.0)

    for m in range(slots):
        mine = entry(metas[0], m)
        near = response(mine - others)
        far = response(mine + others)
        gram_ref[m] = factor * (near + jnp.where(cosine, far, -far))
    for copy in copies:
        copy.wait()


def table_copies(legendre, tables, sems):
    slots, _, _, degrees = tables.shape
    copies = []
    for m in range(slots):
        first = m * (degrees // slots)
        part = (m, slice(None), slice(None), pl.ds(first, degrees - first))
        copies.append(pltpu.make_async_copy(legendre.at[part], tables.at[part], sems.at[m]))
    return copies


def forward_kernel(layout, groups, meta_ref, tables, pieces_ref, *rest):
    parts = rest[: len(layout)]
    phases_ref, *messages, coefs = rest[len(layout) :]
    slots, _, count, degrees = tables.shape
    width = parts[0].shape[2]
    blocks = degrees // width
    stratum = degrees // slots
    meta = meta_ref[...]
    place = ring_place(lax.axis_index("blk"), blocks)
    for part, (low, step) in zip(parts, layout):
        first = pl.multiple_of(block_at(place + step, blocks) * width, LANES)
        for m in range(part.shape[0]):
            coefs[low + m, :, pl.ds(first, width)] = part[m]
    lane = lax.broadcasted_iota(jnp.int32, (count, LANES), 1)
    phases = jnp.zeros((count, LANES), jnp.float32)
    for m in range(slots):
        floor = jnp.maximum(entry(meta, m).astype(jnp.int32), 2)
        first = stratum * m // LANES
        p = [jnp.zeros((count, LANES), jnp.float32)] * 4
        n = [jnp.zeros((count, LANES), jnp.float32)] * 4
        for t in range(first, degrees // LANES):
            span = slice(t * LANES, (t + 1) * LANES)
            plus = tables[m, 0, :, span]
            minus = tables[m, 1, :, span]
            if t * LANES < stratum * (m + 1):
                keep = lane >= floor - t * LANES
                plus = jnp.where(keep, plus, 0.0)
                minus = jnp.where(keep, minus, 0.0)
            for a in range(4):
                c = coefs[m, a : a + 1, span]
                if t * LANES < stratum * (m + 1):
                    c = jnp.where(keep[:1], c, 0.0)
                p[a] = p[a] + plus * c
                n[a] = n[a] + minus * c
        for a, total in enumerate([n[3] - p[0], -p[1] - n[2], -p[2] - n[1], n[0] - p[3]]):
            value = jnp.sum(total, axis=1, keepdims=True)
            phases = jnp.where(lane == a * slots + m, value, phases)
    phases_ref[...] = phases
    for d in range(1, groups):
        messages[d - 1][:count] = phases
        messages[d - 1][count:] = pieces_ref[d]


def fold_rows(values, row):
    for step in (1, 2, 4):
        low = (row & step) == 0
        values = [
            jnp.where(low, values[i], values[i + 1])
            + pltpu.roll(jnp.where(low, values[i + 1], values[i]), step, 0)
            for i in range(0, len(values), 2)
        ]
    return values[0]


def backward_kernel(groups, cycles, tables, gram_ref, pieces_ref, phases_ref, *rest):
    messages = rest[: groups - 1]
    out, low_ref, high_ref, sky = rest[groups - 1 :]
    slots, _, count, degrees = tables.shape
    blocks, _, _, width = out.shape
    stratum = degrees // slots
    place = ring_place(lax.axis_index("blk"), blocks)
    owner = lax.axis_index("order")
    ring = ring_of(blocks)
    step_of = [lax.rem(ring.index(b) - place + blocks, blocks) for b in range(blocks)]
    wide = 4 * slots
    pairs = []
    for d in range(groups):
        phases = phases_ref[...] if d == 0 else messages[d - 1][:count]
        piece = pieces_ref[0] if d == 0 else messages[d - 1][count:]
        sky[pl.ds((owner ^ d) * cycles, cycles)] = piece[:cycles]
        pairs.append(phases)
    lane = lax.broadcasted_iota(jnp.int32, (count, LANES), 1)
    row8 = lax.broadcasted_iota(jnp.int32, (8, LANES), 0)
    per = LANES // wide
    packed = []
    for start in range(0, groups, per):
        value = pairs[start]
        for k in range(1, per):
            value = jnp.where(
                lane // wide == k, pltpu.roll(pairs[start + k], k * wide, 1), value
            )
        packed.append(value)
    observed = sky[...]
    for m in range(slots):
        total = jnp.where((lane < wide) & (lane % slots == m), observed, 0.0)
        for k, value in enumerate(packed):
            total = total - gram_ref[m, :, k * LANES : (k + 1) * LANES] * value
        an = []
        for a in range(4):
            value = jnp.where((lane % wide) // slots == a, total, 0.0)
            value = jnp.sum(value, axis=1, keepdims=True)
            an.append(jnp.broadcast_to(value, (count, LANES)))
        ng = [-value for value in an]
        for t in range(stratum * m // LANES, degrees // LANES, 2):
            values = []
            for u in (t, t + 1):
                span = slice(u * LANES, (u + 1) * LANES)
                plus = tables[m, 0, :, span]
                minus = tables[m, 1, :, span]
                four = [
                    plus * ng[0] + minus * an[3],
                    plus * ng[1] + minus * ng[2],
                    plus * ng[2] + minus * ng[1],
                    plus * ng[3] + minus * an[0],
                ]
                values += [
                    sum(v[8 * k : 8 * k + 8] for k in range(count // 8)) for v in four
                ]
            folded = fold_rows(values, row8)
            for k, u in enumerate((t, t + 1)):
                step = step_of[u * LANES // width]
                inner = u * LANES % width
                out[step, m, :, inner : inner + LANES] = folded[4 * k : 4 * k + 4]
    middle = low_ref.shape[0]
    low_ref[...] = out[blocks // 2, :middle]
    high_ref[...] = out[blocks // 2, middle:]


def residual_kernel(groups, slots, cycles, *rest):
    metas = [ref[...] for ref in rest[:groups]]
    sky_ref, acs_ref, asc_ref, fine_ref, phases_ref = rest[groups : groups + 5]
    messages = rest[groups + 5 : 2 * groups + 4]
    out_ref, spread = rest[2 * groups + 4 :]
    owner = lax.axis_index("order")
    rows, both = acs_ref.shape[1:]
    every = both // 2
    count = phases_ref.shape[0]
    source = lax.broadcasted_iota(jnp.int32, (LANES, both), 0)
    lane = lax.broadcasted_iota(jnp.int32, (LANES, both), 1) % every
    ids = spread_ids(metas, slots, [d for _ in range(2) for d in range(groups)])
    factor = jnp.where(ids == 0.0, 1.0, 2.0)
    for a in range(4):
        total = jnp.zeros((count, both), jnp.float32)
        for d in range(groups):
            phases = phases_ref[...] if d == 0 else messages[d - 1][:count]
            place = (lane - d * slots == source - a * slots) & (lane // slots == d)
            total = total + jnp.dot(
                phases, place.astype(jnp.float32), precision=HIGHEST,
                preferred_element_type=jnp.float32,
            )
        spread[a] = total * factor
    even = lax.broadcasted_iota(jnp.int32, (rows, both), 0) % 2 == 0
    for c in range(cycles):
        q_re, q_im, u_re, u_im = [spread[a, pl.ds(owner * cycles + c, 1)] for a in range(4)]
        weights = jnp.where(even, q_re, u_re) * acs_ref[c]
        weights = weights - jnp.where(even, q_im, u_im) * asc_ref[c]
        model = lax.dot_general(
            weights, fine_ref[c], (((1,), (1,)), ((), ())), precision=HIGHEST,
            preferred_element_type=jnp.float32,
        )
        inside = pixel_mask((rows, LANES), entry(metas[0], slots + c).astype(jnp.int32))
        out_ref[c] = jnp.where(inside, sky_ref[c] - model, 0.0)


def add_kernel(index, piece_ref, value_ref, out_ref, first=0):
    size = value_ref.shape[0]
    slots = out_ref.shape[0]
    out_ref[first : first + size] = piece_ref[index, first : first + size] + value_ref[...]
    if first:
        out_ref[:first] = piece_ref[index, :first]
    if first + size < slots:
        out_ref[first + size :] = piece_ref[index, first + size :]


def final_kernel(meta_ref, harmonics_ref, piece_ref, ahead_ref, behind_ref, out_ref):
    slots, parts, width = out_ref.shape
    start = lax.axis_index("blk") * width
    degree = start + lax.broadcasted_iota(jnp.int32, (parts, width), 1)
    meta = meta_ref[...]
    for m in range(slots):
        update = piece_ref[0, m] + ahead_ref[m] + behind_ref[m]
        valid = degree >= jnp.maximum(entry(meta, m).astype(jnp.int32), 2)
        out_ref[m] = jnp.where(valid, harmonics_ref[m] + update, 0.0)


def vmem():
    return pl.BlockSpec(memory_space=VMEM)


def shape(*dims):
    return jax.ShapeDtypeStruct(dims, jnp.float32)


def body(harmonics, legendre, sky_map, cycle_length, cycle_offset, cycle_weight, order_ids):
    groups = lax.axis_size("order")
    blocks = lax.axis_size("blk")
    slots, _, width = harmonics.shape
    count, degrees = legendre.shape[2:]
    cycles, _, pixels = sky_map.shape
    rows = pixels // LANES
    stratum = degrees // slots
    every = slots * groups
    normalise = math.sqrt(degrees * every / (cycles * groups * blocks * pixels))

    def swap(value, axis, step):
        size = lax.axis_size(axis)
        return lax.ppermute(value, axis, [(i, i ^ step) for i in range(size)])

    ring = ring_of(blocks)

    def turn(value, way, step, first=0):
        pairs = [
            (ring[p], ring[(p + way) % blocks])
            for p in range(blocks)
            if needed(ring[(p + step) % blocks], first, width, stratum)
        ]
        return lax.ppermute(value, "blk", pairs)

    hbm = pl.BlockSpec(memory_space=pl.ANY)
    small = (order_ids, cycle_length, cycle_offset, cycle_weight)
    meta = pl.pallas_call(
        lambda *refs: meta_kernel(slots, cycles, *refs),
        out_shape=pltpu.VMEM((1, LANES), jnp.float32),
        in_specs=[hbm] * 4,
        out_specs=vmem(),
        scratch_shapes=[pltpu.SMEM(v.shape, v.dtype) for v in small]
        + [pltpu.SemaphoreType.DMA((len(small),))],
        compiler_params=pltpu.CompilerParams(vmem_limit_bytes=2 * MIB),
        name="meta",
    )(*[pltpu.with_memory_space_constraint(v, pltpu.HBM) for v in small])
    harmonics, meta = lax.optimization_barrier((harmonics, meta))
    metas = [meta] + [swap(meta, "order", d) for d in range(1, groups)]

    far = blocks // 2
    middle = slots // 2
    ahead, behind = turn(harmonics, 1, 0), turn(harmonics, -1, 0)
    parts, layout = [harmonics, ahead, behind], [(0, 0), (0, -1), (0, 1)]
    ahead, behind, *metas = lax.optimization_barrier((ahead, behind, *metas))

    sky = sky_map.reshape(cycles, 2, rows, LANES).transpose(0, 2, 1, 3)
    sky = sky.reshape(cycles, 2 * rows, LANES)
    pieces, gram, acs, asc, fine, tables = pl.pallas_call(
        lambda *refs: sky_kernel(normalise, groups, slots, cycles, *refs),
        out_shape=(
            shape(groups, 8, LANES),
            shape(slots, count, 4 * every),
            shape(cycles, 2 * rows, 2 * every),
            shape(cycles, 2 * rows, 2 * every),
            shape(cycles, LANES, 2 * every),
            pltpu.VMEM(legendre.shape, jnp.float32),
        ),
        in_specs=[vmem()] * (groups + 1) + [hbm],
        out_specs=(vmem(), vmem(), vmem(), vmem(), vmem(), hbm),
        scratch_shapes=[pltpu.SemaphoreType.DMA((slots,))],
        compiler_params=pltpu.CompilerParams(vmem_limit_bytes=16 * MIB),
        cost_estimate=pl.CostEstimate(flops=10**8, bytes_accessed=12 * MIB, transcendentals=0),
        name="sky_analysis",
    )(
        *metas, sky,
        pltpu.with_memory_space_constraint(legendre, pltpu.HBM),
    )

    for k in range(2, far):
        ahead, behind = turn(ahead, 1, 1 - k), turn(behind, -1, k - 1)
        parts += [ahead, behind]
        layout += [(0, -k), (0, k)]
        if k == 2:
            ahead, behind, pieces = lax.optimization_barrier((ahead, behind, pieces))
    parts += [turn(ahead[:middle], 1, 1 - far), turn(behind[middle:], -1, far - 1, middle)]
    layout += [(0, far), (middle, far)]

    outs = pl.pallas_call(
        lambda *refs: forward_kernel(layout, groups, *refs),
        out_shape=[shape(count, LANES)] + [shape(count + 8, LANES)] * (groups - 1),
        in_specs=[vmem()] * (3 + len(parts)),
        out_specs=[vmem()] * groups,
        scratch_shapes=[pltpu.VMEM((slots, 4, degrees), jnp.float32)],
        compiler_params=pltpu.CompilerParams(vmem_limit_bytes=24 * MIB),
        cost_estimate=pl.CostEstimate(flops=10**8, bytes_accessed=8 * MIB, transcendentals=0),
        name="forward",
    )(meta, tables, pieces, *parts)
    phases = outs[0]
    messages = [swap(outs[d], "order", d) for d in range(1, groups)]

    half = pltpu.VMEM((middle, 4, width), jnp.float32)
    block = pltpu.VMEM((slots, 4, width), jnp.float32)
    piece, low_part, high_part = pl.pallas_call(
        lambda *refs: backward_kernel(groups, cycles, *refs),
        out_shape=[pltpu.VMEM((blocks, slots, 4, width), jnp.float32), half, half],
        in_specs=[vmem()] * (3 + groups),
        out_specs=[vmem()] * 3,
        scratch_shapes=[pltpu.VMEM((count, LANES), jnp.float32)],
        compiler_params=pltpu.CompilerParams(vmem_limit_bytes=24 * MIB),
        cost_estimate=pl.CostEstimate(flops=10**8, bytes_accessed=8 * MIB, transcendentals=0),
        name="backward",
    )(tables, gram, pieces, phases, *messages)

    def add(index, value, first=0):
        return pl.pallas_call(
            lambda *refs: add_kernel(index, *refs, first=first),
            out_shape=block,
            in_specs=[vmem()] * 2,
            out_specs=vmem(),
            compiler_params=pltpu.CompilerParams(vmem_limit_bytes=4 * MIB),
            cost_estimate=pl.CostEstimate(flops=10**5, bytes_accessed=10**6, transcendentals=0),
            name="add",
        )(piece, pltpu.with_memory_space_constraint(value, pltpu.VMEM))

    ahead, behind = turn(low_part, 1, far), turn(high_part, -1, -far, middle)
    ahead, behind = add(far - 1, ahead), add(far + 1, behind, middle)
    for k in reversed(range(1, far)):
        ahead, behind = turn(ahead, 1, k), turn(behind, -1, -k)
        if k > 1:
            ahead, behind = add(k - 1, ahead), add(blocks - k + 1, behind)
    refined = pl.pallas_call(
        final_kernel,
        out_shape=shape(*harmonics.shape),
        in_specs=[vmem()] * 5,
        out_specs=vmem(),
        compiler_params=pltpu.CompilerParams(vmem_limit_bytes=8 * MIB),
        cost_estimate=pl.CostEstimate(flops=10**5, bytes_accessed=10**6, transcendentals=0),
        name="refine",
    )(
        meta, harmonics, piece,
        pltpu.with_memory_space_constraint(ahead, pltpu.VMEM),
        pltpu.with_memory_space_constraint(behind, pltpu.VMEM),
    )

    residual = pl.pallas_call(
        lambda *refs: residual_kernel(groups, slots, cycles, *refs),
        out_shape=shape(cycles, 2 * rows, LANES),
        in_specs=[vmem()] * (4 + 2 * groups),
        out_specs=vmem(),
        scratch_shapes=[pltpu.VMEM((4, count, 2 * every), jnp.float32)],
        compiler_params=pltpu.CompilerParams(vmem_limit_bytes=16 * MIB),
        cost_estimate=pl.CostEstimate(flops=10**8, bytes_accessed=2 * MIB, transcendentals=0),
        name="residual",
    )(*metas, sky, acs, asc, fine, phases, *messages)
    residual = residual.reshape(cycles, rows, 2, LANES).transpose(0, 2, 1, 3)
    return (refined, residual.reshape(sky_map.shape))


def solution(mesh):
    return jax.shard_map(
        body,
        mesh=mesh,
        in_specs=(
            P("order", None, "blk"),
            P("order", None, "blk", None),
            P(("blk", "order"), None, None),
            P(("blk", "order")),
            P(("blk", "order")),
            P(("blk", "order")),
            P("order"),
        ),
        out_specs=(P("order", None, "blk"), P(("blk", "order"), None, None)),
        check_vma=False,
    )
```

```python
import math

import jax
import jax.numpy as jnp
from jax import lax
from jax.experimental import pallas as pl
from jax.experimental.pallas import tpu as pltpu
from jax.sharding import PartitionSpec as P

HIGHEST = lax.Precision.HIGHEST
LANES = 128
VMEM = pltpu.VMEM
MIB = 1024 * 1024


def ring_of(blocks):
    return list(range(0, blocks, 2)) + list(range(blocks - 1, 0, -2))


def ring_place(block, blocks):
    return jnp.where(block % 2 == 0, block // 2, blocks - 1 - block // 2)


def block_at(place, blocks):
    place = lax.rem(place + 2 * blocks, blocks)
    return jnp.where(place < blocks // 2, 2 * place, 2 * (blocks - 1 - place) + 1)


def sin_pi(x):
    turns = jnp.round(x)
    y = (x - turns) * math.pi
    z = y * y
    value = -1.0 / 39916800
    for term in (1.0 / 362880, -1.0 / 5040, 1.0 / 120, -1.0 / 6, 1.0):
        value = value * z + term
    value = value * y
    return jnp.where(turns.astype(jnp.int32) % 2 != 0, -value, value)


def half_turns(order, step, length):
    total = order * step
    period = 2 * length
    scale = 0.5 / length.astype(jnp.float32)
    for _ in range(2):
        total = total - jnp.floor(total.astype(jnp.float32) * scale).astype(jnp.int32) * period
    return total.astype(jnp.float32) / length.astype(jnp.float32)


def pixel_mask(shape, length):
    pixel = lax.broadcasted_iota(jnp.int32, shape, 0) // 2 * shape[1]
    pixel = pixel + lax.broadcasted_iota(jnp.int32, shape, 1)
    return pixel < length


def meta_kernel(slots, cycles, ids, length, offset, weight, out_ref, *scratch):
    *held, sems = scratch
    copies = [
        pltpu.make_async_copy(source, target, sems.at[k])
        for k, (source, target) in enumerate(zip((ids, length, offset, weight), held))
    ]
    for copy in copies:
        copy.start()
    for copy in copies:
        copy.wait()
    lane = lax.broadcasted_iota(jnp.int32, (1, LANES), 1)
    out = jnp.zeros((1, LANES), jnp.float32)
    for m in range(slots):
        out = jnp.where(lane == m, held[0][m].astype(jnp.float32), out)
    for c in range(cycles):
        for k in range(3):
            value = held[1 + k][c].astype(jnp.float32)
            out = jnp.where(lane == slots + k * cycles + c, value, out)
    out_ref[...] = out


def entry(meta, at):
    return meta[:, at : at + 1]


def spread_ids(metas, slots, sources):
    per = LANES // slots
    lane = lax.broadcasted_iota(jnp.int32, (1, LANES), 1)
    pieces = []
    for start in range(0, len(sources), per):
        piece = jnp.zeros((1, LANES), jnp.float32)
        for k in range(per):
            value = metas[sources[start + k]]
            value = pltpu.roll(value, k * slots, 1) if k else value
            piece = jnp.where(lane // slots == k, value, piece)
        pieces.append(piece)
    return jnp.concatenate(pieces, axis=1)


def sky_kernel(normalise, groups, slots, cycles, *rest):
    metas = [ref[...] for ref in rest[:groups]]
    sky_hbm, pieces_ref, acs_ref, asc_ref, fine_ref, section_ref, sky_ref, sky_sem = rest[groups:]
    sky_copy = pltpu.make_async_copy(sky_hbm, sky_ref, sky_sem)
    sky_copy.start()
    rows, both = acs_ref.shape[1:]
    every = both // 2
    ids = spread_ids(metas, slots, [d for _ in range(2) for d in range(groups)])
    ids = ids.astype(jnp.int32)
    row8 = lax.broadcasted_iota(jnp.int32, (8, both), 0)
    sums = [jnp.zeros((8, both), jnp.float32) for _ in range(4)]
    for c in range(cycles):
        length = entry(metas[0], slots + c).astype(jnp.int32)
        offset = entry(metas[0], slots + cycles + c).astype(jnp.int32)
        coarse = lax.broadcasted_iota(jnp.int32, (rows, both), 0) // 2 * (2 * LANES) + offset
        x = half_turns(ids, coarse, length)
        first = lax.broadcasted_iota(jnp.int32, (rows, both), 1) < every
        acs = sin_pi(x + jnp.where(first, 0.5, 1.0))
        asc = sin_pi(x + jnp.where(first, 0.0, 0.5))
        acs_ref[c] = acs
        asc_ref[c] = asc
        fine = 2 * lax.broadcasted_iota(jnp.int32, (LANES, both), 0)
        x = half_turns(ids, fine, length)
        first = lax.broadcasted_iota(jnp.int32, (LANES, both), 1) < every
        table = sin_pi(x + jnp.where(first, 0.5, 0.0))
        fine_ref[c] = table
        if c == 0:
            sky_copy.wait()
        section = jnp.where(pixel_mask((rows, LANES), length), sky_ref[c], 0.0)
        section_ref[c] = section
        spun = jnp.dot(section, table, precision=HIGHEST, preferred_element_type=jnp.float32)
        weight = entry(metas[0], slots + 2 * cycles + c) * normalise
        for k, value in enumerate((spun * acs, spun * asc)):
            value = sum(value[8 * i : 8 * i + 8] for i in range(rows // 8))
            for q in range(2):
                total = jnp.sum(jnp.where(row8 % 2 == q, value, 0.0), axis=0, keepdims=True)
                total = total * (-weight if k else weight)
                sums[2 * q + k] = jnp.where(row8 == c, total, sums[2 * q + k])
    lane = lax.broadcasted_iota(jnp.int32, (8, LANES), 1)
    totals = []
    for value in sums:
        tiles = [value[:, i : i + LANES] for i in range(0, both, LANES)]
        if every < LANES:
            shift = every
            while shift < LANES:
                tiles[0] = tiles[0] + pltpu.roll(tiles[0], shift, 1)
                shift *= 2
            totals.append(tiles)
        else:
            half = len(tiles) // 2
            totals.append([tiles[i] + tiles[half + i] for i in range(half)])
    for d in range(groups):
        piece = jnp.zeros((8, LANES), jnp.float32)
        tile, at = divmod(d * slots, LANES)
        for a in range(4):
            shift = (a * slots - at) % LANES
            value = totals[a][tile]
            value = pltpu.roll(value, shift, 1) if shift else value
            piece = jnp.where(lane // slots == a, value, piece)
        pieces_ref[d] = piece


def gram_kernel(normalise, groups, slots, cycles, *rest):
    metas = [ref[...] for ref in rest[:groups]]
    (gram_ref,) = rest[groups:]
    me = lax.axis_index("order")
    count, wide = gram_ref.shape[1:]
    row = lax.broadcasted_iota(jnp.int32, (count, wide), 0)
    length = jnp.ones((count, wide), jnp.float32)
    offset = jnp.zeros((count, wide), jnp.float32)
    weight = jnp.zeros((count, wide), jnp.float32)
    for d in range(groups):
        for c in range(cycles):
            here = row == (me ^ d) * cycles + c
            length = jnp.where(here, entry(metas[d], slots + c), length)
            offset = jnp.where(here, entry(metas[d], slots + cycles + c), offset)
            weight = jnp.where(here, entry(metas[d], slots + 2 * cycles + c), weight)
    others = spread_ids(metas, slots, [d for d in range(groups) for _ in range(4)])
    lane = lax.broadcasted_iota(jnp.int32, (count, wide), 1)
    cosine = (lane // slots) % 2 == 0
    factor = jnp.where(others == 0.0, 0.5, 1.0) * normalise * weight * length
    inverse = 1.0 / length
    odd = offset > 0.5

    def response(n):
        turns = jnp.round(n * inverse)
        sign = jnp.where(odd & (turns.astype(jnp.int32) % 2 != 0), -1.0, 1.0)
        return jnp.where(turns * length == n, sign, 0.0)

    for m in range(slots):
        mine = entry(metas[0], m)
        near = response(mine - others)
        far = response(mine + others)
        gram_ref[m] = factor * (near + jnp.where(cosine, far, -far))


def table_copies(legendre, tables, sems):
    slots, _, _, degrees = tables.shape
    copies = []
    for m in range(slots):
        first = m * (degrees // slots)
        part = (m, slice(None), slice(None), pl.ds(first, degrees - first))
        copies.append(pltpu.make_async_copy(legendre.at[part], tables.at[part], sems.at[m]))
    return copies


def use_tile(tables, m, span, keep, coefs, p, n):
    plus = tables[m, 0, :, span]
    minus = tables[m, 1, :, span]
    if keep is not None:
        plus = jnp.where(keep, plus, 0.0)
        minus = jnp.where(keep, minus, 0.0)
    for a in range(4):
        c = coefs(a)
        if keep is not None:
            c = jnp.where(keep[:1], c, 0.0)
        p[a] = p[a] + plus * c
        n[a] = n[a] + minus * c


def combine(p, n):
    return [n[3] - p[0], -p[1] - n[2], -p[2] - n[1], n[0] - p[3]]


def tables_kernel(legendre, tables, sems):
    copies = table_copies(legendre, tables, sems)
    for copy in copies:
        copy.start()
    for copy in copies:
        copy.wait()


def forward_kernel(steps, firsts, meta_ref, tables, *rest):
    parts = rest[: len(steps)]
    sums_ref, coefs = rest[len(steps) :]
    slots, _, count, degrees = tables.shape
    width = parts[0].shape[2]
    blocks = degrees // width
    stratum = degrees // slots
    meta = meta_ref[...]
    place = ring_place(lax.axis_index("blk"), blocks)
    for part, step, low in zip(parts, steps, firsts):
        first = pl.multiple_of(block_at(place + step, blocks) * width, LANES)
        for m in range(part.shape[0]):
            coefs[low + m, :, pl.ds(first, width)] = part[m]
    first = pl.multiple_of(block_at(place + blocks // 2, blocks) * width, LANES)
    for m in range(slots):
        coefs[m, :, pl.ds(first, width)] = jnp.zeros((4, width), jnp.float32)
    lane = lax.broadcasted_iota(jnp.int32, (count, LANES), 1)
    for m in range(slots):
        floor = jnp.maximum(entry(meta, m).astype(jnp.int32), 2)
        p = [jnp.zeros((count, LANES), jnp.float32)] * 4
        n = [jnp.zeros((count, LANES), jnp.float32)] * 4
        for t in range(stratum * m // LANES, degrees // LANES):
            span = slice(t * LANES, (t + 1) * LANES)
            keep = lane >= floor - t * LANES if t * LANES < stratum * (m + 1) else None
            use_tile(tables, m, span, keep, lambda a: coefs[m, a : a + 1, span], p, n)
        for a, total in enumerate(combine(p, n)):
            sums_ref[m, a] = total


def phases_kernel(groups, meta_ref, tables, pieces_ref, sums_ref, low_ref, high_ref, *rest):
    phases_ref, *messages = rest
    slots, _, count, degrees = tables.shape
    middle, _, width = low_ref.shape
    blocks = degrees // width
    meta = meta_ref[...]
    place = ring_place(lax.axis_index("blk"), blocks)
    first = pl.multiple_of(block_at(place + blocks // 2, blocks) * width, LANES)
    lane = lax.broadcasted_iota(jnp.int32, (count, LANES), 1)
    phases = jnp.zeros((count, LANES), jnp.float32)
    for m in range(slots):
        floor = jnp.maximum(entry(meta, m).astype(jnp.int32), 2) - first
        part, at = (low_ref, m) if m < middle else (high_ref, m - middle)
        p = [jnp.zeros((count, LANES), jnp.float32)] * 4
        n = [jnp.zeros((count, LANES), jnp.float32)] * 4
        for t in range(width // LANES):
            here = slice(t * LANES, (t + 1) * LANES)
            keep = lane >= floor - t * LANES
            span = pl.ds(first + t * LANES, LANES)
            use_tile(tables, m, span, keep, lambda a: part[at, a : a + 1, here], p, n)
        for a, total in enumerate(combine(p, n)):
            value = jnp.sum(total + sums_ref[m, a], axis=1, keepdims=True)
            phases = jnp.where(lane == a * slots + m, value, phases)
    phases_ref[...] = phases
    for d in range(1, groups):
        messages[d - 1][:count] = phases
        messages[d - 1][count:] = pieces_ref[d]


def fold_rows(values, row):
    for step in (1, 2, 4):
        low = (row & step) == 0
        values = [
            jnp.where(low, values[i], values[i + 1])
            + pltpu.roll(jnp.where(low, values[i + 1], values[i]), step, 0)
            for i in range(0, len(values), 2)
        ]
    return values[0]


def update_tiles(tables, m, spans, an, ng, row8):
    count = tables.shape[2]
    values = []
    for span in spans:
        plus = tables[m, 0, :, span]
        minus = tables[m, 1, :, span]
        four = [
            plus * ng[0] + minus * an[3],
            plus * ng[1] + minus * ng[2],
            plus * ng[2] + minus * ng[1],
            plus * ng[3] + minus * an[0],
        ]
        values += [sum(v[8 * k : 8 * k + 8] for k in range(count // 8)) for v in four]
    return fold_rows(values, row8)


def analysed_kernel(groups, cycles, tables, gram_ref, pieces_ref, phases_ref, *rest):
    messages = rest[: groups - 1]
    *sends, analysed_ref, sky = rest[groups - 1 :]
    slots, _, count, degrees = tables.shape
    middle, _, width = sends[0].shape
    blocks = degrees // width
    far = blocks // 2
    place = ring_place(lax.axis_index("blk"), blocks)
    firsts = [
        pl.multiple_of(block_at(place + step, blocks) * width, LANES)
        for step in (far, -far, 1 - far, far - 1)
    ]
    owner = lax.axis_index("order")
    wide = 4 * slots
    pairs = []
    for d in range(groups):
        phases = phases_ref[...] if d == 0 else messages[d - 1][:count]
        piece = pieces_ref[0] if d == 0 else messages[d - 1][count:]
        sky[pl.ds((owner ^ d) * cycles, cycles)] = piece[:cycles]
        pairs.append(phases)
    lane = lax.broadcasted_iota(jnp.int32, (count, LANES), 1)
    row8 = lax.broadcasted_iota(jnp.int32, (8, LANES), 0)
    per = LANES // wide
    packed = []
    for start in range(0, groups, per):
        value = pairs[start]
        for k in range(1, per):
            value = jnp.where(
                lane // wide == k, pltpu.roll(pairs[start + k], k * wide, 1), value
            )
        packed.append(value)
    observed = sky[...]
    for m in range(slots):
        total = jnp.where((lane < wide) & (lane % slots == m), observed, 0.0)
        for k, value in enumerate(packed):
            total = total - gram_ref[m, :, k * LANES : (k + 1) * LANES] * value
        an = []
        for a in range(4):
            value = jnp.where((lane % wide) // slots == a, total, 0.0)
            value = jnp.sum(value, axis=1, keepdims=True)
            an.append(jnp.broadcast_to(value, (count, LANES)))
            analysed_ref[m, a] = an[a]
        ng = [-value for value in an]
        half, at = divmod(m, middle)
        for part, first in zip(sends[half::2], firsts[half::2]):
            for t in range(0, width // LANES, 2):
                spans = [pl.ds(first + u * LANES, LANES) for u in (t, t + 1)]
                folded = update_tiles(tables, m, spans, an, ng, row8)
                for k, u in enumerate((t, t + 1)):
                    part[at, :, u * LANES : (u + 1) * LANES] = folded[4 * k : 4 * k + 4]


def backward_kernel(tables, analysed_ref, out):
    slots, _, _, degrees = tables.shape
    blocks, _, _, width = out.shape
    stratum = degrees // slots
    place = ring_place(lax.axis_index("blk"), blocks)
    ring = ring_of(blocks)
    step_of = [lax.rem(ring.index(b) - place + blocks, blocks) for b in range(blocks)]
    row8 = lax.broadcasted_iota(jnp.int32, (8, LANES), 0)
    for m in range(slots):
        an = [analysed_ref[m, a] for a in range(4)]
        ng = [-value for value in an]
        for t in range(stratum * m // LANES, degrees // LANES, 2):
            spans = [slice(u * LANES, (u + 1) * LANES) for u in (t, t + 1)]
            folded = update_tiles(tables, m, spans, an, ng, row8)
            for k, u in enumerate((t, t + 1)):
                inner = u * LANES % width
                out[step_of[u * LANES // width], m, :, inner : inner + LANES] = folded[
                    4 * k : 4 * k + 4
                ]


def residual_kernel(groups, slots, cycles, *rest):
    metas = [ref[...] for ref in rest[:groups]]
    section_ref, acs_ref, asc_ref, fine_ref, phases_ref = rest[groups : groups + 5]
    messages = rest[groups + 5 : 2 * groups + 4]
    out_ref, spread = rest[2 * groups + 4 :]
    owner = lax.axis_index("order")
    rows, both = acs_ref.shape[1:]
    every = both // 2
    count = phases_ref.shape[0]
    lane = lax.broadcasted_iota(jnp.int32, (count, LANES), 1)
    ids = spread_ids(metas, slots, [d for _ in range(2) for d in range(groups)])
    factor = jnp.where(ids == 0.0, 1.0, 2.0)
    per = LANES // slots
    values = [phases_ref[...]] + [ref[:count] for ref in messages]
    for a in range(4):
        tiles = []
        for start in range(0, 2 * groups, per):
            tile = jnp.zeros((count, LANES), jnp.float32)
            for k in range(per):
                shift = (k - a) * slots % LANES
                value = values[(start + k) % groups]
                value = pltpu.roll(value, shift, 1) if shift else value
                tile = jnp.where(lane // slots == k, value, tile)
            tiles.append(tile)
        spread[a] = jnp.concatenate(tiles, axis=1) * factor
    even = lax.broadcasted_iota(jnp.int32, (rows, both), 0) % 2 == 0
    for c in range(cycles):
        q_re, q_im, u_re, u_im = [spread[a, pl.ds(owner * cycles + c, 1)] for a in range(4)]
        weights = jnp.where(even, q_re, u_re) * acs_ref[c]
        weights = weights - jnp.where(even, q_im, u_im) * asc_ref[c]
        model = lax.dot_general(
            weights, fine_ref[c], (((1,), (1,)), ((), ())), precision=HIGHEST,
            preferred_element_type=jnp.float32,
        )
        inside = pixel_mask((rows, LANES), entry(metas[0], slots + c).astype(jnp.int32))
        out_ref[c] = section_ref[c] - jnp.where(inside, model, 0.0)


def add_kernel(index, first, piece_ref, value_ref, out_ref):
    out_ref[...] = piece_ref[index, first : first + out_ref.shape[0]] + value_ref[...]


def final_kernel(meta_ref, harmonics_ref, piece_ref, *rest):
    *received, out_ref = rest
    slots, parts, width = out_ref.shape
    middle = slots // 2
    start = lax.axis_index("blk") * width
    degree = start + lax.broadcasted_iota(jnp.int32, (parts, width), 1)
    meta = meta_ref[...]
    for m in range(slots):
        h, at = divmod(m, middle)
        update = piece_ref[0, m] + (received[h][at] + received[2 + h][at])
        valid = degree >= jnp.maximum(entry(meta, m).astype(jnp.int32), 2)
        out_ref[m] = jnp.where(valid, harmonics_ref[m] + update, 0.0)


def vmem():
    return pl.BlockSpec(memory_space=VMEM)


def shape(*dims):
    return jax.ShapeDtypeStruct(dims, jnp.float32)


def body(harmonics, legendre, sky_map, cycle_length, cycle_offset, cycle_weight, order_ids):
    groups = lax.axis_size("order")
    blocks = lax.axis_size("blk")
    slots, _, width = harmonics.shape
    count, degrees = legendre.shape[2:]
    cycles, _, pixels = sky_map.shape
    rows = pixels // LANES
    every = slots * groups
    normalise = math.sqrt(degrees * every / (cycles * groups * blocks * pixels))

    def swap(value, axis, step):
        size = lax.axis_size(axis)
        return lax.ppermute(value, axis, [(i, i ^ step) for i in range(size)])

    ring = ring_of(blocks)

    def turn(value, way):
        pairs = [(ring[p], ring[(p + way) % blocks]) for p in range(blocks)]
        return lax.ppermute(value, "blk", pairs)

    def estimate(micros):
        return pl.CostEstimate(flops=0, bytes_accessed=int(micros * 3.0e6), transcendentals=0)

    hbm = pl.BlockSpec(memory_space=pl.ANY)
    small = (order_ids, cycle_length, cycle_offset, cycle_weight)
    meta = pl.pallas_call(
        lambda *refs: meta_kernel(slots, cycles, *refs),
        out_shape=pltpu.VMEM((1, LANES), jnp.float32),
        in_specs=[hbm] * 4,
        out_specs=vmem(),
        scratch_shapes=[pltpu.SMEM(v.shape, v.dtype) for v in small]
        + [pltpu.SemaphoreType.DMA((len(small),))],
        compiler_params=pltpu.CompilerParams(vmem_limit_bytes=2 * MIB),
        name="meta",
    )(*[pltpu.with_memory_space_constraint(v, pltpu.HBM) for v in small])
    metas = [meta] + [swap(meta, "order", d) for d in range(1, groups)]

    far = blocks // 2
    middle = slots // 2
    ahead, behind = turn(harmonics, 1), turn(harmonics, -1)
    parts, steps, firsts = [harmonics, ahead, behind], [0, -1, 1], [0, 0, 0]
    tables = pl.pallas_call(
        tables_kernel,
        out_shape=pltpu.VMEM(legendre.shape, jnp.float32),
        in_specs=[hbm],
        out_specs=hbm,
        scratch_shapes=[pltpu.SemaphoreType.DMA((slots,))],
        compiler_params=pltpu.CompilerParams(vmem_limit_bytes=2 * MIB),
        cost_estimate=estimate(1.5),
        name="tables",
    )(pltpu.with_memory_space_constraint(legendre, pltpu.HBM))
    behind, tables, *metas = lax.optimization_barrier((behind, tables, *metas))
    ahead = [ahead[:middle], ahead[middle:]]
    behind = [behind[:middle], behind[middle:]]

    sky = sky_map.reshape(cycles, 2, rows, LANES).transpose(0, 2, 1, 3)
    sky = sky.reshape(cycles, 2 * rows, LANES)
    pieces, acs, asc, fine, section = pl.pallas_call(
        lambda *refs: sky_kernel(normalise, groups, slots, cycles, *refs),
        out_shape=(
            shape(groups, 8, LANES),
            shape(cycles, 2 * rows, 2 * every),
            shape(cycles, 2 * rows, 2 * every),
            shape(cycles, LANES, 2 * every),
            shape(cycles, 2 * rows, LANES),
        ),
        in_specs=[vmem()] * groups + [hbm],
        out_specs=(vmem(),) * 5,
        scratch_shapes=[
            pltpu.VMEM((cycles, 2 * rows, LANES), jnp.float32),
            pltpu.SemaphoreType.DMA,
        ],
        compiler_params=pltpu.CompilerParams(vmem_limit_bytes=16 * MIB),
        cost_estimate=estimate(3),
        name="sky_analysis",
    )(*metas, pltpu.with_memory_space_constraint(sky, pltpu.HBM))
    gram = pl.pallas_call(
        lambda *refs: gram_kernel(normalise, groups, slots, cycles, *refs),
        out_shape=shape(slots, count, 4 * every),
        in_specs=[vmem()] * groups,
        out_specs=vmem(),
        compiler_params=pltpu.CompilerParams(vmem_limit_bytes=8 * MIB),
        cost_estimate=estimate(1),
        name="response",
    )(*metas)

    for k in range(2, far):
        ahead = [turn(value, 1) for value in ahead]
        behind = [turn(value, -1) for value in behind[::-1]][::-1]
        parts += ahead + behind
        steps += [-k, -k, k, k]
        firsts += [0, middle] * 2
        if k == 2:
            behind[0], pieces = lax.optimization_barrier((behind[0], pieces))
        if k == 3:
            behind[0], gram = lax.optimization_barrier((behind[0], gram))
    ends = [turn(ahead[0], 1), turn(behind[1], -1)]

    whole = pltpu.VMEM((slots, 4, count, LANES), jnp.float32)
    sums = pl.pallas_call(
        lambda *refs: forward_kernel(steps, firsts, *refs),
        out_shape=whole,
        in_specs=[vmem()] * (2 + len(parts)),
        out_specs=vmem(),
        scratch_shapes=[pltpu.VMEM((slots, 4, degrees), jnp.float32)],
        compiler_params=pltpu.CompilerParams(vmem_limit_bytes=24 * MIB),
        cost_estimate=estimate(2),
        name="forward",
    )(meta, tables, *parts)
    phases, *outs = pl.pallas_call(
        lambda *refs: phases_kernel(groups, *refs),
        out_shape=[shape(count, LANES)] + [shape(count + 8, LANES)] * (groups - 1),
        in_specs=[vmem()] * 6,
        out_specs=[vmem()] * groups,
        compiler_params=pltpu.CompilerParams(vmem_limit_bytes=16 * MIB),
        cost_estimate=estimate(1),
        name="phases",
    )(meta, tables, pieces, sums, *ends)
    messages = [swap(outs[d - 1], "order", d) for d in range(1, groups)]

    half = pltpu.VMEM((middle, 4, width), jnp.float32)
    *sends, analysed = pl.pallas_call(
        lambda *refs: analysed_kernel(groups, cycles, *refs),
        out_shape=[half] * 4 + [whole],
        in_specs=[vmem()] * (3 + groups),
        out_specs=[vmem()] * 5,
        scratch_shapes=[pltpu.VMEM((count, LANES), jnp.float32)],
        compiler_params=pltpu.CompilerParams(vmem_limit_bytes=16 * MIB),
        cost_estimate=estimate(1),
        name="analysed",
    )(tables, gram, pieces, phases, *messages)
    piece = pl.pallas_call(
        backward_kernel,
        out_shape=pltpu.VMEM((blocks, slots, 4, width), jnp.float32),
        in_specs=[vmem()] * 2,
        out_specs=vmem(),
        compiler_params=pltpu.CompilerParams(vmem_limit_bytes=16 * MIB),
        cost_estimate=estimate(2),
        name="backward",
    )(tables, analysed)

    def add(index, first, value):
        return pl.pallas_call(
            lambda *refs: add_kernel(index, first, *refs),
            out_shape=half,
            in_specs=[vmem()] * 2,
            out_specs=vmem(),
            compiler_params=pltpu.CompilerParams(vmem_limit_bytes=4 * MIB),
            cost_estimate=estimate(0.1),
            name="add",
        )(piece, pltpu.with_memory_space_constraint(value, pltpu.VMEM))

    sent = dict(zip(((1, 0), (-1, middle), (-1, 0), (1, middle)), sends))
    first_hop = {key: turn(sent[key], key[0]) for key in ((1, 0), (-1, middle))}
    for key in ((1, 0), (-1, middle)):
        sent[key] = add((key[0] * (far - 1)) % blocks, key[1], first_hop[key])
    for k in reversed(range(1, far)):
        for key in ((1, middle), (-1, 0), (1, 0), (-1, middle)):
            sent[key] = turn(sent[key], key[0])
            if k > 1:
                sent[key] = add((key[0] * (k - 1)) % blocks, key[1], sent[key])
    received = [sent[key] for key in ((1, 0), (1, middle), (-1, 0), (-1, middle))]
    refined = pl.pallas_call(
        final_kernel,
        out_shape=shape(*harmonics.shape),
        in_specs=[vmem()] * 7,
        out_specs=vmem(),
        compiler_params=pltpu.CompilerParams(vmem_limit_bytes=8 * MIB),
        cost_estimate=pl.CostEstimate(flops=10**5, bytes_accessed=10**6, transcendentals=0),
        name="refine",
    )(
        meta, harmonics, piece,
        *[pltpu.with_memory_space_constraint(value, pltpu.VMEM) for value in received],
    )

    residual = pl.pallas_call(
        lambda *refs: residual_kernel(groups, slots, cycles, *refs),
        out_shape=shape(cycles, 2 * rows, LANES),
        in_specs=[vmem()] * (4 + 2 * groups),
        out_specs=vmem(),
        scratch_shapes=[pltpu.VMEM((4, count, 2 * every), jnp.float32)],
        compiler_params=pltpu.CompilerParams(vmem_limit_bytes=16 * MIB),
        cost_estimate=pl.CostEstimate(flops=10**8, bytes_accessed=2 * MIB, transcendentals=0),
        name="residual",
    )(*metas, section, acs, asc, fine, phases, *messages)
    residual = residual.reshape(cycles, rows, 2, LANES).transpose(0, 2, 1, 3)
    return (refined, residual.reshape(sky_map.shape))


def solution(mesh):
    return jax.shard_map(
        body,
        mesh=mesh,
        in_specs=(
            P("order", None, "blk"),
            P("order", None, "blk", None),
            P(("blk", "order"), None, None),
            P(("blk", "order")),
            P(("blk", "order")),
            P(("blk", "order")),
            P("order"),
        ),
        out_specs=(P("order", None, "blk"), P(("blk", "order"), None, None)),
        check_vma=False,
    )
```

```python
import math

import jax
import jax.numpy as jnp
from jax import lax
from jax.experimental import pallas as pl
from jax.experimental.pallas import tpu as pltpu
from jax.sharding import PartitionSpec as P

HIGHEST = lax.Precision.HIGHEST
LANES = 128
VMEM = pltpu.VMEM
MIB = 1024 * 1024


def ring_of(blocks):
    return list(range(0, blocks, 2)) + list(range(blocks - 1, 0, -2))


def ring_place(block, blocks):
    return jnp.where(block % 2 == 0, block // 2, blocks - 1 - block // 2)


def block_at(place, blocks):
    place = lax.rem(place + 2 * blocks, blocks)
    return jnp.where(place < blocks // 2, 2 * place, 2 * (blocks - 1 - place) + 1)


def sin_pi(x):
    turns = jnp.round(x)
    y = (x - turns) * math.pi
    z = y * y
    value = -1.0 / 39916800
    for term in (1.0 / 362880, -1.0 / 5040, 1.0 / 120, -1.0 / 6, 1.0):
        value = value * z + term
    value = value * y
    return jnp.where(turns.astype(jnp.int32) % 2 != 0, -value, value)


def half_turns(order, step, length):
    total = order * step
    period = 2 * length
    scale = 0.5 / length.astype(jnp.float32)
    for _ in range(2):
        total = total - jnp.floor(total.astype(jnp.float32) * scale).astype(jnp.int32) * period
    return total.astype(jnp.float32) / length.astype(jnp.float32)


def pixel_mask(shape, length):
    pixel = lax.broadcasted_iota(jnp.int32, shape, 0) // 2 * shape[1]
    pixel = pixel + lax.broadcasted_iota(jnp.int32, shape, 1)
    return pixel < length


def meta_kernel(slots, cycles, ids, length, offset, weight, out_ref, *scratch):
    *held, sems = scratch
    copies = [
        pltpu.make_async_copy(source, target, sems.at[k])
        for k, (source, target) in enumerate(zip((ids, length, offset, weight), held))
    ]
    for copy in copies:
        copy.start()
    for copy in copies:
        copy.wait()
    lane = lax.broadcasted_iota(jnp.int32, (1, LANES), 1)
    out = jnp.zeros((1, LANES), jnp.float32)
    for m in range(slots):
        out = jnp.where(lane == m, held[0][m].astype(jnp.float32), out)
    for c in range(cycles):
        for k in range(3):
            value = held[1 + k][c].astype(jnp.float32)
            out = jnp.where(lane == slots + k * cycles + c, value, out)
    out_ref[...] = out


def entry(meta, at):
    return meta[:, at : at + 1]


def spread_ids(metas, slots, sources):
    per = LANES // slots
    lane = lax.broadcasted_iota(jnp.int32, (1, LANES), 1)
    pieces = []
    for start in range(0, len(sources), per):
        piece = jnp.zeros((1, LANES), jnp.float32)
        for k in range(per):
            value = metas[sources[start + k]]
            value = pltpu.roll(value, k * slots, 1) if k else value
            piece = jnp.where(lane // slots == k, value, piece)
        pieces.append(piece)
    return jnp.concatenate(pieces, axis=1)


def sky_kernel(normalise, groups, slots, cycles, *rest):
    metas = [ref[...] for ref in rest[:groups]]
    sky_hbm, pieces_ref, acs_ref, asc_ref, fine_ref, section_ref, sky_ref, sky_sem = rest[groups:]
    sky_copy = pltpu.make_async_copy(sky_hbm, sky_ref, sky_sem)
    sky_copy.start()
    rows, both = acs_ref.shape[1:]
    every = both // 2
    ids = spread_ids(metas, slots, [d for _ in range(2) for d in range(groups)])
    ids = ids.astype(jnp.int32)
    row8 = lax.broadcasted_iota(jnp.int32, (8, both), 0)
    sums = [jnp.zeros((8, both), jnp.float32) for _ in range(4)]
    for c in range(cycles):
        length = entry(metas[0], slots + c).astype(jnp.int32)
        offset = entry(metas[0], slots + cycles + c).astype(jnp.int32)
        coarse = lax.broadcasted_iota(jnp.int32, (rows, both), 0) // 2 * (2 * LANES) + offset
        x = half_turns(ids, coarse, length)
        first = lax.broadcasted_iota(jnp.int32, (rows, both), 1) < every
        acs = sin_pi(x + jnp.where(first, 0.5, 1.0))
        asc = sin_pi(x + jnp.where(first, 0.0, 0.5))
        acs_ref[c] = acs
        asc_ref[c] = asc
        fine = 2 * lax.broadcasted_iota(jnp.int32, (LANES, both), 0)
        x = half_turns(ids, fine, length)
        first = lax.broadcasted_iota(jnp.int32, (LANES, both), 1) < every
        table = sin_pi(x + jnp.where(first, 0.5, 0.0))
        fine_ref[c] = table
        if c == 0:
            sky_copy.wait()
        section = jnp.where(pixel_mask((rows, LANES), length), sky_ref[c], 0.0)
        section_ref[c] = section
        spun = jnp.dot(section, table, precision=HIGHEST, preferred_element_type=jnp.float32)
        weight = entry(metas[0], slots + 2 * cycles + c) * normalise
        for k, value in enumerate((spun * acs, spun * asc)):
            value = sum(value[8 * i : 8 * i + 8] for i in range(rows // 8))
            for q in range(2):
                total = jnp.sum(jnp.where(row8 % 2 == q, value, 0.0), axis=0, keepdims=True)
                total = total * (-weight if k else weight)
                sums[2 * q + k] = jnp.where(row8 == c, total, sums[2 * q + k])
    lane = lax.broadcasted_iota(jnp.int32, (8, LANES), 1)
    totals = []
    for value in sums:
        tiles = [value[:, i : i + LANES] for i in range(0, both, LANES)]
        if every < LANES:
            shift = every
            while shift < LANES:
                tiles[0] = tiles[0] + pltpu.roll(tiles[0], shift, 1)
                shift *= 2
            totals.append(tiles)
        else:
            half = len(tiles) // 2
            totals.append([tiles[i] + tiles[half + i] for i in range(half)])
    for d in range(groups):
        piece = jnp.zeros((8, LANES), jnp.float32)
        tile, at = divmod(d * slots, LANES)
        for a in range(4):
            shift = (a * slots - at) % LANES
            value = totals[a][tile]
            value = pltpu.roll(value, shift, 1) if shift else value
            piece = jnp.where(lane // slots == a, value, piece)
        pieces_ref[d] = piece


def gram_kernel(normalise, groups, slots, cycles, *rest):
    metas = [ref[...] for ref in rest[:groups]]
    (gram_ref,) = rest[groups:]
    me = lax.axis_index("order")
    count, wide = gram_ref.shape[1:]
    row = lax.broadcasted_iota(jnp.int32, (count, wide), 0)
    length = jnp.ones((count, wide), jnp.float32)
    offset = jnp.zeros((count, wide), jnp.float32)
    weight = jnp.zeros((count, wide), jnp.float32)
    for d in range(groups):
        for c in range(cycles):
            here = row == (me ^ d) * cycles + c
            length = jnp.where(here, entry(metas[d], slots + c), length)
            offset = jnp.where(here, entry(metas[d], slots + cycles + c), offset)
            weight = jnp.where(here, entry(metas[d], slots + 2 * cycles + c), weight)
    others = spread_ids(metas, slots, [d for d in range(groups) for _ in range(4)])
    lane = lax.broadcasted_iota(jnp.int32, (count, wide), 1)
    cosine = (lane // slots) % 2 == 0
    factor = jnp.where(others == 0.0, 0.5, 1.0) * normalise * weight * length
    inverse = 1.0 / length
    odd = offset > 0.5

    def response(n):
        turns = jnp.round(n * inverse)
        sign = jnp.where(odd & (turns.astype(jnp.int32) % 2 != 0), -1.0, 1.0)
        return jnp.where(turns * length == n, sign, 0.0)

    for m in range(slots):
        mine = entry(metas[0], m)
        near = response(mine - others)
        far = response(mine + others)
        gram_ref[m] = factor * (near + jnp.where(cosine, far, -far))


def table_copies(legendre, tables, sems):
    slots, _, _, degrees = tables.shape
    copies = []
    for m in range(slots):
        first = m * (degrees // slots)
        part = (m, slice(None), slice(None), pl.ds(first, degrees - first))
        copies.append(pltpu.make_async_copy(legendre.at[part], tables.at[part], sems.at[m]))
    return copies


def use_tile(tables, m, span, keep, coefs, p, n):
    plus = tables[m, 0, :, span]
    minus = tables[m, 1, :, span]
    if keep is not None:
        plus = jnp.where(keep, plus, 0.0)
        minus = jnp.where(keep, minus, 0.0)
    for a in range(4):
        c = coefs(a)
        if keep is not None:
            c = jnp.where(keep[:1], c, 0.0)
        p[a] = p[a] + plus * c
        n[a] = n[a] + minus * c


def fold_lanes(values, lane):
    step = 1
    while step < LANES:
        if len(values) > 1:
            low = (lane & step) == 0
            values = [
                jnp.where(low, values[i], values[i + 1])
                + pltpu.roll(jnp.where(low, values[i + 1], values[i]), step, 1)
                for i in range(0, len(values), 2)
            ]
        else:
            values = [values[0] + pltpu.roll(values[0], step, 1)]
        step *= 2
    return values[0]


def combine(p, n):
    return [n[3] - p[0], -p[1] - n[2], -p[2] - n[1], n[0] - p[3]]


def on_core(core):
    return lax.axis_index("order") % 2 == core


def tables_kernel(legendre, tables, sems):
    copies = table_copies(legendre, tables, sems)
    for copy in copies:
        copy.start()
    for copy in copies:
        copy.wait()


def forward_kernel(steps, firsts, meta_ref, tables, *rest):
    parts = rest[: len(steps)]
    sums_ref, coefs = rest[len(steps) :]
    slots, _, count, degrees = tables.shape
    width = parts[0].shape[2]
    blocks = degrees // width
    stratum = degrees // slots
    meta = meta_ref[...]
    place = ring_place(lax.axis_index("blk"), blocks)
    for part, step, low in zip(parts, steps, firsts):
        first = pl.multiple_of(block_at(place + step, blocks) * width, LANES)
        for m in range(part.shape[0]):
            coefs[low + m, :, pl.ds(first, width)] = part[m]
    first = pl.multiple_of(block_at(place + blocks // 2, blocks) * width, LANES)
    for m in range(slots):
        coefs[m, :, pl.ds(first, width)] = jnp.zeros((4, width), jnp.float32)
    lane = lax.broadcasted_iota(jnp.int32, (count, LANES), 1)
    for m in range(slots):
        floor = jnp.maximum(entry(meta, m).astype(jnp.int32), 2)
        p = [jnp.zeros((count, LANES), jnp.float32)] * 4
        n = [jnp.zeros((count, LANES), jnp.float32)] * 4
        for t in range(stratum * m // LANES, degrees // LANES):
            span = slice(t * LANES, (t + 1) * LANES)
            keep = lane >= floor - t * LANES if t * LANES < stratum * (m + 1) else None
            use_tile(tables, m, span, keep, lambda a: coefs[m, a : a + 1, span], p, n)
        for a, total in enumerate(combine(p, n)):
            sums_ref[m, a] = total


def phases_kernel(groups, meta_ref, tables, pieces_ref, sums_ref, low_ref, high_ref, *rest):
    phases_ref, *messages = rest
    slots, _, count, degrees = tables.shape
    middle, _, width = low_ref.shape
    blocks = degrees // width
    meta = meta_ref[...]
    place = ring_place(lax.axis_index("blk"), blocks)
    first = pl.multiple_of(block_at(place + blocks // 2, blocks) * width, LANES)
    lane = lax.broadcasted_iota(jnp.int32, (count, LANES), 1)
    totals = [None] * (4 * slots)
    for m in range(slots):
        floor = jnp.maximum(entry(meta, m).astype(jnp.int32), 2) - first
        part, at = (low_ref, m) if m < middle else (high_ref, m - middle)
        p = [jnp.zeros((count, LANES), jnp.float32)] * 4
        n = [jnp.zeros((count, LANES), jnp.float32)] * 4
        for t in range(width // LANES):
            here = slice(t * LANES, (t + 1) * LANES)
            keep = lane >= floor - t * LANES
            span = pl.ds(first + t * LANES, LANES)
            use_tile(tables, m, span, keep, lambda a: part[at, a : a + 1, here], p, n)
        for a, total in enumerate(combine(p, n)):
            totals[a * slots + m] = total + sums_ref[m, a]
    phases = fold_lanes(totals, lane)
    phases_ref[...] = phases
    for d in range(1, groups):
        messages[d - 1][:count] = phases
        messages[d - 1][count:] = pieces_ref[d]


def fold_rows(values, row):
    for step in (1, 2, 4):
        low = (row & step) == 0
        values = [
            jnp.where(low, values[i], values[i + 1])
            + pltpu.roll(jnp.where(low, values[i + 1], values[i]), step, 0)
            for i in range(0, len(values), 2)
        ]
    return values[0]


def update_tiles(tables, m, spans, an, ng, row8):
    count = tables.shape[2]
    values = []
    for span in spans:
        plus = tables[m, 0, :, span]
        minus = tables[m, 1, :, span]
        four = [
            plus * ng[0] + minus * an[3],
            plus * ng[1] + minus * ng[2],
            plus * ng[2] + minus * ng[1],
            plus * ng[3] + minus * an[0],
        ]
        values += [sum(v[8 * k : 8 * k + 8] for k in range(count // 8)) for v in four]
    return fold_rows(values, row8)


def analysed_kernel(groups, cycles, tables, gram_ref, pieces_ref, phases_ref, *rest):
    messages = rest[: groups - 1]
    *sends, analysed_ref, sky = rest[groups - 1 :]
    slots, _, count, degrees = tables.shape
    middle, _, width = sends[0].shape
    blocks = degrees // width
    far = blocks // 2
    place = ring_place(lax.axis_index("blk"), blocks)
    firsts = [
        pl.multiple_of(block_at(place + step, blocks) * width, LANES)
        for step in (far, -far, 1 - far, far - 1)
    ]
    owner = lax.axis_index("order")
    wide = 4 * slots
    pairs = []
    for d in range(groups):
        phases = phases_ref[...] if d == 0 else messages[d - 1][:count]
        piece = pieces_ref[0] if d == 0 else messages[d - 1][count:]
        sky[pl.ds((owner ^ d) * cycles, cycles)] = piece[:cycles]
        pairs.append(phases)
    lane = lax.broadcasted_iota(jnp.int32, (count, LANES), 1)
    row8 = lax.broadcasted_iota(jnp.int32, (8, LANES), 0)
    per = LANES // wide
    packed = []
    for start in range(0, groups, per):
        value = pairs[start]
        for k in range(1, per):
            value = jnp.where(
                lane // wide == k, pltpu.roll(pairs[start + k], k * wide, 1), value
            )
        packed.append(value)
    observed = sky[...]
    for m in range(slots):
        total = jnp.where((lane < wide) & (lane % slots == m), observed, 0.0)
        for k, value in enumerate(packed):
            total = total - gram_ref[m, :, k * LANES : (k + 1) * LANES] * value
        an = []
        for a in range(4):
            value = jnp.where((lane % wide) // slots == a, total, 0.0)
            value = jnp.sum(value, axis=1, keepdims=True)
            an.append(jnp.broadcast_to(value, (count, LANES)))
            analysed_ref[m, a] = an[a]
        ng = [-value for value in an]
        half, at = divmod(m, middle)
        for part, first in zip(sends[half::2], firsts[half::2]):
            for t in range(0, width // LANES, 2):
                spans = [pl.ds(first + u * LANES, LANES) for u in (t, t + 1)]
                folded = update_tiles(tables, m, spans, an, ng, row8)
                for k, u in enumerate((t, t + 1)):
                    part[at, :, u * LANES : (u + 1) * LANES] = folded[4 * k : 4 * k + 4]


def backward_kernel(core, tables, analysed_ref, *rest):
    pl.when(on_core(core))(lambda: backward_blocks(tables, analysed_ref, rest[-1]))


def backward_blocks(tables, analysed_ref, out):
    slots, _, _, degrees = tables.shape
    blocks, _, _, width = out.shape
    stratum = degrees // slots
    place = ring_place(lax.axis_index("blk"), blocks)
    ring = ring_of(blocks)
    step_of = [lax.rem(ring.index(b) - place + blocks, blocks) for b in range(blocks)]
    row8 = lax.broadcasted_iota(jnp.int32, (8, LANES), 0)
    for m in range(slots):
        an = [analysed_ref[m, a] for a in range(4)]
        ng = [-value for value in an]
        for t in range(stratum * m // LANES, degrees // LANES, 2):
            spans = [slice(u * LANES, (u + 1) * LANES) for u in (t, t + 1)]
            folded = update_tiles(tables, m, spans, an, ng, row8)
            for k, u in enumerate((t, t + 1)):
                inner = u * LANES % width
                out[step_of[u * LANES // width], m, :, inner : inner + LANES] = folded[
                    4 * k : 4 * k + 4
                ]


def residual_kernel(groups, slots, cycles, *rest):
    metas = [ref[...] for ref in rest[:groups]]
    section_ref, acs_ref, asc_ref, fine_ref, phases_ref = rest[groups : groups + 5]
    messages = rest[groups + 5 : 2 * groups + 4]
    out_ref, spread = rest[2 * groups + 4 :]
    owner = lax.axis_index("order")
    rows, both = acs_ref.shape[1:]
    every = both // 2
    count = phases_ref.shape[0]
    lane = lax.broadcasted_iota(jnp.int32, (count, LANES), 1)
    ids = spread_ids(metas, slots, [d for _ in range(2) for d in range(groups)])
    factor = jnp.where(ids == 0.0, 1.0, 2.0)
    per = LANES // slots
    values = [phases_ref[...]] + [ref[:count] for ref in messages]
    for a in range(4):
        tiles = []
        for start in range(0, 2 * groups, per):
            tile = jnp.zeros((count, LANES), jnp.float32)
            for k in range(per):
                shift = (k - a) * slots % LANES
                value = values[(start + k) % groups]
                value = pltpu.roll(value, shift, 1) if shift else value
                tile = jnp.where(lane // slots == k, value, tile)
            tiles.append(tile)
        spread[a] = jnp.concatenate(tiles, axis=1) * factor
    even = lax.broadcasted_iota(jnp.int32, (rows, both), 0) % 2 == 0
    for c in range(cycles):
        q_re, q_im, u_re, u_im = [spread[a, pl.ds(owner * cycles + c, 1)] for a in range(4)]
        weights = jnp.where(even, q_re, u_re) * acs_ref[c]
        weights = weights - jnp.where(even, q_im, u_im) * asc_ref[c]
        model = lax.dot_general(
            weights, fine_ref[c], (((1,), (1,)), ((), ())), precision=HIGHEST,
            preferred_element_type=jnp.float32,
        )
        inside = pixel_mask((rows, LANES), entry(metas[0], slots + c).astype(jnp.int32))
        out_ref[c] = section_ref[c] - jnp.where(inside, model, 0.0)


def add_kernel(index, first, piece_ref, value_ref, out_ref):
    out_ref[...] = piece_ref[index, first : first + out_ref.shape[0]] + value_ref[...]


def final_kernel(meta_ref, harmonics_ref, piece_ref, *rest):
    *received, out_ref = rest
    slots, parts, width = out_ref.shape
    middle = slots // 2
    start = lax.axis_index("blk") * width
    degree = start + lax.broadcasted_iota(jnp.int32, (parts, width), 1)
    meta = meta_ref[...]
    for m in range(slots):
        h, at = divmod(m, middle)
        update = piece_ref[0, m] + (received[h][at] + received[2 + h][at])
        valid = degree >= jnp.maximum(entry(meta, m).astype(jnp.int32), 2)
        out_ref[m] = jnp.where(valid, harmonics_ref[m] + update, 0.0)


def vmem():
    return pl.BlockSpec(memory_space=VMEM)


def shape(*dims):
    return jax.ShapeDtypeStruct(dims, jnp.float32)


def body(harmonics, legendre, sky_map, cycle_length, cycle_offset, cycle_weight, order_ids):
    groups = lax.axis_size("order")
    blocks = lax.axis_size("blk")
    slots, _, width = harmonics.shape
    count, degrees = legendre.shape[2:]
    cycles, _, pixels = sky_map.shape
    rows = pixels // LANES
    every = slots * groups
    normalise = math.sqrt(degrees * every / (cycles * groups * blocks * pixels))

    def swap(value, axis, step):
        size = lax.axis_size(axis)
        return lax.ppermute(value, axis, [(i, i ^ step) for i in range(size)])

    ring = ring_of(blocks)

    def turn(value, way):
        pairs = [(ring[p], ring[(p + way) % blocks]) for p in range(blocks)]
        return lax.ppermute(value, "blk", pairs)

    def estimate(micros):
        return pl.CostEstimate(flops=0, bytes_accessed=int(micros * 3.0e6), transcendentals=0)

    hbm = pl.BlockSpec(memory_space=pl.ANY)
    small = (order_ids, cycle_length, cycle_offset, cycle_weight)
    meta = pl.pallas_call(
        lambda *refs: meta_kernel(slots, cycles, *refs),
        out_shape=pltpu.VMEM((1, LANES), jnp.float32),
        in_specs=[hbm] * 4,
        out_specs=vmem(),
        scratch_shapes=[pltpu.SMEM(v.shape, v.dtype) for v in small]
        + [pltpu.SemaphoreType.DMA((len(small),))],
        compiler_params=pltpu.CompilerParams(vmem_limit_bytes=2 * MIB),
        name="meta",
    )(*[pltpu.with_memory_space_constraint(v, pltpu.HBM) for v in small])
    metas = [meta] + [swap(meta, "order", d) for d in range(1, groups)]

    far = blocks // 2
    middle = slots // 2
    ahead, behind = turn(harmonics, 1), turn(harmonics, -1)
    parts, steps, firsts = [harmonics, ahead, behind], [0, -1, 1], [0, 0, 0]
    tables = pl.pallas_call(
        tables_kernel,
        out_shape=pltpu.VMEM(legendre.shape, jnp.float32),
        in_specs=[hbm],
        out_specs=hbm,
        scratch_shapes=[pltpu.SemaphoreType.DMA((slots,))],
        compiler_params=pltpu.CompilerParams(vmem_limit_bytes=2 * MIB),
        cost_estimate=estimate(1.5),
        name="tables",
    )(pltpu.with_memory_space_constraint(legendre, pltpu.HBM))
    ahead, tables, *metas = lax.optimization_barrier((ahead, tables, *metas))
    ahead = [ahead[:middle], ahead[middle:]]
    behind = [behind[:middle], behind[middle:]]

    sky = sky_map.reshape(cycles, 2, rows, LANES).transpose(0, 2, 1, 3)
    sky = sky.reshape(cycles, 2 * rows, LANES)
    pieces, acs, asc, fine, section = pl.pallas_call(
        lambda *refs: sky_kernel(normalise, groups, slots, cycles, *refs),
        out_shape=(
            shape(groups, 8, LANES),
            shape(cycles, 2 * rows, 2 * every),
            shape(cycles, 2 * rows, 2 * every),
            shape(cycles, LANES, 2 * every),
            shape(cycles, 2 * rows, LANES),
        ),
        in_specs=[vmem()] * groups + [hbm],
        out_specs=(vmem(),) * 5,
        scratch_shapes=[
            pltpu.VMEM((cycles, 2 * rows, LANES), jnp.float32),
            pltpu.SemaphoreType.DMA,
        ],
        compiler_params=pltpu.CompilerParams(vmem_limit_bytes=16 * MIB),
        cost_estimate=estimate(3),
        name="sky_analysis",
    )(*metas, pltpu.with_memory_space_constraint(sky, pltpu.HBM))
    gram = pl.pallas_call(
        lambda *refs: gram_kernel(normalise, groups, slots, cycles, *refs),
        out_shape=shape(slots, count, 4 * every),
        in_specs=[vmem()] * groups,
        out_specs=vmem(),
        compiler_params=pltpu.CompilerParams(vmem_limit_bytes=8 * MIB),
        cost_estimate=estimate(1),
        name="response",
    )(*metas)

    for k in range(2, far):
        ahead = [turn(value, 1) for value in ahead]
        behind = [turn(value, -1) for value in behind[::-1]][::-1]
        parts += ahead + behind
        steps += [-k, -k, k, k]
        firsts += [0, middle] * 2
        if k == 2:
            ahead[0], pieces = lax.optimization_barrier((ahead[0], pieces))
    ends = [turn(ahead[0], 1), turn(behind[1], -1)]

    whole = pltpu.VMEM((slots, 4, count, LANES), jnp.float32)
    sums = pl.pallas_call(
        lambda *refs: forward_kernel(steps, firsts, *refs),
        out_shape=whole,
        in_specs=[vmem()] * (2 + len(parts)),
        out_specs=vmem(),
        scratch_shapes=[pltpu.VMEM((slots, 4, degrees), jnp.float32)],
        compiler_params=pltpu.CompilerParams(vmem_limit_bytes=24 * MIB),
        cost_estimate=estimate(2),
        name="forward",
    )(meta, tables, *parts)
    phases, *outs = pl.pallas_call(
        lambda *refs: phases_kernel(groups, *refs),
        out_shape=[shape(count, LANES)] + [shape(count + 8, LANES)] * (groups - 1),
        in_specs=[vmem()] * 6,
        out_specs=[vmem()] * groups,
        compiler_params=pltpu.CompilerParams(vmem_limit_bytes=16 * MIB),
        cost_estimate=estimate(1),
        name="phases",
    )(meta, tables, pieces, sums, *ends)
    messages = [swap(outs[d - 1], "order", d) for d in range(1, groups)]

    half = pltpu.VMEM((middle, 4, width), jnp.float32)
    *sends, analysed = pl.pallas_call(
        lambda *refs: analysed_kernel(groups, cycles, *refs),
        out_shape=[half] * 4 + [whole],
        in_specs=[vmem()] * (3 + groups),
        out_specs=[vmem()] * 5,
        scratch_shapes=[pltpu.VMEM((count, LANES), jnp.float32)],
        compiler_params=pltpu.CompilerParams(vmem_limit_bytes=16 * MIB),
        cost_estimate=estimate(1),
        name="analysed",
    )(tables, gram, pieces, phases, *messages)
    def backward(core, *before):
        return pl.pallas_call(
            lambda *refs: backward_kernel(core, *refs),
            out_shape=pltpu.VMEM((blocks, slots, 4, width), jnp.float32),
            in_specs=[vmem()] * 2 + [hbm] * len(before),
            out_specs=vmem(),
            input_output_aliases={2: 0} if before else {},
            compiler_params=pltpu.CompilerParams(vmem_limit_bytes=16 * MIB),
            cost_estimate=estimate(2),
            name="backward",
        )(
            tables, analysed,
            *[pltpu.with_memory_space_constraint(value, pltpu.VMEM) for value in before],
        )

    piece = backward(1)
    *sends, piece = lax.optimization_barrier((*sends, piece))
    piece = backward(0, piece)

    def add(index, first, value):
        return pl.pallas_call(
            lambda *refs: add_kernel(index, first, *refs),
            out_shape=half,
            in_specs=[vmem()] * 2,
            out_specs=vmem(),
            compiler_params=pltpu.CompilerParams(vmem_limit_bytes=4 * MIB),
            cost_estimate=estimate(0.1),
            name="add",
        )(piece, pltpu.with_memory_space_constraint(value, pltpu.VMEM))

    sent = dict(zip(((1, 0), (-1, middle), (-1, 0), (1, middle)), sends))
    first_hop = {key: turn(sent[key], key[0]) for key in ((1, 0), (-1, middle))}
    for key in ((1, 0), (-1, middle)):
        sent[key] = add((key[0] * (far - 1)) % blocks, key[1], first_hop[key])
    for k in reversed(range(1, far)):
        for key in ((1, middle), (-1, 0), (1, 0), (-1, middle)):
            sent[key] = turn(sent[key], key[0])
            if k > 1:
                sent[key] = add((key[0] * (k - 1)) % blocks, key[1], sent[key])
    received = [sent[key] for key in ((1, 0), (1, middle), (-1, 0), (-1, middle))]
    refined = pl.pallas_call(
        final_kernel,
        out_shape=shape(*harmonics.shape),
        in_specs=[vmem()] * 7,
        out_specs=vmem(),
        compiler_params=pltpu.CompilerParams(vmem_limit_bytes=8 * MIB),
        cost_estimate=pl.CostEstimate(flops=10**5, bytes_accessed=10**6, transcendentals=0),
        name="refine",
    )(
        meta, harmonics, piece,
        *[pltpu.with_memory_space_constraint(value, pltpu.VMEM) for value in received],
    )

    residual = pl.pallas_call(
        lambda *refs: residual_kernel(groups, slots, cycles, *refs),
        out_shape=shape(cycles, 2 * rows, LANES),
        in_specs=[vmem()] * (4 + 2 * groups),
        out_specs=vmem(),
        scratch_shapes=[pltpu.VMEM((4, count, 2 * every), jnp.float32)],
        compiler_params=pltpu.CompilerParams(vmem_limit_bytes=16 * MIB),
        cost_estimate=pl.CostEstimate(flops=10**8, bytes_accessed=2 * MIB, transcendentals=0),
        name="residual",
    )(*metas, section, acs, asc, fine, phases, *messages)
    residual = residual.reshape(cycles, rows, 2, LANES).transpose(0, 2, 1, 3)
    return (refined, residual.reshape(sky_map.shape))


def solution(mesh):
    return jax.shard_map(
        body,
        mesh=mesh,
        in_specs=(
            P("order", None, "blk"),
            P("order", None, "blk", None),
            P(("blk", "order"), None, None),
            P(("blk", "order")),
            P(("blk", "order")),
            P(("blk", "order")),
            P("order"),
        ),
        out_specs=(P("order", None, "blk"), P(("blk", "order"), None, None)),
        check_vma=False,
    )
```

```python
import math

import jax
import jax.numpy as jnp
from jax import lax
from jax.experimental import pallas as pl
from jax.experimental.pallas import tpu as pltpu
from jax.sharding import PartitionSpec as P

HIGHEST = lax.Precision.HIGHEST
LANES = 128
VMEM = pltpu.VMEM
MIB = 1024 * 1024


def ring_of(blocks):
    return list(range(0, blocks, 2)) + list(range(blocks - 1, 0, -2))


def ring_place(block, blocks):
    return jnp.where(block % 2 == 0, block // 2, blocks - 1 - block // 2)


def block_at(place, blocks):
    place = lax.rem(place + 2 * blocks, blocks)
    return jnp.where(place < blocks // 2, 2 * place, 2 * (blocks - 1 - place) + 1)


def sin_pi(x):
    turns = jnp.round(x)
    y = (x - turns) * math.pi
    z = y * y
    value = -1.0 / 39916800
    for term in (1.0 / 362880, -1.0 / 5040, 1.0 / 120, -1.0 / 6, 1.0):
        value = value * z + term
    value = value * y
    return jnp.where(turns.astype(jnp.int32) % 2 != 0, -value, value)


def half_turns(order, step, length):
    total = order * step
    period = 2 * length
    scale = 0.5 / length.astype(jnp.float32)
    for _ in range(2):
        total = total - jnp.floor(total.astype(jnp.float32) * scale).astype(jnp.int32) * period
    return total.astype(jnp.float32) / length.astype(jnp.float32)


def pixel_mask(shape, length):
    pixel = lax.broadcasted_iota(jnp.int32, shape, 0) // 2 * shape[1]
    pixel = pixel + lax.broadcasted_iota(jnp.int32, shape, 1)
    return pixel < length


def meta_kernel(slots, cycles, ids, length, offset, weight, out_ref, *scratch):
    *held, sems = scratch
    copies = [
        pltpu.make_async_copy(source, target, sems.at[k])
        for k, (source, target) in enumerate(zip((ids, length, offset, weight), held))
    ]
    for copy in copies:
        copy.start()
    for copy in copies:
        copy.wait()
    lane = lax.broadcasted_iota(jnp.int32, (1, LANES), 1)
    out = jnp.zeros((1, LANES), jnp.float32)
    for m in range(slots):
        out = jnp.where(lane == m, held[0][m].astype(jnp.float32), out)
    for c in range(cycles):
        for k in range(3):
            value = held[1 + k][c].astype(jnp.float32)
            out = jnp.where(lane == slots + k * cycles + c, value, out)
    out_ref[...] = out


def entry(meta, at):
    return meta[:, at : at + 1]


def spread_ids(metas, slots, sources):
    per = LANES // slots
    lane = lax.broadcasted_iota(jnp.int32, (1, LANES), 1)
    pieces = []
    for start in range(0, len(sources), per):
        piece = jnp.zeros((1, LANES), jnp.float32)
        for k in range(per):
            value = metas[sources[start + k]]
            value = pltpu.roll(value, k * slots, 1) if k else value
            piece = jnp.where(lane // slots == k, value, piece)
        pieces.append(piece)
    return jnp.concatenate(pieces, axis=1)


def sky_kernel(normalise, groups, slots, cycles, *rest):
    metas = [ref[...] for ref in rest[:groups]]
    sky_hbm, pieces_ref, acs_ref, asc_ref, fine_ref, section_ref, sky_ref, sky_sem = rest[groups:]
    sky_copy = pltpu.make_async_copy(sky_hbm, sky_ref, sky_sem)
    sky_copy.start()
    rows, both = acs_ref.shape[1:]
    every = both // 2
    ids = spread_ids(metas, slots, [d for _ in range(2) for d in range(groups)])
    ids = ids.astype(jnp.int32)
    row8 = lax.broadcasted_iota(jnp.int32, (8, both), 0)
    sums = [jnp.zeros((8, both), jnp.float32) for _ in range(4)]
    for c in range(cycles):
        length = entry(metas[0], slots + c).astype(jnp.int32)
        offset = entry(metas[0], slots + cycles + c).astype(jnp.int32)
        coarse = lax.broadcasted_iota(jnp.int32, (rows, both), 0) // 2 * (2 * LANES) + offset
        x = half_turns(ids, coarse, length)
        first = lax.broadcasted_iota(jnp.int32, (rows, both), 1) < every
        acs = sin_pi(x + jnp.where(first, 0.5, 1.0))
        asc = sin_pi(x + jnp.where(first, 0.0, 0.5))
        acs_ref[c] = acs
        asc_ref[c] = asc
        fine = 2 * lax.broadcasted_iota(jnp.int32, (LANES, both), 0)
        x = half_turns(ids, fine, length)
        first = lax.broadcasted_iota(jnp.int32, (LANES, both), 1) < every
        table = sin_pi(x + jnp.where(first, 0.5, 0.0))
        fine_ref[c] = table
        if c == 0:
            sky_copy.wait()
        section = jnp.where(pixel_mask((rows, LANES), length), sky_ref[c], 0.0)
        section_ref[c] = section
        spun = jnp.dot(section, table, precision=HIGHEST, preferred_element_type=jnp.float32)
        weight = entry(metas[0], slots + 2 * cycles + c) * normalise
        for k, value in enumerate((spun * acs, spun * asc)):
            value = sum(value[8 * i : 8 * i + 8] for i in range(rows // 8))
            for q in range(2):
                total = jnp.sum(jnp.where(row8 % 2 == q, value, 0.0), axis=0, keepdims=True)
                total = total * (-weight if k else weight)
                sums[2 * q + k] = jnp.where(row8 == c, total, sums[2 * q + k])
    lane = lax.broadcasted_iota(jnp.int32, (8, LANES), 1)
    totals = []
    for value in sums:
        tiles = [value[:, i : i + LANES] for i in range(0, both, LANES)]
        if every < LANES:
            shift = every
            while shift < LANES:
                tiles[0] = tiles[0] + pltpu.roll(tiles[0], shift, 1)
                shift *= 2
            totals.append(tiles)
        else:
            half = len(tiles) // 2
            totals.append([tiles[i] + tiles[half + i] for i in range(half)])
    for d in range(groups):
        piece = jnp.zeros((8, LANES), jnp.float32)
        tile, at = divmod(d * slots, LANES)
        for a in range(4):
            shift = (a * slots - at) % LANES
            value = totals[a][tile]
            value = pltpu.roll(value, shift, 1) if shift else value
            piece = jnp.where(lane // slots == a, value, piece)
        pieces_ref[d] = piece


def gram_kernel(normalise, groups, slots, cycles, *rest):
    metas = [ref[...] for ref in rest[:groups]]
    (gram_ref,) = rest[groups:]
    me = lax.axis_index("order")
    count, wide = gram_ref.shape[1:]
    row = lax.broadcasted_iota(jnp.int32, (count, wide), 0)
    length = jnp.ones((count, wide), jnp.float32)
    offset = jnp.zeros((count, wide), jnp.float32)
    weight = jnp.zeros((count, wide), jnp.float32)
    for d in range(groups):
        for c in range(cycles):
            here = row == (me ^ d) * cycles + c
            length = jnp.where(here, entry(metas[d], slots + c), length)
            offset = jnp.where(here, entry(metas[d], slots + cycles + c), offset)
            weight = jnp.where(here, entry(metas[d], slots + 2 * cycles + c), weight)
    others = spread_ids(metas, slots, [d for d in range(groups) for _ in range(4)])
    lane = lax.broadcasted_iota(jnp.int32, (count, wide), 1)
    cosine = (lane // slots) % 2 == 0
    factor = jnp.where(others == 0.0, 0.5, 1.0) * normalise * weight * length
    inverse = 1.0 / length
    odd = offset > 0.5

    def response(n):
        turns = jnp.round(n * inverse)
        sign = jnp.where(odd & (turns.astype(jnp.int32) % 2 != 0), -1.0, 1.0)
        return jnp.where(turns * length == n, sign, 0.0)

    for m in range(slots):
        mine = entry(metas[0], m)
        near = response(mine - others)
        far = response(mine + others)
        gram_ref[m] = factor * (near + jnp.where(cosine, far, -far))


def table_copies(legendre, tables, sems):
    slots, _, _, degrees = tables.shape
    copies = []
    for m in range(slots):
        first = m * (degrees // slots)
        part = (m, slice(None), slice(None), pl.ds(first, degrees - first))
        copies.append(pltpu.make_async_copy(legendre.at[part], tables.at[part], sems.at[m]))
    return copies


def use_tile(tables, m, span, keep, coefs, p, n):
    plus = tables[m, 0, :, span]
    minus = tables[m, 1, :, span]
    if keep is not None:
        plus = jnp.where(keep, plus, 0.0)
        minus = jnp.where(keep, minus, 0.0)
    for a in range(4):
        c = coefs(a)
        if keep is not None:
            c = jnp.where(keep[:1], c, 0.0)
        p[a] = p[a] + plus * c
        n[a] = n[a] + minus * c


def fold_lanes(values, lane):
    step = 1
    while step < LANES:
        if len(values) > 1:
            low = (lane & step) == 0
            values = [
                jnp.where(low, values[i], values[i + 1])
                + pltpu.roll(jnp.where(low, values[i + 1], values[i]), step, 1)
                for i in range(0, len(values), 2)
            ]
        else:
            values = [values[0] + pltpu.roll(values[0], step, 1)]
        step *= 2
    return values[0]


def combine(p, n):
    return [n[3] - p[0], -p[1] - n[2], -p[2] - n[1], n[0] - p[3]]


def on_core(core):
    return lax.axis_index("order") % 2 == core


def tables_kernel(legendre, tables, sems):
    copies = table_copies(legendre, tables, sems)
    for copy in copies:
        copy.start()
    for copy in copies:
        copy.wait()


def forward_kernel(steps, firsts, meta_ref, tables, *rest):
    parts = rest[: len(steps)]
    sums_ref, coefs = rest[len(steps) :]
    slots, _, count, degrees = tables.shape
    width = parts[0].shape[2]
    blocks = degrees // width
    stratum = degrees // slots
    meta = meta_ref[...]
    place = ring_place(lax.axis_index("blk"), blocks)
    for part, step, low in zip(parts, steps, firsts):
        first = pl.multiple_of(block_at(place + step, blocks) * width, LANES)
        for m in range(part.shape[0]):
            coefs[low + m, :, pl.ds(first, width)] = part[m]
    first = pl.multiple_of(block_at(place + blocks // 2, blocks) * width, LANES)
    for m in range(slots):
        coefs[m, :, pl.ds(first, width)] = jnp.zeros((4, width), jnp.float32)
    lane = lax.broadcasted_iota(jnp.int32, (count, LANES), 1)
    for m in range(slots):
        floor = jnp.maximum(entry(meta, m).astype(jnp.int32), 2)
        p = [jnp.zeros((count, LANES), jnp.float32)] * 4
        n = [jnp.zeros((count, LANES), jnp.float32)] * 4
        for t in range(stratum * m // LANES, degrees // LANES):
            span = slice(t * LANES, (t + 1) * LANES)
            keep = lane >= floor - t * LANES if t * LANES < stratum * (m + 1) else None
            use_tile(tables, m, span, keep, lambda a: coefs[m, a : a + 1, span], p, n)
        for a, total in enumerate(combine(p, n)):
            sums_ref[m, a] = total


def phases_kernel(groups, meta_ref, tables, pieces_ref, sums_ref, low_ref, high_ref, *rest):
    phases_ref, *messages = rest
    slots, _, count, degrees = tables.shape
    middle, _, width = low_ref.shape
    blocks = degrees // width
    meta = meta_ref[...]
    place = ring_place(lax.axis_index("blk"), blocks)
    first = pl.multiple_of(block_at(place + blocks // 2, blocks) * width, LANES)
    lane = lax.broadcasted_iota(jnp.int32, (count, LANES), 1)
    totals = [None] * (4 * slots)
    for m in range(slots):
        floor = jnp.maximum(entry(meta, m).astype(jnp.int32), 2) - first
        part, at = (low_ref, m) if m < middle else (high_ref, m - middle)
        p = [jnp.zeros((count, LANES), jnp.float32)] * 4
        n = [jnp.zeros((count, LANES), jnp.float32)] * 4
        for t in range(width // LANES):
            here = slice(t * LANES, (t + 1) * LANES)
            keep = lane >= floor - t * LANES
            span = pl.ds(first + t * LANES, LANES)
            use_tile(tables, m, span, keep, lambda a: part[at, a : a + 1, here], p, n)
        for a, total in enumerate(combine(p, n)):
            totals[a * slots + m] = total + sums_ref[m, a]
    phases = fold_lanes(totals, lane)
    phases_ref[...] = phases
    for d in range(1, groups):
        messages[d - 1][:count] = phases
        messages[d - 1][count:] = pieces_ref[d]


def fold_rows(values, row):
    for step in (1, 2, 4):
        low = (row & step) == 0
        values = [
            jnp.where(low, values[i], values[i + 1])
            + pltpu.roll(jnp.where(low, values[i + 1], values[i]), step, 0)
            for i in range(0, len(values), 2)
        ]
    return values[0]


def update_tiles(tables, m, spans, an, ng, row8):
    count = tables.shape[2]
    values = []
    for span in spans:
        plus = tables[m, 0, :, span]
        minus = tables[m, 1, :, span]
        four = [
            plus * ng[0] + minus * an[3],
            plus * ng[1] + minus * ng[2],
            plus * ng[2] + minus * ng[1],
            plus * ng[3] + minus * an[0],
        ]
        values += [sum(v[8 * k : 8 * k + 8] for k in range(count // 8)) for v in four]
    return fold_rows(values, row8)


def update_block(tables, m, first, an, ng, row8, out, at):
    for t in range(0, out.shape[2] // LANES, 2):
        spans = [pl.ds(first + u * LANES, LANES) for u in (t, t + 1)]
        folded = update_tiles(tables, m, spans, an, ng, row8)
        for k, u in enumerate((t, t + 1)):
            out[at, :, u * LANES : (u + 1) * LANES] = folded[4 * k : 4 * k + 4]


def analysed_kernel(groups, cycles, tables, gram_ref, pieces_ref, phases_ref, *rest):
    messages = rest[: groups - 1]
    *sends, analysed_ref, sky = rest[groups - 1 :]
    slots, _, count, degrees = tables.shape
    middle, _, width = sends[0].shape
    blocks = degrees // width
    far = blocks // 2
    place = ring_place(lax.axis_index("blk"), blocks)
    first = pl.multiple_of(block_at(place + far, blocks) * width, LANES)
    owner = lax.axis_index("order")
    wide = 4 * slots
    pairs = []
    for d in range(groups):
        phases = phases_ref[...] if d == 0 else messages[d - 1][:count]
        piece = pieces_ref[0] if d == 0 else messages[d - 1][count:]
        sky[pl.ds((owner ^ d) * cycles, cycles)] = piece[:cycles]
        pairs.append(phases)
    lane = lax.broadcasted_iota(jnp.int32, (count, LANES), 1)
    row8 = lax.broadcasted_iota(jnp.int32, (8, LANES), 0)
    per = LANES // wide
    packed = []
    for start in range(0, groups, per):
        value = pairs[start]
        for k in range(1, per):
            value = jnp.where(
                lane // wide == k, pltpu.roll(pairs[start + k], k * wide, 1), value
            )
        packed.append(value)
    observed = sky[...]
    for m in range(slots):
        total = jnp.where((lane < wide) & (lane % slots == m), observed, 0.0)
        for k, value in enumerate(packed):
            total = total - gram_ref[m, :, k * LANES : (k + 1) * LANES] * value
        an = []
        for a in range(4):
            value = jnp.where((lane % wide) // slots == a, total, 0.0)
            value = jnp.sum(value, axis=1, keepdims=True)
            an.append(jnp.broadcast_to(value, (count, LANES)))
            analysed_ref[m, a] = an[a]
        ng = [-value for value in an]
        half, at = divmod(m, middle)
        update_block(tables, m, first, an, ng, row8, sends[half], at)


def second_kernel(tables, analysed_ref, low_ref, high_ref):
    slots, _, _, degrees = tables.shape
    middle, _, width = low_ref.shape
    blocks = degrees // width
    place = ring_place(lax.axis_index("blk"), blocks)
    row8 = lax.broadcasted_iota(jnp.int32, (8, LANES), 0)
    for m in range(slots):
        half, at = divmod(m, middle)
        step = (1 - blocks // 2, blocks // 2 - 1)[half]
        first = pl.multiple_of(block_at(place + step, blocks) * width, LANES)
        an = [analysed_ref[m, a] for a in range(4)]
        ng = [-value for value in an]
        update_block(tables, m, first, an, ng, row8, (low_ref, high_ref)[half], at)


def backward_kernel(core, tables, analysed_ref, *rest):
    pl.when(on_core(core))(lambda: backward_blocks(tables, analysed_ref, rest[-1]))


def backward_blocks(tables, analysed_ref, out):
    slots, _, _, degrees = tables.shape
    blocks, _, _, width = out.shape
    stratum = degrees // slots
    place = ring_place(lax.axis_index("blk"), blocks)
    ring = ring_of(blocks)
    step_of = [lax.rem(ring.index(b) - place + blocks, blocks) for b in range(blocks)]
    row8 = lax.broadcasted_iota(jnp.int32, (8, LANES), 0)
    for m in range(slots):
        an = [analysed_ref[m, a] for a in range(4)]
        ng = [-value for value in an]
        for t in range(stratum * m // LANES, degrees // LANES, 2):
            spans = [slice(u * LANES, (u + 1) * LANES) for u in (t, t + 1)]
            folded = update_tiles(tables, m, spans, an, ng, row8)
            for k, u in enumerate((t, t + 1)):
                inner = u * LANES % width
                out[step_of[u * LANES // width], m, :, inner : inner + LANES] = folded[
                    4 * k : 4 * k + 4
                ]


def residual_kernel(groups, slots, cycles, *rest):
    metas = [ref[...] for ref in rest[:groups]]
    section_ref, acs_ref, asc_ref, fine_ref, phases_ref = rest[groups : groups + 5]
    messages = rest[groups + 5 : 2 * groups + 4]
    out_ref, spread = rest[2 * groups + 4 :]
    owner = lax.axis_index("order")
    rows, both = acs_ref.shape[1:]
    every = both // 2
    count = phases_ref.shape[0]
    lane = lax.broadcasted_iota(jnp.int32, (count, LANES), 1)
    ids = spread_ids(metas, slots, [d for _ in range(2) for d in range(groups)])
    factor = jnp.where(ids == 0.0, 1.0, 2.0)
    per = LANES // slots
    values = [phases_ref[...]] + [ref[:count] for ref in messages]
    for a in range(4):
        tiles = []
        for start in range(0, 2 * groups, per):
            tile = jnp.zeros((count, LANES), jnp.float32)
            for k in range(per):
                shift = (k - a) * slots % LANES
                value = values[(start + k) % groups]
                value = pltpu.roll(value, shift, 1) if shift else value
                tile = jnp.where(lane // slots == k, value, tile)
            tiles.append(tile)
        spread[a] = jnp.concatenate(tiles, axis=1) * factor
    even = lax.broadcasted_iota(jnp.int32, (rows, both), 0) % 2 == 0
    for c in range(cycles):
        q_re, q_im, u_re, u_im = [spread[a, pl.ds(owner * cycles + c, 1)] for a in range(4)]
        weights = jnp.where(even, q_re, u_re) * acs_ref[c]
        weights = weights - jnp.where(even, q_im, u_im) * asc_ref[c]
        model = lax.dot_general(
            weights, fine_ref[c], (((1,), (1,)), ((), ())), precision=HIGHEST,
            preferred_element_type=jnp.float32,
        )
        inside = pixel_mask((rows, LANES), entry(metas[0], slots + c).astype(jnp.int32))
        out_ref[c] = section_ref[c] - jnp.where(inside, model, 0.0)


def add_kernel(index, first, piece_ref, value_ref, out_ref):
    out_ref[...] = piece_ref[index, first : first + out_ref.shape[0]] + value_ref[...]


def final_kernel(meta_ref, harmonics_ref, piece_ref, *rest):
    *received, out_ref = rest
    slots, parts, width = out_ref.shape
    middle = slots // 2
    start = lax.axis_index("blk") * width
    degree = start + lax.broadcasted_iota(jnp.int32, (parts, width), 1)
    meta = meta_ref[...]
    for m in range(slots):
        h, at = divmod(m, middle)
        update = piece_ref[0, m] + (received[h][at] + received[2 + h][at])
        valid = degree >= jnp.maximum(entry(meta, m).astype(jnp.int32), 2)
        out_ref[m] = jnp.where(valid, harmonics_ref[m] + update, 0.0)


def vmem():
    return pl.BlockSpec(memory_space=VMEM)


def shape(*dims):
    return jax.ShapeDtypeStruct(dims, jnp.float32)


def body(harmonics, legendre, sky_map, cycle_length, cycle_offset, cycle_weight, order_ids):
    groups = lax.axis_size("order")
    blocks = lax.axis_size("blk")
    slots, _, width = harmonics.shape
    count, degrees = legendre.shape[2:]
    cycles, _, pixels = sky_map.shape
    rows = pixels // LANES
    every = slots * groups
    normalise = math.sqrt(degrees * every / (cycles * groups * blocks * pixels))

    def swap(value, axis, step):
        size = lax.axis_size(axis)
        return lax.ppermute(value, axis, [(i, i ^ step) for i in range(size)])

    ring = ring_of(blocks)

    def turn(value, way):
        pairs = [(ring[p], ring[(p + way) % blocks]) for p in range(blocks)]
        return lax.ppermute(value, "blk", pairs)

    def estimate(micros):
        return pl.CostEstimate(flops=0, bytes_accessed=int(micros * 3.0e6), transcendentals=0)

    hbm = pl.BlockSpec(memory_space=pl.ANY)
    small = (order_ids, cycle_length, cycle_offset, cycle_weight)
    meta = pl.pallas_call(
        lambda *refs: meta_kernel(slots, cycles, *refs),
        out_shape=pltpu.VMEM((1, LANES), jnp.float32),
        in_specs=[hbm] * 4,
        out_specs=vmem(),
        scratch_shapes=[pltpu.SMEM(v.shape, v.dtype) for v in small]
        + [pltpu.SemaphoreType.DMA((len(small),))],
        compiler_params=pltpu.CompilerParams(vmem_limit_bytes=2 * MIB),
        name="meta",
    )(*[pltpu.with_memory_space_constraint(v, pltpu.HBM) for v in small])
    metas = [meta] + [swap(meta, "order", d) for d in range(1, groups)]

    far = blocks // 2
    middle = slots // 2
    ahead, behind = turn(harmonics, 1), turn(harmonics, -1)
    parts, steps, firsts = [harmonics, ahead, behind], [0, -1, 1], [0, 0, 0]
    tables = pl.pallas_call(
        tables_kernel,
        out_shape=pltpu.VMEM(legendre.shape, jnp.float32),
        in_specs=[hbm],
        out_specs=hbm,
        scratch_shapes=[pltpu.SemaphoreType.DMA((slots,))],
        compiler_params=pltpu.CompilerParams(vmem_limit_bytes=2 * MIB),
        cost_estimate=estimate(1.5),
        name="tables",
    )(pltpu.with_memory_space_constraint(legendre, pltpu.HBM))
    ahead, tables, *metas = lax.optimization_barrier((ahead, tables, *metas))
    ahead = [ahead[:middle], ahead[middle:]]
    behind = [behind[:middle], behind[middle:]]

    sky = sky_map.reshape(cycles, 2, rows, LANES).transpose(0, 2, 1, 3)
    sky = sky.reshape(cycles, 2 * rows, LANES)
    pieces, acs, asc, fine, section = pl.pallas_call(
        lambda *refs: sky_kernel(normalise, groups, slots, cycles, *refs),
        out_shape=(
            shape(groups, 8, LANES),
            shape(cycles, 2 * rows, 2 * every),
            shape(cycles, 2 * rows, 2 * every),
            shape(cycles, LANES, 2 * every),
            shape(cycles, 2 * rows, LANES),
        ),
        in_specs=[vmem()] * groups + [hbm],
        out_specs=(vmem(),) * 5,
        scratch_shapes=[
            pltpu.VMEM((cycles, 2 * rows, LANES), jnp.float32),
            pltpu.SemaphoreType.DMA,
        ],
        compiler_params=pltpu.CompilerParams(vmem_limit_bytes=16 * MIB),
        cost_estimate=estimate(3),
        name="sky_analysis",
    )(*metas, pltpu.with_memory_space_constraint(sky, pltpu.HBM))
    gram = pl.pallas_call(
        lambda *refs: gram_kernel(normalise, groups, slots, cycles, *refs),
        out_shape=shape(slots, count, 4 * every),
        in_specs=[vmem()] * groups,
        out_specs=vmem(),
        compiler_params=pltpu.CompilerParams(vmem_limit_bytes=8 * MIB),
        cost_estimate=estimate(1),
        name="response",
    )(*metas)

    for k in range(2, far):
        ahead = [turn(value, 1) for value in ahead]
        behind = [turn(value, -1) for value in behind[::-1]][::-1]
        parts += ahead + behind
        steps += [-k, -k, k, k]
        firsts += [0, middle] * 2
        if k == 2:
            ahead[0], pieces = lax.optimization_barrier((ahead[0], pieces))
    ends = [turn(ahead[0], 1), turn(behind[1], -1)]

    whole = pltpu.VMEM((slots, 4, count, LANES), jnp.float32)
    sums = pl.pallas_call(
        lambda *refs: forward_kernel(steps, firsts, *refs),
        out_shape=whole,
        in_specs=[vmem()] * (2 + len(parts)),
        out_specs=vmem(),
        scratch_shapes=[pltpu.VMEM((slots, 4, degrees), jnp.float32)],
        compiler_params=pltpu.CompilerParams(vmem_limit_bytes=24 * MIB),
        cost_estimate=estimate(2),
        name="forward",
    )(meta, tables, *parts)
    phases, *outs = pl.pallas_call(
        lambda *refs: phases_kernel(groups, *refs),
        out_shape=[shape(count, LANES)] + [shape(count + 8, LANES)] * (groups - 1),
        in_specs=[vmem()] * 6,
        out_specs=[vmem()] * groups,
        compiler_params=pltpu.CompilerParams(vmem_limit_bytes=16 * MIB),
        cost_estimate=estimate(1),
        name="phases",
    )(meta, tables, pieces, sums, *ends)
    messages = [swap(outs[d - 1], "order", d) for d in range(1, groups)]

    half = pltpu.VMEM((middle, 4, width), jnp.float32)
    *sends, analysed = pl.pallas_call(
        lambda *refs: analysed_kernel(groups, cycles, *refs),
        out_shape=[half] * 2 + [whole],
        in_specs=[vmem()] * (3 + groups),
        out_specs=[vmem()] * 3,
        scratch_shapes=[pltpu.VMEM((count, LANES), jnp.float32)],
        compiler_params=pltpu.CompilerParams(vmem_limit_bytes=16 * MIB),
        cost_estimate=estimate(1),
        name="analysed",
    )(tables, gram, pieces, phases, *messages)
    second = pl.pallas_call(
        second_kernel,
        out_shape=[half] * 2,
        in_specs=[vmem()] * 2,
        out_specs=[vmem()] * 2,
        compiler_params=pltpu.CompilerParams(vmem_limit_bytes=16 * MIB),
        cost_estimate=estimate(0.5),
        name="second",
    )(tables, analysed)

    def backward(core, *before):
        return pl.pallas_call(
            lambda *refs: backward_kernel(core, *refs),
            out_shape=pltpu.VMEM((blocks, slots, 4, width), jnp.float32),
            in_specs=[vmem()] * 2 + [hbm] * len(before),
            out_specs=vmem(),
            input_output_aliases={2: 0} if before else {},
            compiler_params=pltpu.CompilerParams(vmem_limit_bytes=16 * MIB),
            cost_estimate=estimate(2),
            name="backward",
        )(
            tables, analysed,
            *[pltpu.with_memory_space_constraint(value, pltpu.VMEM) for value in before],
        )

    piece = backward(1)
    *sends, piece = lax.optimization_barrier((*sends, piece))
    piece = backward(0, piece)

    def add(index, first, value):
        return pl.pallas_call(
            lambda *refs: add_kernel(index, first, *refs),
            out_shape=half,
            in_specs=[vmem()] * 2,
            out_specs=vmem(),
            compiler_params=pltpu.CompilerParams(vmem_limit_bytes=4 * MIB),
            cost_estimate=estimate(0.1),
            name="add",
        )(piece, pltpu.with_memory_space_constraint(value, pltpu.VMEM))

    sent = dict(zip(((1, 0), (-1, middle), (-1, 0), (1, middle)), (*sends, *second)))
    first_hop = {key: turn(sent[key], key[0]) for key in ((1, 0), (-1, middle))}
    for key in ((1, 0), (-1, middle)):
        sent[key] = add((key[0] * (far - 1)) % blocks, key[1], first_hop[key])
    for k in reversed(range(1, far)):
        for key in ((1, middle), (-1, 0), (1, 0), (-1, middle)):
            sent[key] = turn(sent[key], key[0])
            if k > 1:
                sent[key] = add((key[0] * (k - 1)) % blocks, key[1], sent[key])
    received = [sent[key] for key in ((1, 0), (1, middle), (-1, 0), (-1, middle))]
    refined = pl.pallas_call(
        final_kernel,
        out_shape=shape(*harmonics.shape),
        in_specs=[vmem()] * 7,
        out_specs=vmem(),
        compiler_params=pltpu.CompilerParams(vmem_limit_bytes=8 * MIB),
        cost_estimate=pl.CostEstimate(flops=10**5, bytes_accessed=10**6, transcendentals=0),
        name="refine",
    )(
        meta, harmonics, piece,
        *[pltpu.with_memory_space_constraint(value, pltpu.VMEM) for value in received],
    )

    residual = pl.pallas_call(
        lambda *refs: residual_kernel(groups, slots, cycles, *refs),
        out_shape=shape(cycles, 2 * rows, LANES),
        in_specs=[vmem()] * (4 + 2 * groups),
        out_specs=vmem(),
        scratch_shapes=[pltpu.VMEM((4, count, 2 * every), jnp.float32)],
        compiler_params=pltpu.CompilerParams(vmem_limit_bytes=16 * MIB),
        cost_estimate=pl.CostEstimate(flops=10**8, bytes_accessed=2 * MIB, transcendentals=0),
        name="residual",
    )(*metas, section, acs, asc, fine, phases, *messages)
    residual = residual.reshape(cycles, rows, 2, LANES).transpose(0, 2, 1, 3)
    return (refined, residual.reshape(sky_map.shape))


def solution(mesh):
    return jax.shard_map(
        body,
        mesh=mesh,
        in_specs=(
            P("order", None, "blk"),
            P("order", None, "blk", None),
            P(("blk", "order"), None, None),
            P(("blk", "order")),
            P(("blk", "order")),
            P(("blk", "order")),
            P("order"),
        ),
        out_specs=(P("order", None, "blk"), P(("blk", "order"), None, None)),
        check_vma=False,
    )
```

```python
import math

import jax
import jax.numpy as jnp
from jax import lax
from jax.experimental import pallas as pl
from jax.experimental.pallas import tpu as pltpu
from jax.sharding import PartitionSpec as P

HIGHEST = lax.Precision.HIGHEST
LANES = 128
VMEM = pltpu.VMEM
MIB = 1024 * 1024


def ring_of(blocks):
    return list(range(0, blocks, 2)) + list(range(blocks - 1, 0, -2))


def ring_place(block, blocks):
    return jnp.where(block % 2 == 0, block // 2, blocks - 1 - block // 2)


def block_at(place, blocks):
    place = lax.rem(place + 2 * blocks, blocks)
    return jnp.where(place < blocks // 2, 2 * place, 2 * (blocks - 1 - place) + 1)


def sin_pi(x):
    turns = jnp.round(x)
    y = (x - turns) * math.pi
    z = y * y
    value = -1.0 / 39916800
    for term in (1.0 / 362880, -1.0 / 5040, 1.0 / 120, -1.0 / 6, 1.0):
        value = value * z + term
    value = value * y
    return jnp.where(turns.astype(jnp.int32) % 2 != 0, -value, value)


def half_turns(order, step, length):
    total = order * step
    period = 2 * length
    scale = 0.5 / length.astype(jnp.float32)
    for _ in range(2):
        total = total - jnp.floor(total.astype(jnp.float32) * scale).astype(jnp.int32) * period
    return total.astype(jnp.float32) / length.astype(jnp.float32)


def pixel_mask(shape, length):
    pixel = lax.broadcasted_iota(jnp.int32, shape, 0) // 2 * shape[1]
    pixel = pixel + lax.broadcasted_iota(jnp.int32, shape, 1)
    return pixel < length


def meta_kernel(slots, cycles, ids, length, offset, weight, out_ref, *scratch):
    *held, sems = scratch
    copies = [
        pltpu.make_async_copy(source, target, sems.at[k])
        for k, (source, target) in enumerate(zip((ids, length, offset, weight), held))
    ]
    for copy in copies:
        copy.start()
    for copy in copies:
        copy.wait()
    lane = lax.broadcasted_iota(jnp.int32, (1, LANES), 1)
    out = jnp.zeros((1, LANES), jnp.float32)
    for m in range(slots):
        out = jnp.where(lane == m, held[0][m].astype(jnp.float32), out)
    for c in range(cycles):
        for k in range(3):
            value = held[1 + k][c].astype(jnp.float32)
            out = jnp.where(lane == slots + k * cycles + c, value, out)
    out_ref[...] = out


def entry(meta, at):
    return meta[:, at : at + 1]


def spread_ids(metas, slots, sources):
    per = LANES // slots
    lane = lax.broadcasted_iota(jnp.int32, (1, LANES), 1)
    pieces = []
    for start in range(0, len(sources), per):
        piece = jnp.zeros((1, LANES), jnp.float32)
        for k in range(per):
            value = metas[sources[start + k]]
            value = pltpu.roll(value, k * slots, 1) if k else value
            piece = jnp.where(lane // slots == k, value, piece)
        pieces.append(piece)
    return jnp.concatenate(pieces, axis=1)


def sky_kernel(normalise, groups, slots, cycles, *rest):
    metas = [ref[...] for ref in rest[:groups]]
    sky_hbm, pieces_ref, acs_ref, asc_ref, fine_ref, section_ref, sky_ref, sky_sem = rest[groups:]
    sky_copy = pltpu.make_async_copy(sky_hbm, sky_ref, sky_sem)
    sky_copy.start()
    rows, both = acs_ref.shape[1:]
    every = both // 2
    ids = spread_ids(metas, slots, [d for _ in range(2) for d in range(groups)])
    ids = ids.astype(jnp.int32)
    row8 = lax.broadcasted_iota(jnp.int32, (8, both), 0)
    sums = [jnp.zeros((8, both), jnp.float32) for _ in range(4)]
    for c in range(cycles):
        length = entry(metas[0], slots + c).astype(jnp.int32)
        offset = entry(metas[0], slots + cycles + c).astype(jnp.int32)
        coarse = lax.broadcasted_iota(jnp.int32, (rows, both), 0) // 2 * (2 * LANES) + offset
        x = half_turns(ids, coarse, length)
        first = lax.broadcasted_iota(jnp.int32, (rows, both), 1) < every
        acs = sin_pi(x + jnp.where(first, 0.5, 1.0))
        asc = sin_pi(x + jnp.where(first, 0.0, 0.5))
        acs_ref[c] = acs
        asc_ref[c] = asc
        fine = 2 * lax.broadcasted_iota(jnp.int32, (LANES, both), 0)
        x = half_turns(ids, fine, length)
        first = lax.broadcasted_iota(jnp.int32, (LANES, both), 1) < every
        table = sin_pi(x + jnp.where(first, 0.5, 0.0))
        fine_ref[c] = table
        if c == 0:
            sky_copy.wait()
        section = jnp.where(pixel_mask((rows, LANES), length), sky_ref[c], 0.0)
        section_ref[c] = section
        spun = jnp.dot(section, table, precision=HIGHEST, preferred_element_type=jnp.float32)
        weight = entry(metas[0], slots + 2 * cycles + c) * normalise
        for k, value in enumerate((spun * acs, spun * asc)):
            value = sum(value[8 * i : 8 * i + 8] for i in range(rows // 8))
            for q in range(2):
                total = jnp.sum(jnp.where(row8 % 2 == q, value, 0.0), axis=0, keepdims=True)
                total = total * (-weight if k else weight)
                sums[2 * q + k] = jnp.where(row8 == c, total, sums[2 * q + k])
    lane = lax.broadcasted_iota(jnp.int32, (8, LANES), 1)
    totals = []
    for value in sums:
        tiles = [value[:, i : i + LANES] for i in range(0, both, LANES)]
        if every < LANES:
            shift = every
            while shift < LANES:
                tiles[0] = tiles[0] + pltpu.roll(tiles[0], shift, 1)
                shift *= 2
            totals.append(tiles)
        else:
            half = len(tiles) // 2
            totals.append([tiles[i] + tiles[half + i] for i in range(half)])
    for d in range(groups):
        piece = jnp.zeros((8, LANES), jnp.float32)
        tile, at = divmod(d * slots, LANES)
        for a in range(4):
            shift = (a * slots - at) % LANES
            value = totals[a][tile]
            value = pltpu.roll(value, shift, 1) if shift else value
            piece = jnp.where(lane // slots == a, value, piece)
        pieces_ref[d] = piece


def gram_kernel(normalise, groups, slots, cycles, *rest):
    metas = [ref[...] for ref in rest[:groups]]
    (gram_ref,) = rest[groups:]
    me = lax.axis_index("order")
    count, wide = gram_ref.shape[1:]
    row = lax.broadcasted_iota(jnp.int32, (count, wide), 0)
    length = jnp.ones((count, wide), jnp.float32)
    offset = jnp.zeros((count, wide), jnp.float32)
    weight = jnp.zeros((count, wide), jnp.float32)
    for d in range(groups):
        for c in range(cycles):
            here = row == (me ^ d) * cycles + c
            length = jnp.where(here, entry(metas[d], slots + c), length)
            offset = jnp.where(here, entry(metas[d], slots + cycles + c), offset)
            weight = jnp.where(here, entry(metas[d], slots + 2 * cycles + c), weight)
    others = spread_ids(metas, slots, [d for d in range(groups) for _ in range(4)])
    lane = lax.broadcasted_iota(jnp.int32, (count, wide), 1)
    cosine = (lane // slots) % 2 == 0
    factor = jnp.where(others == 0.0, 0.5, 1.0) * normalise * weight * length
    inverse = 1.0 / length
    odd = offset > 0.5

    def response(n):
        turns = jnp.round(n * inverse)
        sign = jnp.where(odd & (turns.astype(jnp.int32) % 2 != 0), -1.0, 1.0)
        return jnp.where(turns * length == n, sign, 0.0)

    for m in range(slots):
        mine = entry(metas[0], m)
        near = response(mine - others)
        far = response(mine + others)
        gram_ref[m] = factor * (near + jnp.where(cosine, far, -far))


def table_copies(legendre, tables, sems):
    slots, _, _, degrees = tables.shape
    copies = []
    for m in range(slots):
        first = m * (degrees // slots)
        part = (m, slice(None), slice(None), pl.ds(first, degrees - first))
        copies.append(pltpu.make_async_copy(legendre.at[part], tables.at[part], sems.at[m]))
    return copies


def use_tile(tables, m, span, keep, coefs, p, n):
    plus = tables[m, 0, :, span]
    minus = tables[m, 1, :, span]
    if keep is not None:
        plus = jnp.where(keep, plus, 0.0)
        minus = jnp.where(keep, minus, 0.0)
    for a in range(4):
        c = coefs(a)
        p[a] = p[a] + plus * c
        n[a] = n[a] + minus * c


def fold_lanes(values, lane):
    step = 1
    while step < LANES:
        if len(values) > 1:
            low = (lane & step) == 0
            values = [
                jnp.where(low, values[i], values[i + 1])
                + pltpu.roll(jnp.where(low, values[i + 1], values[i]), step, 1)
                for i in range(0, len(values), 2)
            ]
        else:
            values = [values[0] + pltpu.roll(values[0], step, 1)]
        step *= 2
    return values[0]


def combine(p, n):
    return [n[3] - p[0], -p[1] - n[2], -p[2] - n[1], n[0] - p[3]]


def on_core(core):
    return lax.axis_index("order") % 2 == core


def tables_kernel(legendre, tables, sems):
    copies = table_copies(legendre, tables, sems)
    for copy in copies:
        copy.start()
    for copy in copies:
        copy.wait()


def forward_kernel(steps, firsts, meta_ref, tables, *rest):
    parts = rest[: len(steps)]
    sums_ref, coefs = rest[len(steps) :]
    slots, _, count, degrees = tables.shape
    width = parts[0].shape[2]
    blocks = degrees // width
    stratum = degrees // slots
    meta = meta_ref[...]
    place = ring_place(lax.axis_index("blk"), blocks)
    for part, step, low in zip(parts, steps, firsts):
        first = pl.multiple_of(block_at(place + step, blocks) * width, LANES)
        for m in range(part.shape[0]):
            coefs[low + m, :, pl.ds(first, width)] = part[m]
    first = pl.multiple_of(block_at(place + blocks // 2, blocks) * width, LANES)
    for m in range(slots):
        coefs[m, :, pl.ds(first, width)] = jnp.zeros((4, width), jnp.float32)
    lane = lax.broadcasted_iota(jnp.int32, (count, LANES), 1)
    for m in range(slots):
        floor = jnp.maximum(entry(meta, m).astype(jnp.int32), 2)
        p = [jnp.zeros((count, LANES), jnp.float32)] * 4
        n = [jnp.zeros((count, LANES), jnp.float32)] * 4
        for t in range(stratum * m // LANES, degrees // LANES):
            span = slice(t * LANES, (t + 1) * LANES)
            keep = lane >= floor - t * LANES if t * LANES < stratum * (m + 1) else None
            use_tile(tables, m, span, keep, lambda a: coefs[m, a : a + 1, span], p, n)
        for a, total in enumerate(combine(p, n)):
            sums_ref[m, a] = total


def phases_kernel(groups, meta_ref, tables, pieces_ref, sums_ref, low_ref, high_ref, *rest):
    phases_ref, *messages = rest
    slots, _, count, degrees = tables.shape
    middle, _, width = low_ref.shape
    blocks = degrees // width
    meta = meta_ref[...]
    place = ring_place(lax.axis_index("blk"), blocks)
    first = pl.multiple_of(block_at(place + blocks // 2, blocks) * width, LANES)
    lane = lax.broadcasted_iota(jnp.int32, (count, LANES), 1)
    totals = [None] * (4 * slots)
    for m in range(slots):
        floor = jnp.maximum(entry(meta, m).astype(jnp.int32), 2) - first
        part, at = (low_ref, m) if m < middle else (high_ref, m - middle)
        p = [jnp.zeros((count, LANES), jnp.float32)] * 4
        n = [jnp.zeros((count, LANES), jnp.float32)] * 4
        for t in range(width // LANES):
            here = slice(t * LANES, (t + 1) * LANES)
            keep = lane >= floor - t * LANES
            span = pl.ds(first + t * LANES, LANES)
            use_tile(tables, m, span, keep, lambda a: part[at, a : a + 1, here], p, n)
        for a, total in enumerate(combine(p, n)):
            totals[a * slots + m] = total + sums_ref[m, a]
    phases = fold_lanes(totals, lane)
    phases_ref[...] = phases
    for d in range(1, groups):
        messages[d - 1][:count] = phases
        messages[d - 1][count:] = pieces_ref[d]


def fold_rows(values, row):
    for step in (1, 2, 4):
        low = (row & step) == 0
        values = [
            jnp.where(low, values[i], values[i + 1])
            + pltpu.roll(jnp.where(low, values[i + 1], values[i]), step, 0)
            for i in range(0, len(values), 2)
        ]
    return values[0]


def update_tiles(tables, m, spans, an, ng, row8):
    count = tables.shape[2]
    values = []
    for span in spans:
        plus = tables[m, 0, :, span]
        minus = tables[m, 1, :, span]
        four = [
            plus * ng[0] + minus * an[3],
            plus * ng[1] + minus * ng[2],
            plus * ng[2] + minus * ng[1],
            plus * ng[3] + minus * an[0],
        ]
        values += [sum(v[8 * k : 8 * k + 8] for k in range(count // 8)) for v in four]
    return fold_rows(values, row8)


def update_block(tables, m, first, an, ng, row8, out, at):
    for t in range(0, out.shape[2] // LANES, 2):
        spans = [pl.ds(first + u * LANES, LANES) for u in (t, t + 1)]
        folded = update_tiles(tables, m, spans, an, ng, row8)
        for k, u in enumerate((t, t + 1)):
            out[at, :, u * LANES : (u + 1) * LANES] = folded[4 * k : 4 * k + 4]


def analysed_kernel(groups, cycles, tables, gram_ref, pieces_ref, phases_ref, *rest):
    messages = rest[: groups - 1]
    *sends, analysed_ref, sky = rest[groups - 1 :]
    slots, _, count, degrees = tables.shape
    middle, _, width = sends[0].shape
    blocks = degrees // width
    far = blocks // 2
    place = ring_place(lax.axis_index("blk"), blocks)
    first = pl.multiple_of(block_at(place + far, blocks) * width, LANES)
    owner = lax.axis_index("order")
    wide = 4 * slots
    pairs = []
    for d in range(groups):
        phases = phases_ref[...] if d == 0 else messages[d - 1][:count]
        piece = pieces_ref[0] if d == 0 else messages[d - 1][count:]
        sky[pl.ds((owner ^ d) * cycles, cycles)] = piece[:cycles]
        pairs.append(phases)
    lane = lax.broadcasted_iota(jnp.int32, (count, LANES), 1)
    row8 = lax.broadcasted_iota(jnp.int32, (8, LANES), 0)
    per = LANES // wide
    packed = []
    for start in range(0, groups, per):
        value = pairs[start]
        for k in range(1, per):
            value = jnp.where(
                lane // wide == k, pltpu.roll(pairs[start + k], k * wide, 1), value
            )
        packed.append(value)
    observed = sky[...]
    for m in range(slots):
        total = jnp.where((lane < wide) & (lane % slots == m), observed, 0.0)
        for k, value in enumerate(packed):
            total = total - gram_ref[m, :, k * LANES : (k + 1) * LANES] * value
        an = []
        for a in range(4):
            value = jnp.where((lane % wide) // slots == a, total, 0.0)
            value = jnp.sum(value, axis=1, keepdims=True)
            an.append(jnp.broadcast_to(value, (count, LANES)))
            analysed_ref[m, a] = an[a]
        ng = [-value for value in an]
        half, at = divmod(m, middle)
        update_block(tables, m, first, an, ng, row8, sends[half], at)


def second_kernel(ways, tables, analysed_ref, low_ref, high_ref):
    slots, _, _, degrees = tables.shape
    middle, _, width = low_ref.shape
    blocks = degrees // width
    place = ring_place(lax.axis_index("blk"), blocks)
    row8 = lax.broadcasted_iota(jnp.int32, (8, LANES), 0)
    for m in range(slots):
        half, at = divmod(m, middle)
        step = ways[half] * (blocks // 2 - 1)
        first = pl.multiple_of(block_at(place + step, blocks) * width, LANES)
        an = [analysed_ref[m, a] for a in range(4)]
        ng = [-value for value in an]
        update_block(tables, m, first, an, ng, row8, (low_ref, high_ref)[half], at)


def backward_kernel(core, tables, analysed_ref, *rest):
    if core is None:
        backward_blocks(tables, analysed_ref, rest[-1])
    else:
        pl.when(on_core(core))(lambda: backward_blocks(tables, analysed_ref, rest[-1]))


def backward_blocks(tables, analysed_ref, out):
    slots, _, _, degrees = tables.shape
    blocks, _, _, width = out.shape
    stratum = degrees // slots
    place = ring_place(lax.axis_index("blk"), blocks)
    ring = ring_of(blocks)
    step_of = [lax.rem(ring.index(b) - place + blocks, blocks) for b in range(blocks)]
    row8 = lax.broadcasted_iota(jnp.int32, (8, LANES), 0)
    for m in range(slots):
        an = [analysed_ref[m, a] for a in range(4)]
        ng = [-value for value in an]
        for t in range(stratum * m // LANES, degrees // LANES, 2):
            spans = [slice(u * LANES, (u + 1) * LANES) for u in (t, t + 1)]
            folded = update_tiles(tables, m, spans, an, ng, row8)
            for k, u in enumerate((t, t + 1)):
                inner = u * LANES % width
                out[step_of[u * LANES // width], m, :, inner : inner + LANES] = folded[
                    4 * k : 4 * k + 4
                ]


def residual_kernel(groups, slots, cycles, *rest):
    metas = [ref[...] for ref in rest[:groups]]
    section_ref, acs_ref, asc_ref, fine_ref, phases_ref = rest[groups : groups + 5]
    messages = rest[groups + 5 : 2 * groups + 4]
    out_ref, spread = rest[2 * groups + 4 :]
    owner = lax.axis_index("order")
    rows, both = acs_ref.shape[1:]
    every = both // 2
    count = phases_ref.shape[0]
    lane = lax.broadcasted_iota(jnp.int32, (count, LANES), 1)
    ids = spread_ids(metas, slots, [d for _ in range(2) for d in range(groups)])
    factor = jnp.where(ids == 0.0, 1.0, 2.0)
    per = LANES // slots
    values = [phases_ref[...]] + [ref[:count] for ref in messages]
    for a in range(4):
        tiles = []
        for start in range(0, 2 * groups, per):
            tile = jnp.zeros((count, LANES), jnp.float32)
            for k in range(per):
                shift = (k - a) * slots % LANES
                value = values[(start + k) % groups]
                value = pltpu.roll(value, shift, 1) if shift else value
                tile = jnp.where(lane // slots == k, value, tile)
            tiles.append(tile)
        spread[a] = jnp.concatenate(tiles, axis=1) * factor
    even = lax.broadcasted_iota(jnp.int32, (rows, both), 0) % 2 == 0
    for c in range(cycles):
        q_re, q_im, u_re, u_im = [spread[a, pl.ds(owner * cycles + c, 1)] for a in range(4)]
        weights = jnp.where(even, q_re, u_re) * acs_ref[c]
        weights = weights - jnp.where(even, q_im, u_im) * asc_ref[c]
        model = lax.dot_general(
            weights, fine_ref[c], (((1,), (1,)), ((), ())), precision=HIGHEST,
            preferred_element_type=jnp.float32,
        )
        inside = pixel_mask((rows, LANES), entry(metas[0], slots + c).astype(jnp.int32))
        out_ref[c] = section_ref[c] - jnp.where(inside, model, 0.0)


def join_kernel(own_ref, value_ref, out_ref):
    out_ref[...] = own_ref[...] + value_ref[...]


def add_kernel(index, first, piece_ref, value_ref, out_ref):
    out_ref[...] = piece_ref[index, first : first + out_ref.shape[0]] + value_ref[...]


def final_kernel(meta_ref, harmonics_ref, piece_ref, *rest):
    *received, out_ref = rest
    slots, parts, width = out_ref.shape
    middle = slots // 2
    start = lax.axis_index("blk") * width
    degree = start + lax.broadcasted_iota(jnp.int32, (parts, width), 1)
    meta = meta_ref[...]
    for m in range(slots):
        h, at = divmod(m, middle)
        update = piece_ref[0, m] + (received[h][at] + received[2 + h][at])
        valid = degree >= jnp.maximum(entry(meta, m).astype(jnp.int32), 2)
        out_ref[m] = jnp.where(valid, harmonics_ref[m] + update, 0.0)


def vmem():
    return pl.BlockSpec(memory_space=VMEM)


def shape(*dims):
    return jax.ShapeDtypeStruct(dims, jnp.float32)


def body(harmonics, legendre, sky_map, cycle_length, cycle_offset, cycle_weight, order_ids):
    groups = lax.axis_size("order")
    blocks = lax.axis_size("blk")
    slots, _, width = harmonics.shape
    count, degrees = legendre.shape[2:]
    cycles, _, pixels = sky_map.shape
    rows = pixels // LANES
    every = slots * groups
    normalise = math.sqrt(degrees * every / (cycles * groups * blocks * pixels))

    def swap(value, axis, step):
        size = lax.axis_size(axis)
        return lax.ppermute(value, axis, [(i, i ^ step) for i in range(size)])

    ring = ring_of(blocks)

    def turn(value, way):
        pairs = [(ring[p], ring[(p + way) % blocks]) for p in range(blocks)]
        return lax.ppermute(value, "blk", pairs)

    def estimate(micros):
        return pl.CostEstimate(flops=0, bytes_accessed=int(micros * 3.0e6), transcendentals=0)

    hbm = pl.BlockSpec(memory_space=pl.ANY)
    small = (order_ids, cycle_length, cycle_offset, cycle_weight)
    meta = pl.pallas_call(
        lambda *refs: meta_kernel(slots, cycles, *refs),
        out_shape=pltpu.VMEM((1, LANES), jnp.float32),
        in_specs=[hbm] * 4,
        out_specs=vmem(),
        scratch_shapes=[pltpu.SMEM(v.shape, v.dtype) for v in small]
        + [pltpu.SemaphoreType.DMA((len(small),))],
        compiler_params=pltpu.CompilerParams(vmem_limit_bytes=2 * MIB),
        name="meta",
    )(*[pltpu.with_memory_space_constraint(v, pltpu.HBM) for v in small])
    metas = [meta] + [swap(meta, "order", d) for d in range(1, groups)]

    far = blocks // 2
    middle = slots // 2
    ahead, behind = turn(harmonics, 1), turn(harmonics, -1)
    parts, steps, firsts = [harmonics, ahead, behind], [0, -1, 1], [0, 0, 0]
    tables = pl.pallas_call(
        tables_kernel,
        out_shape=pltpu.VMEM(legendre.shape, jnp.float32),
        in_specs=[hbm],
        out_specs=hbm,
        scratch_shapes=[pltpu.SemaphoreType.DMA((slots,))],
        compiler_params=pltpu.CompilerParams(vmem_limit_bytes=2 * MIB),
        cost_estimate=estimate(1.5),
        name="tables",
    )(pltpu.with_memory_space_constraint(legendre, pltpu.HBM))
    ahead, tables, *metas = lax.optimization_barrier((ahead, tables, *metas))
    ahead = [ahead[:middle], ahead[middle:]]
    behind = [behind[:middle], behind[middle:]]

    sky = sky_map.reshape(cycles, 2, rows, LANES).transpose(0, 2, 1, 3)
    sky = sky.reshape(cycles, 2 * rows, LANES)
    pieces, acs, asc, fine, section = pl.pallas_call(
        lambda *refs: sky_kernel(normalise, groups, slots, cycles, *refs),
        out_shape=(
            shape(groups, 8, LANES),
            shape(cycles, 2 * rows, 2 * every),
            shape(cycles, 2 * rows, 2 * every),
            shape(cycles, LANES, 2 * every),
            shape(cycles, 2 * rows, LANES),
        ),
        in_specs=[vmem()] * groups + [hbm],
        out_specs=(vmem(),) * 5,
        scratch_shapes=[
            pltpu.VMEM((cycles, 2 * rows, LANES), jnp.float32),
            pltpu.SemaphoreType.DMA,
        ],
        compiler_params=pltpu.CompilerParams(vmem_limit_bytes=16 * MIB),
        cost_estimate=estimate(3),
        name="sky_analysis",
    )(*metas, pltpu.with_memory_space_constraint(sky, pltpu.HBM))
    gram = pl.pallas_call(
        lambda *refs: gram_kernel(normalise, groups, slots, cycles, *refs),
        out_shape=shape(slots, count, 4 * every),
        in_specs=[vmem()] * groups,
        out_specs=vmem(),
        compiler_params=pltpu.CompilerParams(vmem_limit_bytes=8 * MIB),
        cost_estimate=estimate(1),
        name="response",
    )(*metas)

    for k in range(2, far):
        ahead = [turn(value, 1) for value in ahead]
        behind = [turn(value, -1) for value in behind[::-1]][::-1]
        parts += ahead + behind
        steps += [-k, -k, k, k]
        firsts += [0, middle] * 2
        if k == 2:
            ahead[0], pieces = lax.optimization_barrier((ahead[0], pieces))
    ends = [turn(ahead[0], 1), turn(behind[1], -1)]

    whole = pltpu.VMEM((slots, 4, count, LANES), jnp.float32)
    sums = pl.pallas_call(
        lambda *refs: forward_kernel(steps, firsts, *refs),
        out_shape=whole,
        in_specs=[vmem()] * (2 + len(parts)),
        out_specs=vmem(),
        scratch_shapes=[pltpu.VMEM((slots, 4, degrees), jnp.float32)],
        compiler_params=pltpu.CompilerParams(vmem_limit_bytes=24 * MIB),
        cost_estimate=estimate(2),
        name="forward",
    )(meta, tables, *parts)
    phases, *outs = pl.pallas_call(
        lambda *refs: phases_kernel(groups, *refs),
        out_shape=[shape(count, LANES)] + [shape(count + 8, LANES)] * (groups - 1),
        in_specs=[vmem()] * 6,
        out_specs=[vmem()] * groups,
        compiler_params=pltpu.CompilerParams(vmem_limit_bytes=16 * MIB),
        cost_estimate=estimate(1),
        name="phases",
    )(meta, tables, pieces, sums, *ends)
    messages = [swap(outs[d - 1], "order", d) for d in range(1, groups)]

    half = pltpu.VMEM((middle, 4, width), jnp.float32)
    *sends, analysed = pl.pallas_call(
        lambda *refs: analysed_kernel(groups, cycles, *refs),
        out_shape=[half] * 2 + [whole],
        in_specs=[vmem()] * (3 + groups),
        out_specs=[vmem()] * 3,
        scratch_shapes=[pltpu.VMEM((count, LANES), jnp.float32)],
        compiler_params=pltpu.CompilerParams(vmem_limit_bytes=16 * MIB),
        cost_estimate=estimate(1),
        name="analysed",
    )(tables, gram, pieces, phases, *messages)
    def nearer(ways):
        return pl.pallas_call(
            lambda *refs: second_kernel(ways, *refs),
            out_shape=[half] * 2,
            in_specs=[vmem()] * 2,
            out_specs=[vmem()] * 2,
            compiler_params=pltpu.CompilerParams(vmem_limit_bytes=16 * MIB),
            cost_estimate=estimate(0.5),
            name="second",
        )(tables, analysed)

    second = nearer((-1, 1))
    third = nearer((1, -1))

    def backward(core, *before):
        return pl.pallas_call(
            lambda *refs: backward_kernel(core, *refs),
            out_shape=pltpu.VMEM((blocks, slots, 4, width), jnp.float32),
            in_specs=[vmem()] * 2 + [hbm] * len(before),
            out_specs=vmem(),
            input_output_aliases={2: 0} if before else {},
            compiler_params=pltpu.CompilerParams(vmem_limit_bytes=16 * MIB),
            cost_estimate=estimate(2),
            name="backward",
        )(
            tables, analysed,
            *[pltpu.with_memory_space_constraint(value, pltpu.VMEM) for value in before],
        )

    piece = backward(None)

    def add(index, first, value):
        return pl.pallas_call(
            lambda *refs: add_kernel(index, first, *refs),
            out_shape=half,
            in_specs=[vmem()] * 2,
            out_specs=vmem(),
            compiler_params=pltpu.CompilerParams(vmem_limit_bytes=4 * MIB),
            cost_estimate=estimate(0.1),
            name="add",
        )(piece, pltpu.with_memory_space_constraint(value, pltpu.VMEM))

    sent = dict(zip(((1, 0), (-1, middle), (-1, 0), (1, middle)), (*sends, *second)))
    first_hop = {key: turn(sent[key], key[0]) for key in ((1, 0), (-1, middle))}
    for key, own in zip(((1, 0), (-1, middle)), third):
        sent[key] = pl.pallas_call(
            join_kernel,
            out_shape=half,
            in_specs=[vmem()] * 2,
            out_specs=vmem(),
            compiler_params=pltpu.CompilerParams(vmem_limit_bytes=4 * MIB),
            cost_estimate=estimate(0.1),
            name="join",
        )(own, pltpu.with_memory_space_constraint(first_hop[key], pltpu.VMEM))
    for k in reversed(range(1, far)):
        for key in ((1, middle), (-1, 0), (1, 0), (-1, middle)):
            sent[key] = turn(sent[key], key[0])
            if k > 1:
                sent[key] = add((key[0] * (k - 1)) % blocks, key[1], sent[key])
    received = [sent[key] for key in ((1, 0), (1, middle), (-1, 0), (-1, middle))]
    refined = pl.pallas_call(
        final_kernel,
        out_shape=shape(*harmonics.shape),
        in_specs=[vmem()] * 7,
        out_specs=vmem(),
        compiler_params=pltpu.CompilerParams(vmem_limit_bytes=8 * MIB),
        cost_estimate=pl.CostEstimate(flops=10**5, bytes_accessed=10**6, transcendentals=0),
        name="refine",
    )(
        meta, harmonics, piece,
        *[pltpu.with_memory_space_constraint(value, pltpu.VMEM) for value in received],
    )

    residual = pl.pallas_call(
        lambda *refs: residual_kernel(groups, slots, cycles, *refs),
        out_shape=shape(cycles, 2 * rows, LANES),
        in_specs=[vmem()] * (4 + 2 * groups),
        out_specs=vmem(),
        scratch_shapes=[pltpu.VMEM((4, count, 2 * every), jnp.float32)],
        compiler_params=pltpu.CompilerParams(vmem_limit_bytes=16 * MIB),
        cost_estimate=pl.CostEstimate(flops=10**8, bytes_accessed=2 * MIB, transcendentals=0),
        name="residual",
    )(*metas, section, acs, asc, fine, phases, *messages)
    residual = residual.reshape(cycles, rows, 2, LANES).transpose(0, 2, 1, 3)
    return (refined, residual.reshape(sky_map.shape))


def solution(mesh):
    return jax.shard_map(
        body,
        mesh=mesh,
        in_specs=(
            P("order", None, "blk"),
            P("order", None, "blk", None),
            P(("blk", "order"), None, None),
            P(("blk", "order")),
            P(("blk", "order")),
            P(("blk", "order")),
            P("order"),
        ),
        out_specs=(P("order", None, "blk"), P(("blk", "order"), None, None)),
        check_vma=False,
    )
```

```python
import math

import jax
import jax.numpy as jnp
from jax import lax
from jax.experimental import pallas as pl
from jax.experimental.pallas import tpu as pltpu
from jax.sharding import PartitionSpec as P

HIGHEST = lax.Precision.HIGHEST
LANES = 128
VMEM = pltpu.VMEM
MIB = 1024 * 1024


def ring_of(blocks):
    return list(range(0, blocks, 2)) + list(range(blocks - 1, 0, -2))


def ring_place(block, blocks):
    return jnp.where(block % 2 == 0, block // 2, blocks - 1 - block // 2)


def block_at(place, blocks):
    place = lax.rem(place + 2 * blocks, blocks)
    return jnp.where(place < blocks // 2, 2 * place, 2 * (blocks - 1 - place) + 1)


def sin_pi(x):
    turns = jnp.round(x)
    y = (x - turns) * math.pi
    z = y * y
    value = -1.0 / 39916800
    for term in (1.0 / 362880, -1.0 / 5040, 1.0 / 120, -1.0 / 6, 1.0):
        value = value * z + term
    value = value * y
    return jnp.where(turns.astype(jnp.int32) % 2 != 0, -value, value)


def half_turns(order, step, length):
    total = order * step
    period = 2 * length
    scale = 0.5 / length.astype(jnp.float32)
    for _ in range(2):
        total = total - jnp.floor(total.astype(jnp.float32) * scale).astype(jnp.int32) * period
    return total.astype(jnp.float32) / length.astype(jnp.float32)


def pixel_mask(shape, length):
    pixel = lax.broadcasted_iota(jnp.int32, shape, 0) // 2 * shape[1]
    pixel = pixel + lax.broadcasted_iota(jnp.int32, shape, 1)
    return pixel < length


def meta_kernel(slots, cycles, ids, length, offset, weight, out_ref, *scratch):
    *held, sems = scratch
    copies = [
        pltpu.make_async_copy(source, target, sems.at[k])
        for k, (source, target) in enumerate(zip((ids, length, offset, weight), held))
    ]
    for copy in copies:
        copy.start()
    for copy in copies:
        copy.wait()
    lane = lax.broadcasted_iota(jnp.int32, (1, LANES), 1)
    out = jnp.zeros((1, LANES), jnp.float32)
    for m in range(slots):
        out = jnp.where(lane == m, held[0][m].astype(jnp.float32), out)
    for c in range(cycles):
        for k in range(3):
            value = held[1 + k][c].astype(jnp.float32)
            out = jnp.where(lane == slots + k * cycles + c, value, out)
    out_ref[...] = out


def entry(meta, at):
    return meta[:, at : at + 1]


def spread_ids(metas, slots, sources):
    per = LANES // slots
    lane = lax.broadcasted_iota(jnp.int32, (1, LANES), 1)
    pieces = []
    for start in range(0, len(sources), per):
        piece = jnp.zeros((1, LANES), jnp.float32)
        for k in range(per):
            value = metas[sources[start + k]]
            value = pltpu.roll(value, k * slots, 1) if k else value
            piece = jnp.where(lane // slots == k, value, piece)
        pieces.append(piece)
    return jnp.concatenate(pieces, axis=1)


def sky_kernel(normalise, groups, slots, cycles, *rest):
    metas = [ref[...] for ref in rest[:groups]]
    sky_hbm, pieces_ref, acs_ref, asc_ref, fine_ref, section_ref, sky_ref, sky_sem = rest[groups:]
    sky_copy = pltpu.make_async_copy(sky_hbm, sky_ref, sky_sem)
    sky_copy.start()
    rows, both = acs_ref.shape[1:]
    every = both // 2
    ids = spread_ids(metas, slots, [d for _ in range(2) for d in range(groups)])
    ids = ids.astype(jnp.int32)
    row8 = lax.broadcasted_iota(jnp.int32, (8, both), 0)
    sums = [jnp.zeros((8, both), jnp.float32) for _ in range(4)]
    for c in range(cycles):
        length = entry(metas[0], slots + c).astype(jnp.int32)
        offset = entry(metas[0], slots + cycles + c).astype(jnp.int32)
        coarse = lax.broadcasted_iota(jnp.int32, (rows, both), 0) // 2 * (2 * LANES) + offset
        x = half_turns(ids, coarse, length)
        first = lax.broadcasted_iota(jnp.int32, (rows, both), 1) < every
        acs = sin_pi(x + jnp.where(first, 0.5, 1.0))
        asc = sin_pi(x + jnp.where(first, 0.0, 0.5))
        acs_ref[c] = acs
        asc_ref[c] = asc
        fine = 2 * lax.broadcasted_iota(jnp.int32, (LANES, both), 0)
        x = half_turns(ids, fine, length)
        first = lax.broadcasted_iota(jnp.int32, (LANES, both), 1) < every
        table = sin_pi(x + jnp.where(first, 0.5, 0.0))
        fine_ref[c] = table
        if c == 0:
            sky_copy.wait()
        section = jnp.where(pixel_mask((rows, LANES), length), sky_ref[c], 0.0)
        section_ref[c] = section
        spun = jnp.dot(section, table, precision=HIGHEST, preferred_element_type=jnp.float32)
        weight = entry(metas[0], slots + 2 * cycles + c) * normalise
        for k, value in enumerate((spun * acs, spun * asc)):
            value = sum(value[8 * i : 8 * i + 8] for i in range(rows // 8))
            for q in range(2):
                total = jnp.sum(jnp.where(row8 % 2 == q, value, 0.0), axis=0, keepdims=True)
                total = total * (-weight if k else weight)
                sums[2 * q + k] = jnp.where(row8 == c, total, sums[2 * q + k])
    lane = lax.broadcasted_iota(jnp.int32, (8, LANES), 1)
    totals = []
    for value in sums:
        tiles = [value[:, i : i + LANES] for i in range(0, both, LANES)]
        if every < LANES:
            shift = every
            while shift < LANES:
                tiles[0] = tiles[0] + pltpu.roll(tiles[0], shift, 1)
                shift *= 2
            totals.append(tiles)
        else:
            half = len(tiles) // 2
            totals.append([tiles[i] + tiles[half + i] for i in range(half)])
    for d in range(groups):
        piece = jnp.zeros((8, LANES), jnp.float32)
        tile, at = divmod(d * slots, LANES)
        for a in range(4):
            shift = (a * slots - at) % LANES
            value = totals[a][tile]
            value = pltpu.roll(value, shift, 1) if shift else value
            piece = jnp.where(lane // slots == a, value, piece)
        pieces_ref[d] = piece


def gram_kernel(normalise, groups, slots, cycles, *rest):
    metas = [ref[...] for ref in rest[:groups]]
    (gram_ref,) = rest[groups:]
    me = lax.axis_index("order")
    count, wide = gram_ref.shape[1:]
    row = lax.broadcasted_iota(jnp.int32, (count, wide), 0)
    length = jnp.ones((count, wide), jnp.float32)
    offset = jnp.zeros((count, wide), jnp.float32)
    weight = jnp.zeros((count, wide), jnp.float32)
    for d in range(groups):
        for c in range(cycles):
            here = row == (me ^ d) * cycles + c
            length = jnp.where(here, entry(metas[d], slots + c), length)
            offset = jnp.where(here, entry(metas[d], slots + cycles + c), offset)
            weight = jnp.where(here, entry(metas[d], slots + 2 * cycles + c), weight)
    others = spread_ids(metas, slots, [d for d in range(groups) for _ in range(4)])
    lane = lax.broadcasted_iota(jnp.int32, (count, wide), 1)
    cosine = (lane // slots) % 2 == 0
    factor = jnp.where(others == 0.0, 0.5, 1.0) * normalise * weight * length
    inverse = 1.0 / length
    odd = offset > 0.5

    def response(n):
        turns = jnp.round(n * inverse)
        sign = jnp.where(odd & (turns.astype(jnp.int32) % 2 != 0), -1.0, 1.0)
        return jnp.where(turns * length == n, sign, 0.0)

    for m in range(slots):
        mine = entry(metas[0], m)
        near = response(mine - others)
        far = response(mine + others)
        gram_ref[m] = factor * (near + jnp.where(cosine, far, -far))


def table_copies(legendre, tables, sems):
    slots, _, _, degrees = tables.shape
    copies = []
    for m in range(slots):
        first = m * (degrees // slots)
        part = (m, slice(None), slice(None), pl.ds(first, degrees - first))
        copies.append(pltpu.make_async_copy(legendre.at[part], tables.at[part], sems.at[m]))
    return copies


def use_tile(tables, m, span, keep, coefs, p, n):
    plus = tables[m, 0, :, span]
    minus = tables[m, 1, :, span]
    if keep is not None:
        plus = jnp.where(keep, plus, 0.0)
        minus = jnp.where(keep, minus, 0.0)
    for a in range(4):
        c = coefs(a)
        p[a] = p[a] + plus * c
        n[a] = n[a] + minus * c


def fold_lanes(values, lane):
    step = 1
    while step < LANES:
        if len(values) > 1:
            low = (lane & step) == 0
            values = [
                jnp.where(low, values[i], values[i + 1])
                + pltpu.roll(jnp.where(low, values[i + 1], values[i]), step, 1)
                for i in range(0, len(values), 2)
            ]
        else:
            values = [values[0] + pltpu.roll(values[0], step, 1)]
        step *= 2
    return values[0]


def combine(p, n):
    return [n[3] - p[0], -p[1] - n[2], -p[2] - n[1], n[0] - p[3]]


def tables_kernel(legendre, tables, sems):
    copies = table_copies(legendre, tables, sems)
    for copy in copies:
        copy.start()
    for copy in copies:
        copy.wait()


def forward_kernel(steps, firsts, meta_ref, tables, *rest):
    parts = rest[: len(steps)]
    sums_ref, coefs = rest[len(steps) :]
    slots, _, count, degrees = tables.shape
    width = parts[0].shape[2]
    blocks = degrees // width
    stratum = degrees // slots
    meta = meta_ref[...]
    place = ring_place(lax.axis_index("blk"), blocks)
    for part, step, low in zip(parts, steps, firsts):
        first = pl.multiple_of(block_at(place + step, blocks) * width, LANES)
        for m in range(part.shape[0]):
            coefs[low + m, :, pl.ds(first, width)] = part[m]
    first = pl.multiple_of(block_at(place + blocks // 2, blocks) * width, LANES)
    for m in range(slots):
        coefs[m, :, pl.ds(first, width)] = jnp.zeros((4, width), jnp.float32)
    lane = lax.broadcasted_iota(jnp.int32, (count, LANES), 1)
    for m in range(slots):
        floor = jnp.maximum(entry(meta, m).astype(jnp.int32), 2)
        p = [jnp.zeros((count, LANES), jnp.float32)] * 4
        n = [jnp.zeros((count, LANES), jnp.float32)] * 4
        for t in range(stratum * m // LANES, degrees // LANES):
            span = slice(t * LANES, (t + 1) * LANES)
            keep = lane >= floor - t * LANES if t * LANES < stratum * (m + 1) else None
            use_tile(tables, m, span, keep, lambda a: coefs[m, a : a + 1, span], p, n)
        for a, total in enumerate(combine(p, n)):
            sums_ref[m, a] = total


def phases_kernel(groups, meta_ref, tables, pieces_ref, sums_ref, low_ref, high_ref, *rest):
    phases_ref, *messages = rest
    slots, _, count, degrees = tables.shape
    middle, _, width = low_ref.shape
    blocks = degrees // width
    meta = meta_ref[...]
    place = ring_place(lax.axis_index("blk"), blocks)
    first = pl.multiple_of(block_at(place + blocks // 2, blocks) * width, LANES)
    lane = lax.broadcasted_iota(jnp.int32, (count, LANES), 1)
    totals = [None] * (4 * slots)
    for m in range(slots):
        floor = jnp.maximum(entry(meta, m).astype(jnp.int32), 2) - first
        part, at = (low_ref, m) if m < middle else (high_ref, m - middle)
        p = [jnp.zeros((count, LANES), jnp.float32)] * 4
        n = [jnp.zeros((count, LANES), jnp.float32)] * 4
        for t in range(width // LANES):
            here = slice(t * LANES, (t + 1) * LANES)
            keep = lane >= floor - t * LANES
            span = pl.ds(first + t * LANES, LANES)
            use_tile(tables, m, span, keep, lambda a: part[at, a : a + 1, here], p, n)
        for a, total in enumerate(combine(p, n)):
            totals[a * slots + m] = total + sums_ref[m, a]
    phases = fold_lanes(totals, lane)
    phases_ref[...] = phases
    for d in range(1, groups):
        messages[d - 1][:count] = phases
        messages[d - 1][count:] = pieces_ref[d]


def fold_rows(values, row):
    for step in (1, 2, 4):
        low = (row & step) == 0
        values = [
            jnp.where(low, values[i], values[i + 1])
            + pltpu.roll(jnp.where(low, values[i + 1], values[i]), step, 0)
            for i in range(0, len(values), 2)
        ]
    return values[0]


def update_tiles(tables, m, spans, an, ng, row8):
    count = tables.shape[2]
    values = []
    for span in spans:
        plus = tables[m, 0, :, span]
        minus = tables[m, 1, :, span]
        four = [
            plus * ng[0] + minus * an[3],
            plus * ng[1] + minus * ng[2],
            plus * ng[2] + minus * ng[1],
            plus * ng[3] + minus * an[0],
        ]
        values += [sum(v[8 * k : 8 * k + 8] for k in range(count // 8)) for v in four]
    return fold_rows(values, row8)


def update_block(tables, m, first, an, ng, row8, out, at):
    for t in range(0, out.shape[2] // LANES, 2):
        spans = [pl.ds(first + u * LANES, LANES) for u in (t, t + 1)]
        folded = update_tiles(tables, m, spans, an, ng, row8)
        for k, u in enumerate((t, t + 1)):
            out[at, :, u * LANES : (u + 1) * LANES] = folded[4 * k : 4 * k + 4]


def analysed_kernel(groups, cycles, tables, gram_ref, pieces_ref, phases_ref, *rest):
    messages = rest[: groups - 1]
    *sends, analysed_ref, sky = rest[groups - 1 :]
    slots, _, count, degrees = tables.shape
    middle, _, width = sends[0].shape
    blocks = degrees // width
    far = blocks // 2
    place = ring_place(lax.axis_index("blk"), blocks)
    first = pl.multiple_of(block_at(place + far, blocks) * width, LANES)
    owner = lax.axis_index("order")
    wide = 4 * slots
    pairs = []
    for d in range(groups):
        phases = phases_ref[...] if d == 0 else messages[d - 1][:count]
        piece = pieces_ref[0] if d == 0 else messages[d - 1][count:]
        sky[pl.ds((owner ^ d) * cycles, cycles)] = piece[:cycles]
        pairs.append(phases)
    lane = lax.broadcasted_iota(jnp.int32, (count, LANES), 1)
    row8 = lax.broadcasted_iota(jnp.int32, (8, LANES), 0)
    per = LANES // wide
    packed = []
    for start in range(0, groups, per):
        value = pairs[start]
        for k in range(1, per):
            value = jnp.where(
                lane // wide == k, pltpu.roll(pairs[start + k], k * wide, 1), value
            )
        packed.append(value)
    observed = sky[:count]
    for m in range(slots):
        total = jnp.where((lane < wide) & (lane % slots == m), observed, 0.0)
        for k, value in enumerate(packed):
            total = total - gram_ref[m, :, k * LANES : (k + 1) * LANES] * value
        an = []
        for a in range(4):
            value = jnp.where((lane % wide) // slots == a, total, 0.0)
            value = jnp.sum(value, axis=1, keepdims=True)
            an.append(jnp.broadcast_to(value, (count, LANES)))
            analysed_ref[m, a] = an[a]
        ng = [-value for value in an]
        half, at = divmod(m, middle)
        update_block(tables, m, first, an, ng, row8, sends[half], at)


def second_kernel(ways, tables, analysed_ref, low_ref, high_ref):
    slots, _, _, degrees = tables.shape
    middle, _, width = low_ref.shape
    blocks = degrees // width
    place = ring_place(lax.axis_index("blk"), blocks)
    row8 = lax.broadcasted_iota(jnp.int32, (8, LANES), 0)
    for m in range(slots):
        half, at = divmod(m, middle)
        step = ways[half] * (blocks // 2 - 1)
        first = pl.multiple_of(block_at(place + step, blocks) * width, LANES)
        an = [analysed_ref[m, a] for a in range(4)]
        ng = [-value for value in an]
        update_block(tables, m, first, an, ng, row8, (low_ref, high_ref)[half], at)


def backward_kernel(tables, analysed_ref, out):
    slots, _, _, degrees = tables.shape
    blocks, _, _, width = out.shape
    stratum = degrees // slots
    place = ring_place(lax.axis_index("blk"), blocks)
    ring = ring_of(blocks)
    step_of = [lax.rem(ring.index(b) - place + blocks, blocks) for b in range(blocks)]
    row8 = lax.broadcasted_iota(jnp.int32, (8, LANES), 0)
    for m in range(slots):
        an = [analysed_ref[m, a] for a in range(4)]
        ng = [-value for value in an]
        for t in range(stratum * m // LANES, degrees // LANES, 2):
            spans = [slice(u * LANES, (u + 1) * LANES) for u in (t, t + 1)]
            folded = update_tiles(tables, m, spans, an, ng, row8)
            for k, u in enumerate((t, t + 1)):
                inner = u * LANES % width
                out[step_of[u * LANES // width], m, :, inner : inner + LANES] = folded[
                    4 * k : 4 * k + 4
                ]


def residual_kernel(groups, slots, cycles, *rest):
    metas = [ref[...] for ref in rest[:groups]]
    section_ref, acs_ref, asc_ref, fine_ref, phases_ref = rest[groups : groups + 5]
    messages = rest[groups + 5 : 2 * groups + 4]
    out_ref, spread = rest[2 * groups + 4 :]
    owner = lax.axis_index("order")
    rows, both = acs_ref.shape[1:]
    every = both // 2
    count = phases_ref.shape[0]
    lane = lax.broadcasted_iota(jnp.int32, (count, LANES), 1)
    ids = spread_ids(metas, slots, [d for _ in range(2) for d in range(groups)])
    factor = jnp.where(ids == 0.0, 1.0, 2.0)
    per = LANES // slots
    values = [phases_ref[...]] + [ref[:count] for ref in messages]
    for a in range(4):
        tiles = []
        for start in range(0, 2 * groups, per):
            tile = jnp.zeros((count, LANES), jnp.float32)
            for k in range(per):
                shift = (k - a) * slots % LANES
                value = values[(start + k) % groups]
                value = pltpu.roll(value, shift, 1) if shift else value
                tile = jnp.where(lane // slots == k, value, tile)
            tiles.append(tile)
        spread[a, :count] = jnp.concatenate(tiles, axis=1) * factor
    even = lax.broadcasted_iota(jnp.int32, (rows, both), 0) % 2 == 0
    for c in range(cycles):
        q_re, q_im, u_re, u_im = [spread[a, pl.ds(owner * cycles + c, 1)] for a in range(4)]
        weights = jnp.where(even, q_re, u_re) * acs_ref[c]
        weights = weights - jnp.where(even, q_im, u_im) * asc_ref[c]
        model = lax.dot_general(
            weights, fine_ref[c], (((1,), (1,)), ((), ())), precision=HIGHEST,
            preferred_element_type=jnp.float32,
        )
        inside = pixel_mask((rows, LANES), entry(metas[0], slots + c).astype(jnp.int32))
        out_ref[c] = section_ref[c] - jnp.where(inside, model, 0.0)


def join_kernel(own_ref, value_ref, out_ref):
    out_ref[...] = own_ref[...] + value_ref[...]


def add_kernel(index, first, piece_ref, value_ref, out_ref):
    out_ref[...] = piece_ref[index, first : first + out_ref.shape[0]] + value_ref[...]


def final_kernel(meta_ref, harmonics_ref, piece_ref, *rest):
    *received, out_ref = rest
    slots, parts, width = out_ref.shape
    middle = slots // 2
    start = lax.axis_index("blk") * width
    degree = start + lax.broadcasted_iota(jnp.int32, (parts, width), 1)
    meta = meta_ref[...]
    for m in range(slots):
        h, at = divmod(m, middle)
        update = piece_ref[0, m] + (received[h][at] + received[2 + h][at])
        valid = degree >= jnp.maximum(entry(meta, m).astype(jnp.int32), 2)
        out_ref[m] = jnp.where(valid, harmonics_ref[m] + update, 0.0)


def vmem():
    return pl.BlockSpec(memory_space=VMEM)


def shape(*dims):
    return jax.ShapeDtypeStruct(dims, jnp.float32)


def body(harmonics, legendre, sky_map, cycle_length, cycle_offset, cycle_weight, order_ids):
    groups = lax.axis_size("order")
    blocks = lax.axis_size("blk")
    slots, _, width = harmonics.shape
    count, degrees = legendre.shape[2:]
    cycles, _, pixels = sky_map.shape
    rows = pixels // LANES
    every = slots * groups
    normalise = math.sqrt(degrees * every / (cycles * groups * blocks * pixels))

    def swap(value, axis, step):
        size = lax.axis_size(axis)
        return lax.ppermute(value, axis, [(i, i ^ step) for i in range(size)])

    ring = ring_of(blocks)

    def turn(value, way):
        pairs = [(ring[p], ring[(p + way) % blocks]) for p in range(blocks)]
        return lax.ppermute(value, "blk", pairs)

    def estimate(micros):
        return pl.CostEstimate(flops=0, bytes_accessed=int(micros * 3.0e6), transcendentals=0)

    hbm = pl.BlockSpec(memory_space=pl.ANY)
    small = (order_ids, cycle_length, cycle_offset, cycle_weight)
    meta = pl.pallas_call(
        lambda *refs: meta_kernel(slots, cycles, *refs),
        out_shape=pltpu.VMEM((1, LANES), jnp.float32),
        in_specs=[hbm] * 4,
        out_specs=vmem(),
        scratch_shapes=[pltpu.SMEM(v.shape, v.dtype) for v in small]
        + [pltpu.SemaphoreType.DMA((len(small),))],
        compiler_params=pltpu.CompilerParams(vmem_limit_bytes=2 * MIB),
        name="meta",
    )(*[pltpu.with_memory_space_constraint(v, pltpu.HBM) for v in small])
    metas = [meta] + [swap(meta, "order", d) for d in range(1, groups)]

    far = blocks // 2
    middle = slots // 2
    ahead, behind = turn(harmonics, 1), turn(harmonics, -1)
    parts, steps, firsts = [harmonics, ahead, behind], [0, -1, 1], [0, 0, 0]
    tables = pl.pallas_call(
        tables_kernel,
        out_shape=pltpu.VMEM(legendre.shape, jnp.float32),
        in_specs=[hbm],
        out_specs=hbm,
        scratch_shapes=[pltpu.SemaphoreType.DMA((slots,))],
        compiler_params=pltpu.CompilerParams(vmem_limit_bytes=2 * MIB),
        cost_estimate=estimate(1.5),
        name="tables",
    )(pltpu.with_memory_space_constraint(legendre, pltpu.HBM))
    ahead, tables, *metas = lax.optimization_barrier((ahead, tables, *metas))
    ahead = [ahead[:middle], ahead[middle:]]
    behind = [behind[:middle], behind[middle:]]

    sky = sky_map.reshape(cycles, 2, rows, LANES).transpose(0, 2, 1, 3)
    sky = sky.reshape(cycles, 2 * rows, LANES)
    pieces, acs, asc, fine, section = pl.pallas_call(
        lambda *refs: sky_kernel(normalise, groups, slots, cycles, *refs),
        out_shape=(
            shape(groups, 8, LANES),
            shape(cycles, 2 * rows, 2 * every),
            shape(cycles, 2 * rows, 2 * every),
            shape(cycles, LANES, 2 * every),
            shape(cycles, 2 * rows, LANES),
        ),
        in_specs=[vmem()] * groups + [hbm],
        out_specs=(vmem(),) * 5,
        scratch_shapes=[
            pltpu.VMEM((cycles, 2 * rows, LANES), jnp.float32),
            pltpu.SemaphoreType.DMA,
        ],
        compiler_params=pltpu.CompilerParams(vmem_limit_bytes=16 * MIB),
        cost_estimate=estimate(3),
        name="sky_analysis",
    )(*metas, pltpu.with_memory_space_constraint(sky, pltpu.HBM))
    gram = pl.pallas_call(
        lambda *refs: gram_kernel(normalise, groups, slots, cycles, *refs),
        out_shape=shape(slots, count, 4 * every),
        in_specs=[vmem()] * groups,
        out_specs=vmem(),
        compiler_params=pltpu.CompilerParams(vmem_limit_bytes=8 * MIB),
        cost_estimate=estimate(1),
        name="response",
    )(*metas)

    for k in range(2, far):
        ahead = [turn(value, 1) for value in ahead]
        behind = [turn(value, -1) for value in behind[::-1]][::-1]
        parts += ahead + behind
        steps += [-k, -k, k, k]
        firsts += [0, middle] * 2
        if k == 2:
            ahead[0], pieces = lax.optimization_barrier((ahead[0], pieces))
    ends = [turn(ahead[0], 1), turn(behind[1], -1)]

    whole = pltpu.VMEM((slots, 4, count, LANES), jnp.float32)
    sums = pl.pallas_call(
        lambda *refs: forward_kernel(steps, firsts, *refs),
        out_shape=whole,
        in_specs=[vmem()] * (2 + len(parts)),
        out_specs=vmem(),
        scratch_shapes=[pltpu.VMEM((slots, 4, degrees), jnp.float32)],
        compiler_params=pltpu.CompilerParams(vmem_limit_bytes=24 * MIB),
        cost_estimate=estimate(2),
        name="forward",
    )(meta, tables, *parts)
    phases, *outs = pl.pallas_call(
        lambda *refs: phases_kernel(groups, *refs),
        out_shape=[shape(count, LANES)] + [shape(count + 8, LANES)] * (groups - 1),
        in_specs=[vmem()] * 6,
        out_specs=[vmem()] * groups,
        compiler_params=pltpu.CompilerParams(vmem_limit_bytes=16 * MIB),
        cost_estimate=estimate(1),
        name="phases",
    )(meta, tables, pieces, sums, *ends)
    messages = [swap(outs[d - 1], "order", d) for d in range(1, groups)]

    half = pltpu.VMEM((middle, 4, width), jnp.float32)
    *sends, analysed = pl.pallas_call(
        lambda *refs: analysed_kernel(groups, cycles, *refs),
        out_shape=[half] * 2 + [whole],
        in_specs=[vmem()] * (3 + groups),
        out_specs=[vmem()] * 3,
        scratch_shapes=[pltpu.VMEM((count + 8, LANES), jnp.float32)],
        compiler_params=pltpu.CompilerParams(vmem_limit_bytes=16 * MIB),
        cost_estimate=estimate(1),
        name="analysed",
    )(tables, gram, pieces, phases, *messages)
    def nearer(ways):
        return pl.pallas_call(
            lambda *refs: second_kernel(ways, *refs),
            out_shape=[half] * 2,
            in_specs=[vmem()] * 2,
            out_specs=[vmem()] * 2,
            compiler_params=pltpu.CompilerParams(vmem_limit_bytes=16 * MIB),
            cost_estimate=estimate(0.01),
            name="second",
        )(tables, analysed)

    second = nearer((-1, 1))
    third = nearer((1, -1))

    piece = pl.pallas_call(
        backward_kernel,
        out_shape=pltpu.VMEM((blocks, slots, 4, width), jnp.float32),
        in_specs=[vmem()] * 2,
        out_specs=vmem(),
        compiler_params=pltpu.CompilerParams(vmem_limit_bytes=16 * MIB),
        cost_estimate=estimate(2),
        name="backward",
    )(tables, analysed)

    def add(index, first, value):
        return pl.pallas_call(
            lambda *refs: add_kernel(index, first, *refs),
            out_shape=half,
            in_specs=[vmem()] * 2,
            out_specs=vmem(),
            compiler_params=pltpu.CompilerParams(vmem_limit_bytes=4 * MIB),
            cost_estimate=estimate(0.1),
            name="add",
        )(piece, pltpu.with_memory_space_constraint(value, pltpu.VMEM))

    sent = dict(zip(((1, 0), (-1, middle), (-1, 0), (1, middle)), (*sends, *second)))
    first_hop = {key: turn(sent[key], key[0]) for key in ((1, 0), (-1, middle))}
    for key, own in zip(((1, 0), (-1, middle)), third):
        sent[key] = pl.pallas_call(
            join_kernel,
            out_shape=half,
            in_specs=[vmem()] * 2,
            out_specs=vmem(),
            compiler_params=pltpu.CompilerParams(vmem_limit_bytes=4 * MIB),
            cost_estimate=estimate(0.1),
            name="join",
        )(own, pltpu.with_memory_space_constraint(first_hop[key], pltpu.VMEM))
    for k in reversed(range(1, far)):
        for key in ((1, middle), (-1, 0), (1, 0), (-1, middle)):
            sent[key] = turn(sent[key], key[0])
            if k > 1:
                sent[key] = add((key[0] * (k - 1)) % blocks, key[1], sent[key])
    received = [sent[key] for key in ((1, 0), (1, middle), (-1, 0), (-1, middle))]
    refined = pl.pallas_call(
        final_kernel,
        out_shape=shape(*harmonics.shape),
        in_specs=[vmem()] * 7,
        out_specs=vmem(),
        compiler_params=pltpu.CompilerParams(vmem_limit_bytes=8 * MIB),
        cost_estimate=pl.CostEstimate(flops=10**5, bytes_accessed=10**6, transcendentals=0),
        name="refine",
    )(
        meta, harmonics, piece,
        *[pltpu.with_memory_space_constraint(value, pltpu.VMEM) for value in received],
    )

    residual = pl.pallas_call(
        lambda *refs: residual_kernel(groups, slots, cycles, *refs),
        out_shape=shape(cycles, 2 * rows, LANES),
        in_specs=[vmem()] * (4 + 2 * groups),
        out_specs=vmem(),
        scratch_shapes=[pltpu.VMEM((4, count + 8, 2 * every), jnp.float32)],
        compiler_params=pltpu.CompilerParams(vmem_limit_bytes=16 * MIB),
        cost_estimate=pl.CostEstimate(flops=10**8, bytes_accessed=2 * MIB, transcendentals=0),
        name="residual",
    )(*metas, section, acs, asc, fine, phases, *messages)
    residual = residual.reshape(cycles, rows, 2, LANES).transpose(0, 2, 1, 3)
    return (refined, residual.reshape(sky_map.shape))


def solution(mesh):
    return jax.shard_map(
        body,
        mesh=mesh,
        in_specs=(
            P("order", None, "blk"),
            P("order", None, "blk", None),
            P(("blk", "order"), None, None),
            P(("blk", "order")),
            P(("blk", "order")),
            P(("blk", "order")),
            P("order"),
        ),
        out_specs=(P("order", None, "blk"), P(("blk", "order"), None, None)),
        check_vma=False,
    )
```

```python
import math

import jax
import jax.numpy as jnp
from jax import lax
from jax.experimental import pallas as pl
from jax.experimental.pallas import tpu as pltpu
from jax.sharding import PartitionSpec as P

HIGHEST = lax.Precision.HIGHEST
LANES = 128
VMEM = pltpu.VMEM
MIB = 1024 * 1024


def ring_of(blocks):
    return list(range(0, blocks, 2)) + list(range(blocks - 1, 0, -2))


def ring_place(block, blocks):
    return jnp.where(block % 2 == 0, block // 2, blocks - 1 - block // 2)


def block_at(place, blocks):
    place = lax.rem(place + 2 * blocks, blocks)
    return jnp.where(place < blocks // 2, 2 * place, 2 * (blocks - 1 - place) + 1)


def sin_pi(x):
    turns = jnp.round(x)
    y = (x - turns) * math.pi
    z = y * y
    value = -1.0 / 39916800
    for term in (1.0 / 362880, -1.0 / 5040, 1.0 / 120, -1.0 / 6, 1.0):
        value = value * z + term
    value = value * y
    return jnp.where(turns.astype(jnp.int32) % 2 != 0, -value, value)


def half_turns(order, step, length):
    total = order * step
    period = 2 * length
    scale = 0.5 / length.astype(jnp.float32)
    for _ in range(2):
        total = total - jnp.floor(total.astype(jnp.float32) * scale).astype(jnp.int32) * period
    return total.astype(jnp.float32) / length.astype(jnp.float32)


def pixel_mask(shape, length):
    pixel = lax.broadcasted_iota(jnp.int32, shape, 0) // 2 * shape[1]
    pixel = pixel + lax.broadcasted_iota(jnp.int32, shape, 1)
    return pixel < length


def meta_kernel(slots, cycles, ids, length, offset, weight, out_ref, *scratch):
    *held, sems = scratch
    copies = [
        pltpu.make_async_copy(source, target, sems.at[k])
        for k, (source, target) in enumerate(zip((ids, length, offset, weight), held))
    ]
    for copy in copies:
        copy.start()
    for copy in copies:
        copy.wait()
    lane = lax.broadcasted_iota(jnp.int32, (1, LANES), 1)
    out = jnp.zeros((1, LANES), jnp.float32)
    for m in range(slots):
        out = jnp.where(lane == m, held[0][m].astype(jnp.float32), out)
    for c in range(cycles):
        for k in range(3):
            value = held[1 + k][c].astype(jnp.float32)
            out = jnp.where(lane == slots + k * cycles + c, value, out)
    out_ref[...] = out


def entry(meta, at):
    return meta[:, at : at + 1]


def spread_ids(metas, slots, sources):
    per = LANES // slots
    lane = lax.broadcasted_iota(jnp.int32, (1, LANES), 1)
    pieces = []
    for start in range(0, len(sources), per):
        piece = jnp.zeros((1, LANES), jnp.float32)
        for k in range(per):
            value = metas[sources[start + k]]
            value = pltpu.roll(value, k * slots, 1) if k else value
            piece = jnp.where(lane // slots == k, value, piece)
        pieces.append(piece)
    return jnp.concatenate(pieces, axis=1)


def sky_kernel(normalise, groups, slots, cycles, *rest):
    metas = [ref[...] for ref in rest[:groups]]
    sky_hbm, pieces_ref, acs_ref, asc_ref, fine_ref, section_ref, sky_ref, sky_sem = rest[groups:]
    sky_copy = pltpu.make_async_copy(sky_hbm, sky_ref, sky_sem)
    sky_copy.start()
    rows, both = acs_ref.shape[1:]
    every = both // 2
    ids = spread_ids(metas, slots, [d for _ in range(2) for d in range(groups)])
    ids = ids.astype(jnp.int32)
    row8 = lax.broadcasted_iota(jnp.int32, (8, both), 0)
    sums = [jnp.zeros((8, both), jnp.float32) for _ in range(4)]
    for c in range(cycles):
        length = entry(metas[0], slots + c).astype(jnp.int32)
        offset = entry(metas[0], slots + cycles + c).astype(jnp.int32)
        coarse = lax.broadcasted_iota(jnp.int32, (rows, both), 0) // 2 * (2 * LANES) + offset
        x = half_turns(ids, coarse, length)
        first = lax.broadcasted_iota(jnp.int32, (rows, both), 1) < every
        acs = sin_pi(x + jnp.where(first, 0.5, 1.0))
        asc = sin_pi(x + jnp.where(first, 0.0, 0.5))
        acs_ref[c] = acs
        asc_ref[c] = asc
        fine = 2 * lax.broadcasted_iota(jnp.int32, (LANES, both), 0)
        x = half_turns(ids, fine, length)
        first = lax.broadcasted_iota(jnp.int32, (LANES, both), 1) < every
        table = sin_pi(x + jnp.where(first, 0.5, 0.0))
        fine_ref[c] = table
        if c == 0:
            sky_copy.wait()
        section = jnp.where(pixel_mask((rows, LANES), length), sky_ref[c], 0.0)
        section_ref[c] = section
        spun = jnp.dot(section, table, precision=HIGHEST, preferred_element_type=jnp.float32)
        weight = entry(metas[0], slots + 2 * cycles + c) * normalise
        for k, value in enumerate((spun * acs, spun * asc)):
            value = sum(value[8 * i : 8 * i + 8] for i in range(rows // 8))
            for q in range(2):
                total = jnp.sum(jnp.where(row8 % 2 == q, value, 0.0), axis=0, keepdims=True)
                total = total * (-weight if k else weight)
                sums[2 * q + k] = jnp.where(row8 == c, total, sums[2 * q + k])
    lane = lax.broadcasted_iota(jnp.int32, (8, LANES), 1)
    totals = []
    for value in sums:
        tiles = [value[:, i : i + LANES] for i in range(0, both, LANES)]
        if every < LANES:
            shift = every
            while shift < LANES:
                tiles[0] = tiles[0] + pltpu.roll(tiles[0], shift, 1)
                shift *= 2
            totals.append(tiles)
        else:
            half = len(tiles) // 2
            totals.append([tiles[i] + tiles[half + i] for i in range(half)])
    for d in range(groups):
        piece = jnp.zeros((8, LANES), jnp.float32)
        tile, at = divmod(d * slots, LANES)
        for a in range(4):
            shift = (a * slots - at) % LANES
            value = totals[a][tile]
            value = pltpu.roll(value, shift, 1) if shift else value
            piece = jnp.where(lane // slots == a, value, piece)
        pieces_ref[d] = piece


def gram_kernel(normalise, groups, slots, cycles, *rest):
    metas = [ref[...] for ref in rest[:groups]]
    (gram_ref,) = rest[groups:]
    me = lax.axis_index("order")
    count, wide = gram_ref.shape[1:]
    row = lax.broadcasted_iota(jnp.int32, (count, wide), 0)
    length = jnp.ones((count, wide), jnp.float32)
    offset = jnp.zeros((count, wide), jnp.float32)
    weight = jnp.zeros((count, wide), jnp.float32)
    for d in range(groups):
        for c in range(cycles):
            here = row == (me ^ d) * cycles + c
            length = jnp.where(here, entry(metas[d], slots + c), length)
            offset = jnp.where(here, entry(metas[d], slots + cycles + c), offset)
            weight = jnp.where(here, entry(metas[d], slots + 2 * cycles + c), weight)
    others = spread_ids(metas, slots, [d for d in range(groups) for _ in range(4)])
    lane = lax.broadcasted_iota(jnp.int32, (count, wide), 1)
    cosine = (lane // slots) % 2 == 0
    factor = jnp.where(others == 0.0, 0.5, 1.0) * normalise * weight * length
    inverse = 1.0 / length
    odd = offset > 0.5

    def response(n):
        turns = jnp.round(n * inverse)
        sign = jnp.where(odd & (turns.astype(jnp.int32) % 2 != 0), -1.0, 1.0)
        return jnp.where(turns * length == n, sign, 0.0)

    for m in range(slots):
        mine = entry(metas[0], m)
        near = response(mine - others)
        far = response(mine + others)
        gram_ref[m] = factor * (near + jnp.where(cosine, far, -far))


def table_copies(legendre, tables, sems):
    slots, _, _, degrees = tables.shape
    copies = []
    for m in range(slots):
        first = m * (degrees // slots)
        part = (m, slice(None), slice(None), pl.ds(first, degrees - first))
        copies.append(pltpu.make_async_copy(legendre.at[part], tables.at[part], sems.at[m]))
    return copies


def use_tile(tables, m, span, keep, coefs, p, n):
    plus = tables[m, 0, :, span]
    minus = tables[m, 1, :, span]
    if keep is not None:
        plus = jnp.where(keep, plus, 0.0)
        minus = jnp.where(keep, minus, 0.0)
    for a in range(4):
        c = coefs(a)
        p[a] = p[a] + plus * c
        n[a] = n[a] + minus * c


def fold_lanes(values, lane):
    step = 1
    while step < LANES:
        if len(values) > 1:
            low = (lane & step) == 0
            values = [
                jnp.where(low, values[i], values[i + 1])
                + pltpu.roll(jnp.where(low, values[i + 1], values[i]), step, 1)
                for i in range(0, len(values), 2)
            ]
        else:
            values = [values[0] + pltpu.roll(values[0], step, 1)]
        step *= 2
    return values[0]


def combine(p, n):
    return [n[3] - p[0], -p[1] - n[2], -p[2] - n[1], n[0] - p[3]]


def on_core(core):
    return lax.axis_index("order") % 2 == core


def tables_kernel(legendre, tables, sems):
    copies = table_copies(legendre, tables, sems)
    for copy in copies:
        copy.start()
    for copy in copies:
        copy.wait()


def forward_kernel(steps, firsts, meta_ref, tables, *rest):
    parts = rest[: len(steps)]
    sums_ref, coefs = rest[len(steps) :]
    slots, _, count, degrees = tables.shape
    width = parts[0].shape[2]
    blocks = degrees // width
    stratum = degrees // slots
    meta = meta_ref[...]
    place = ring_place(lax.axis_index("blk"), blocks)
    for part, step, low in zip(parts, steps, firsts):
        first = pl.multiple_of(block_at(place + step, blocks) * width, LANES)
        for m in range(part.shape[0]):
            coefs[low + m, :, pl.ds(first, width)] = part[m]
    first = pl.multiple_of(block_at(place + blocks // 2, blocks) * width, LANES)
    for m in range(slots):
        coefs[m, :, pl.ds(first, width)] = jnp.zeros((4, width), jnp.float32)
    lane = lax.broadcasted_iota(jnp.int32, (count, LANES), 1)
    for m in range(slots):
        floor = jnp.maximum(entry(meta, m).astype(jnp.int32), 2)
        p = [jnp.zeros((count, LANES), jnp.float32)] * 4
        n = [jnp.zeros((count, LANES), jnp.float32)] * 4
        for t in range(stratum * m // LANES, degrees // LANES):
            span = slice(t * LANES, (t + 1) * LANES)
            keep = lane >= floor - t * LANES if t * LANES < stratum * (m + 1) else None
            use_tile(tables, m, span, keep, lambda a: coefs[m, a : a + 1, span], p, n)
        for a, total in enumerate(combine(p, n)):
            sums_ref[m, a] = total


def phases_kernel(groups, meta_ref, tables, pieces_ref, sums_ref, low_ref, high_ref, *rest):
    phases_ref, *messages = rest
    slots, _, count, degrees = tables.shape
    middle, _, width = low_ref.shape
    blocks = degrees // width
    meta = meta_ref[...]
    place = ring_place(lax.axis_index("blk"), blocks)
    first = pl.multiple_of(block_at(place + blocks // 2, blocks) * width, LANES)
    lane = lax.broadcasted_iota(jnp.int32, (count, LANES), 1)
    totals = [None] * (4 * slots)
    for m in range(slots):
        floor = jnp.maximum(entry(meta, m).astype(jnp.int32), 2) - first
        part, at = (low_ref, m) if m < middle else (high_ref, m - middle)
        p = [jnp.zeros((count, LANES), jnp.float32)] * 4
        n = [jnp.zeros((count, LANES), jnp.float32)] * 4
        for t in range(width // LANES):
            here = slice(t * LANES, (t + 1) * LANES)
            keep = lane >= floor - t * LANES
            span = pl.ds(first + t * LANES, LANES)
            use_tile(tables, m, span, keep, lambda a: part[at, a : a + 1, here], p, n)
        for a, total in enumerate(combine(p, n)):
            totals[a * slots + m] = total + sums_ref[m, a]
    phases = fold_lanes(totals, lane)
    phases_ref[...] = phases
    for d in range(1, groups):
        messages[d - 1][:count] = phases
        messages[d - 1][count:] = pieces_ref[d]


def fold_rows(values, row):
    for step in (1, 2, 4):
        low = (row & step) == 0
        values = [
            jnp.where(low, values[i], values[i + 1])
            + pltpu.roll(jnp.where(low, values[i + 1], values[i]), step, 0)
            for i in range(0, len(values), 2)
        ]
    return values[0]


def update_tiles(tables, m, spans, an, ng, row8):
    count = tables.shape[2]
    values = []
    for span in spans:
        plus = tables[m, 0, :, span]
        minus = tables[m, 1, :, span]
        four = [
            plus * ng[0] + minus * an[3],
            plus * ng[1] + minus * ng[2],
            plus * ng[2] + minus * ng[1],
            plus * ng[3] + minus * an[0],
        ]
        values += [sum(v[8 * k : 8 * k + 8] for k in range(count // 8)) for v in four]
    return fold_rows(values, row8)


def update_block(tables, m, first, an, ng, row8, out, at):
    for t in range(0, out.shape[2] // LANES, 2):
        spans = [pl.ds(first + u * LANES, LANES) for u in (t, t + 1)]
        folded = update_tiles(tables, m, spans, an, ng, row8)
        for k, u in enumerate((t, t + 1)):
            out[at, :, u * LANES : (u + 1) * LANES] = folded[4 * k : 4 * k + 4]


def analysed_kernel(groups, cycles, tables, gram_ref, pieces_ref, phases_ref, *rest):
    messages = rest[: groups - 1]
    *sends, analysed_ref, sky = rest[groups - 1 :]
    slots, _, count, degrees = tables.shape
    middle, _, width = sends[0].shape
    blocks = degrees // width
    far = blocks // 2
    place = ring_place(lax.axis_index("blk"), blocks)
    first = pl.multiple_of(block_at(place + far, blocks) * width, LANES)
    owner = lax.axis_index("order")
    wide = 4 * slots
    pairs = []
    for d in range(groups):
        phases = phases_ref[...] if d == 0 else messages[d - 1][:count]
        piece = pieces_ref[0] if d == 0 else messages[d - 1][count:]
        sky[pl.ds((owner ^ d) * cycles, cycles)] = piece[:cycles]
        pairs.append(phases)
    lane = lax.broadcasted_iota(jnp.int32, (count, LANES), 1)
    row8 = lax.broadcasted_iota(jnp.int32, (8, LANES), 0)
    per = LANES // wide
    packed = []
    for start in range(0, groups, per):
        value = pairs[start]
        for k in range(1, per):
            value = jnp.where(
                lane // wide == k, pltpu.roll(pairs[start + k], k * wide, 1), value
            )
        packed.append(value)
    observed = sky[...]
    for m in range(slots):
        total = jnp.where((lane < wide) & (lane % slots == m), observed, 0.0)
        for k, value in enumerate(packed):
            total = total - gram_ref[m, :, k * LANES : (k + 1) * LANES] * value
        an = []
        for a in range(4):
            value = jnp.where((lane % wide) // slots == a, total, 0.0)
            value = jnp.sum(value, axis=1, keepdims=True)
            an.append(jnp.broadcast_to(value, (count, LANES)))
            analysed_ref[m, a] = an[a]
        ng = [-value for value in an]
        half, at = divmod(m, middle)
        update_block(tables, m, first, an, ng, row8, sends[half], at)


def second_kernel(ways, tables, analysed_ref, low_ref, high_ref):
    slots, _, _, degrees = tables.shape
    middle, _, width = low_ref.shape
    blocks = degrees // width
    place = ring_place(lax.axis_index("blk"), blocks)
    row8 = lax.broadcasted_iota(jnp.int32, (8, LANES), 0)
    for m in range(slots):
        half, at = divmod(m, middle)
        step = ways[half] * (blocks // 2 - 1)
        first = pl.multiple_of(block_at(place + step, blocks) * width, LANES)
        an = [analysed_ref[m, a] for a in range(4)]
        ng = [-value for value in an]
        update_block(tables, m, first, an, ng, row8, (low_ref, high_ref)[half], at)


def backward_kernel(core, tables, analysed_ref, *rest):
    if core is None:
        backward_blocks(tables, analysed_ref, rest[-1])
    else:
        pl.when(on_core(core))(lambda: backward_blocks(tables, analysed_ref, rest[-1]))


def backward_blocks(tables, analysed_ref, out):
    slots, _, _, degrees = tables.shape
    blocks, _, _, width = out.shape
    stratum = degrees // slots
    place = ring_place(lax.axis_index("blk"), blocks)
    ring = ring_of(blocks)
    step_of = [lax.rem(ring.index(b) - place + blocks, blocks) for b in range(blocks)]
    row8 = lax.broadcasted_iota(jnp.int32, (8, LANES), 0)
    for m in range(slots):
        an = [analysed_ref[m, a] for a in range(4)]
        ng = [-value for value in an]
        for t in range(stratum * m // LANES, degrees // LANES, 2):
            spans = [slice(u * LANES, (u + 1) * LANES) for u in (t, t + 1)]
            folded = update_tiles(tables, m, spans, an, ng, row8)
            for k, u in enumerate((t, t + 1)):
                inner = u * LANES % width
                out[step_of[u * LANES // width], m, :, inner : inner + LANES] = folded[
                    4 * k : 4 * k + 4
                ]


def residual_kernel(groups, slots, cycles, *rest):
    metas = [ref[...] for ref in rest[:groups]]
    section_ref, acs_ref, asc_ref, fine_ref, phases_ref = rest[groups : groups + 5]
    messages = rest[groups + 5 : 2 * groups + 4]
    out_ref, spread = rest[2 * groups + 4 :]
    owner = lax.axis_index("order")
    rows, both = acs_ref.shape[1:]
    every = both // 2
    count = phases_ref.shape[0]
    lane = lax.broadcasted_iota(jnp.int32, (count, LANES), 1)
    ids = spread_ids(metas, slots, [d for _ in range(2) for d in range(groups)])
    factor = jnp.where(ids == 0.0, 1.0, 2.0)
    per = LANES // slots
    values = [phases_ref[...]] + [ref[:count] for ref in messages]
    for a in range(4):
        tiles = []
        for start in range(0, 2 * groups, per):
            tile = jnp.zeros((count, LANES), jnp.float32)
            for k in range(per):
                shift = (k - a) * slots % LANES
                value = values[(start + k) % groups]
                value = pltpu.roll(value, shift, 1) if shift else value
                tile = jnp.where(lane // slots == k, value, tile)
            tiles.append(tile)
        spread[a] = jnp.concatenate(tiles, axis=1) * factor
    even = lax.broadcasted_iota(jnp.int32, (rows, both), 0) % 2 == 0
    for c in range(cycles):
        q_re, q_im, u_re, u_im = [spread[a, pl.ds(owner * cycles + c, 1)] for a in range(4)]
        weights = jnp.where(even, q_re, u_re) * acs_ref[c]
        weights = weights - jnp.where(even, q_im, u_im) * asc_ref[c]
        model = lax.dot_general(
            weights, fine_ref[c], (((1,), (1,)), ((), ())), precision=HIGHEST,
            preferred_element_type=jnp.float32,
        )
        inside = pixel_mask((rows, LANES), entry(metas[0], slots + c).astype(jnp.int32))
        out_ref[c] = section_ref[c] - jnp.where(inside, model, 0.0)


def join_kernel(own_ref, value_ref, out_ref):
    out_ref[...] = own_ref[...] + value_ref[...]


def add_kernel(index, first, piece_ref, value_ref, out_ref):
    out_ref[...] = piece_ref[index, first : first + out_ref.shape[0]] + value_ref[...]


def final_kernel(meta_ref, harmonics_ref, piece_ref, *rest):
    *received, out, held, sems = rest
    slots, parts, width = held.shape
    middle = slots // 2
    start = lax.axis_index("blk") * width
    degree = start + lax.broadcasted_iota(jnp.int32, (parts, width), 1)
    meta = meta_ref[...]
    copies = []
    for m in range(slots):
        h, at = divmod(m, middle)
        update = piece_ref[0, m] + (received[h][at] + received[2 + h][at])
        valid = degree >= jnp.maximum(entry(meta, m).astype(jnp.int32), 2)
        held[m] = jnp.where(valid, harmonics_ref[m] + update, 0.0)
        if at == middle - 1:
            span = pl.ds(h * middle, middle)
            copies.append(pltpu.make_async_copy(held.at[span], out.at[span], sems.at[h]))
            copies[-1].start()
    for copy in copies:
        copy.wait()


def vmem():
    return pl.BlockSpec(memory_space=VMEM)


def shape(*dims):
    return jax.ShapeDtypeStruct(dims, jnp.float32)


def body(harmonics, legendre, sky_map, cycle_length, cycle_offset, cycle_weight, order_ids):
    groups = lax.axis_size("order")
    blocks = lax.axis_size("blk")
    slots, _, width = harmonics.shape
    count, degrees = legendre.shape[2:]
    cycles, _, pixels = sky_map.shape
    rows = pixels // LANES
    every = slots * groups
    normalise = math.sqrt(degrees * every / (cycles * groups * blocks * pixels))

    def swap(value, axis, step):
        size = lax.axis_size(axis)
        return lax.ppermute(value, axis, [(i, i ^ step) for i in range(size)])

    ring = ring_of(blocks)

    def turn(value, way):
        pairs = [(ring[p], ring[(p + way) % blocks]) for p in range(blocks)]
        return lax.ppermute(value, "blk", pairs)

    def estimate(micros):
        return pl.CostEstimate(flops=0, bytes_accessed=int(micros * 3.0e6), transcendentals=0)

    hbm = pl.BlockSpec(memory_space=pl.ANY)
    small = (order_ids, cycle_length, cycle_offset, cycle_weight)
    meta = pl.pallas_call(
        lambda *refs: meta_kernel(slots, cycles, *refs),
        out_shape=pltpu.VMEM((1, LANES), jnp.float32),
        in_specs=[hbm] * 4,
        out_specs=vmem(),
        scratch_shapes=[pltpu.SMEM(v.shape, v.dtype) for v in small]
        + [pltpu.SemaphoreType.DMA((len(small),))],
        compiler_params=pltpu.CompilerParams(vmem_limit_bytes=2 * MIB),
        name="meta",
    )(*[pltpu.with_memory_space_constraint(v, pltpu.HBM) for v in small])
    metas = [meta] + [swap(meta, "order", d) for d in range(1, groups)]

    far = blocks // 2
    middle = slots // 2
    ahead, behind = turn(harmonics, 1), turn(harmonics, -1)
    parts, steps, firsts = [harmonics, ahead, behind], [0, -1, 1], [0, 0, 0]
    tables = pl.pallas_call(
        tables_kernel,
        out_shape=pltpu.VMEM(legendre.shape, jnp.float32),
        in_specs=[hbm],
        out_specs=hbm,
        scratch_shapes=[pltpu.SemaphoreType.DMA((slots,))],
        compiler_params=pltpu.CompilerParams(vmem_limit_bytes=2 * MIB),
        cost_estimate=estimate(1.5),
        name="tables",
    )(pltpu.with_memory_space_constraint(legendre, pltpu.HBM))
    ahead, tables, *metas = lax.optimization_barrier((ahead, tables, *metas))
    ahead = [ahead[:middle], ahead[middle:]]
    behind = [behind[:middle], behind[middle:]]

    sky = sky_map.reshape(cycles, 2, rows, LANES).transpose(0, 2, 1, 3)
    sky = sky.reshape(cycles, 2 * rows, LANES)
    pieces, acs, asc, fine, section = pl.pallas_call(
        lambda *refs: sky_kernel(normalise, groups, slots, cycles, *refs),
        out_shape=(
            shape(groups, 8, LANES),
            shape(cycles, 2 * rows, 2 * every),
            shape(cycles, 2 * rows, 2 * every),
            shape(cycles, LANES, 2 * every),
            shape(cycles, 2 * rows, LANES),
        ),
        in_specs=[vmem()] * groups + [hbm],
        out_specs=(vmem(),) * 5,
        scratch_shapes=[
            pltpu.VMEM((cycles, 2 * rows, LANES), jnp.float32),
            pltpu.SemaphoreType.DMA,
        ],
        compiler_params=pltpu.CompilerParams(vmem_limit_bytes=16 * MIB),
        cost_estimate=estimate(3),
        name="sky_analysis",
    )(*metas, pltpu.with_memory_space_constraint(sky, pltpu.HBM))
    gram = pl.pallas_call(
        lambda *refs: gram_kernel(normalise, groups, slots, cycles, *refs),
        out_shape=shape(slots, count, 4 * every),
        in_specs=[vmem()] * groups,
        out_specs=vmem(),
        compiler_params=pltpu.CompilerParams(vmem_limit_bytes=8 * MIB),
        cost_estimate=estimate(1),
        name="response",
    )(*metas)

    for k in range(2, far):
        ahead = [turn(value, 1) for value in ahead]
        behind = [turn(value, -1) for value in behind[::-1]][::-1]
        parts += ahead + behind
        steps += [-k, -k, k, k]
        firsts += [0, middle] * 2
        if k == 2:
            ahead[0], pieces = lax.optimization_barrier((ahead[0], pieces))
    ends = [turn(ahead[0], 1), turn(behind[1], -1)]

    whole = pltpu.VMEM((slots, 4, count, LANES), jnp.float32)
    sums = pl.pallas_call(
        lambda *refs: forward_kernel(steps, firsts, *refs),
        out_shape=whole,
        in_specs=[vmem()] * (2 + len(parts)),
        out_specs=vmem(),
        scratch_shapes=[pltpu.VMEM((slots, 4, degrees), jnp.float32)],
        compiler_params=pltpu.CompilerParams(vmem_limit_bytes=24 * MIB),
        cost_estimate=estimate(2),
        name="forward",
    )(meta, tables, *parts)
    phases, *outs = pl.pallas_call(
        lambda *refs: phases_kernel(groups, *refs),
        out_shape=[shape(count, LANES)] + [shape(count + 8, LANES)] * (groups - 1),
        in_specs=[vmem()] * 6,
        out_specs=[vmem()] * groups,
        compiler_params=pltpu.CompilerParams(vmem_limit_bytes=16 * MIB),
        cost_estimate=estimate(1),
        name="phases",
    )(meta, tables, pieces, sums, *ends)
    messages = [swap(outs[d - 1], "order", d) for d in range(1, groups)]

    half = pltpu.VMEM((middle, 4, width), jnp.float32)
    *sends, analysed = pl.pallas_call(
        lambda *refs: analysed_kernel(groups, cycles, *refs),
        out_shape=[half] * 2 + [whole],
        in_specs=[vmem()] * (3 + groups),
        out_specs=[vmem()] * 3,
        scratch_shapes=[pltpu.VMEM((count, LANES), jnp.float32)],
        compiler_params=pltpu.CompilerParams(vmem_limit_bytes=16 * MIB),
        cost_estimate=estimate(1),
        name="analysed",
    )(tables, gram, pieces, phases, *messages)
    def nearer(ways):
        return pl.pallas_call(
            lambda *refs: second_kernel(ways, *refs),
            out_shape=[half] * 2,
            in_specs=[vmem()] * 2,
            out_specs=[vmem()] * 2,
            compiler_params=pltpu.CompilerParams(vmem_limit_bytes=16 * MIB),
            cost_estimate=estimate(0.5),
            name="second",
        )(tables, analysed)

    second = nearer((-1, 1))
    third = nearer((1, -1))

    def backward(core, *before):
        return pl.pallas_call(
            lambda *refs: backward_kernel(core, *refs),
            out_shape=pltpu.VMEM((blocks, slots, 4, width), jnp.float32),
            in_specs=[vmem()] * 2 + [hbm] * len(before),
            out_specs=vmem(),
            input_output_aliases={2: 0} if before else {},
            compiler_params=pltpu.CompilerParams(vmem_limit_bytes=16 * MIB),
            cost_estimate=estimate(2),
            name="backward",
        )(
            tables, analysed,
            *[pltpu.with_memory_space_constraint(value, pltpu.VMEM) for value in before],
        )

    piece = backward(None)

    def add(index, first, value):
        return pl.pallas_call(
            lambda *refs: add_kernel(index, first, *refs),
            out_shape=half,
            in_specs=[vmem()] * 2,
            out_specs=vmem(),
            compiler_params=pltpu.CompilerParams(vmem_limit_bytes=4 * MIB),
            cost_estimate=estimate(0.1),
            name="add",
        )(piece, pltpu.with_memory_space_constraint(value, pltpu.VMEM))

    sent = dict(zip(((1, 0), (-1, middle), (-1, 0), (1, middle)), (*sends, *second)))
    first_hop = {key: turn(sent[key], key[0]) for key in ((1, 0), (-1, middle))}
    for key, own in zip(((1, 0), (-1, middle)), third):
        sent[key] = pl.pallas_call(
            join_kernel,
            out_shape=half,
            in_specs=[vmem()] * 2,
            out_specs=vmem(),
            compiler_params=pltpu.CompilerParams(vmem_limit_bytes=4 * MIB),
            cost_estimate=estimate(0.1),
            name="join",
        )(own, pltpu.with_memory_space_constraint(first_hop[key], pltpu.VMEM))
    for k in reversed(range(1, far)):
        for key in ((1, middle), (-1, 0), (1, 0), (-1, middle)):
            sent[key] = turn(sent[key], key[0])
            if k > 1:
                sent[key] = add((key[0] * (k - 1)) % blocks, key[1], sent[key])
    received = [sent[key] for key in ((1, 0), (1, middle), (-1, 0), (-1, middle))]
    refined = pl.pallas_call(
        final_kernel,
        out_shape=shape(*harmonics.shape),
        in_specs=[vmem()] * 7,
        out_specs=hbm,
        scratch_shapes=[
            pltpu.VMEM(harmonics.shape, jnp.float32),
            pltpu.SemaphoreType.DMA((2,)),
        ],
        compiler_params=pltpu.CompilerParams(vmem_limit_bytes=8 * MIB),
        cost_estimate=pl.CostEstimate(flops=10**5, bytes_accessed=10**6, transcendentals=0),
        name="refine",
    )(
        meta, harmonics, piece,
        *[pltpu.with_memory_space_constraint(value, pltpu.VMEM) for value in received],
    )

    residual = pl.pallas_call(
        lambda *refs: residual_kernel(groups, slots, cycles, *refs),
        out_shape=shape(cycles, 2 * rows, LANES),
        in_specs=[vmem()] * (4 + 2 * groups),
        out_specs=vmem(),
        scratch_shapes=[pltpu.VMEM((4, count, 2 * every), jnp.float32)],
        compiler_params=pltpu.CompilerParams(vmem_limit_bytes=16 * MIB),
        cost_estimate=pl.CostEstimate(flops=10**8, bytes_accessed=2 * MIB, transcendentals=0),
        name="residual",
    )(*metas, section, acs, asc, fine, phases, *messages)
    residual = residual.reshape(cycles, rows, 2, LANES).transpose(0, 2, 1, 3)
    return (refined, residual.reshape(sky_map.shape))


def solution(mesh):
    return jax.shard_map(
        body,
        mesh=mesh,
        in_specs=(
            P("order", None, "blk"),
            P("order", None, "blk", None),
            P(("blk", "order"), None, None),
            P(("blk", "order")),
            P(("blk", "order")),
            P(("blk", "order")),
            P("order"),
        ),
        out_specs=(P("order", None, "blk"), P(("blk", "order"), None, None)),
        check_vma=False,
    )
```
